128 devices in a mesh: pipe: 4 (over z_lo, core), ctx: 8 (over x, z_hi), dp: 4 (over y).
Axes of the slice: x: 4, y: 4, z: 4 (z_hi: 2, z_lo: 2; z = z_hi * 2 + z_lo), core: 2. Of those that a mesh axis runs over, the one named last changes fastest.
Arguments:
- down_input: bfloat16 [4, 2048, 1024], P('dp', 'ctx'), may hold values from -6 to 6
- up_input: bfloat16 [4, 2048, 1024], P('dp', 'ctx'), may hold values from -6 to 6
- down_qkv: bfloat16 [4, 1024, 3072], P('pipe'), may hold values from -0.1875 to 0.1875
- up_qkv: bfloat16 [4, 1024, 3072], P('pipe'), may hold values from -0.1875 to 0.1875
- down_gates: bfloat16 [4, 1024, 16], P('pipe'), may hold values from -0.1875 to 0.1875
- up_gates: bfloat16 [4, 1024, 16], P('pipe'), may hold values from -0.1875 to 0.1875
- down_rates: float32 [4, 8], P('pipe'), may hold values from 0.0002 to 0.05
- up_rates: float32 [4, 8], P('pipe'), may hold values from 0.0002 to 0.05
- down_out: bfloat16 [4, 1024, 1024], P('pipe'), may hold values from -0.1875 to 0.1875
- up_out: bfloat16 [4, 1024, 1024], P('pipe'), may hold values from -0.1875 to 0.1875
- down_cotangent: bfloat16 [4, 4, 2048, 1024], P('pipe', 'dp', 'ctx'), may hold values from -0.046875 to 0.046875
- up_cotangent: bfloat16 [4, 4, 2048, 1024], P('pipe', 'dp', 'ctx'), may hold values from -0.046875 to 0.046875
Outputs:
- down_acts: bfloat16 [4, 4, 2048, 1024], P('pipe', 'dp', 'ctx')
- up_acts: bfloat16 [4, 4, 2048, 1024], P('pipe', 'dp', 'ctx')
- out_grad: float32 [4, 1024, 1024], P('pipe', ('ctx', 'dp'))
The draws below stay inside these ranges and needn't reach their ends.
All inputs are finite; a program needn't handle non-finite values.
Results may differ from the reference program's by a relative error of at most 0.04.
Values may be sent and summed in bfloat16 or wider, within the bound.
A program may use at most 192 MiB of HBM per device.

```python
import math
import jax
import jax.numpy as jnp
from jax import lax

D = 1024
HEADS = 8
BLOCK = 64
HK = 1024
SECTIONS = 4
BATCH = 4
LENGTH = 2048


def level_of(own_key, dims, split, least, high):
    gain, own = 1.0, jax.random.fold_in(own_key, 6)
    for axis_at, shards_of in split:
        draws = jnp.exp(jax.random.uniform(jax.random.fold_in(own, axis_at), (shards_of,), jnp.float32, least / len(split), high / len(split)))
        gain = gain * jnp.repeat(draws, dims[axis_at] // shards_of).reshape([-1 if axis == axis_at else 1 for axis in range(len(dims))])
    return gain


def scatter_about(own_key, extent, scale, most, cuts=(), held_as=jnp.bfloat16):
    values = jax.random.normal(own_key, extent, jnp.float32) * scale
    if len(cuts) > 0:
        values = level_of(own_key, extent, cuts, -0.22, 0.18) * values
    return jnp.clip(values, min=-most, max=most).astype(held_as)


def setup_inputs(seed: int = 0) -> dict:
    splits = jax.random.split(jax.random.key(seed), 13)
    return {
        "down_input": scatter_about(splits[0], (BATCH, LENGTH, D), 1.0, 6.0, ((0, 4), (1, 8))),
        "up_input": scatter_about(splits[1], (BATCH, LENGTH, D), 1.0, 6.0, ((0, 4), (1, 8))),
        "down_qkv": scatter_about(splits[2], (SECTIONS, D, 3 * HK), D ** -0.5, 0.1875, ((0, 4),)),
        "up_qkv": scatter_about(splits[3], (SECTIONS, D, 3 * HK), D ** -0.5, 0.1875, ((0, 4),)),
        "down_gates": scatter_about(splits[4], (SECTIONS, D, 2 * HEADS), D ** -0.5, 0.1875, ((0, 4),)),
        "up_gates": scatter_about(splits[5], (SECTIONS, D, 2 * HEADS), D ** -0.5, 0.1875, ((0, 4),)),
        "down_rates": jnp.clip(jnp.exp(math.log(0.05) - 5.521461 * jax.random.uniform(splits[6], (SECTIONS, HEADS), jnp.float32) ** level_of(splits[6], (SECTIONS, HEADS), ((0, 4),), -0.2, 0.2)), 0.0002, 0.05),
        "up_rates": jnp.clip(jnp.exp(math.log(0.05) - 5.521461 * jax.random.uniform(splits[7], (SECTIONS, HEADS), jnp.float32) ** level_of(splits[7], (SECTIONS, HEADS), ((0, 4),), -0.2, 0.2)), 0.0002, 0.05),
        "down_out": scatter_about(splits[8], (SECTIONS, HK, D), HK ** -0.5, 0.1875, ((0, 4),)),
        "up_out": scatter_about(splits[9], (SECTIONS, HK, D), HK ** -0.5, 0.1875, ((0, 4),)),
        "down_cotangent": scatter_about(splits[10], (SECTIONS, BATCH, LENGTH, D), ((2 * BATCH * LENGTH) ** -0.5), 0.046875, ((0, 4), (1, 4), (2, 8))),
        "up_cotangent": scatter_about(splits[11], (SECTIONS, BATCH, LENGTH, D), ((2 * BATCH * LENGTH) ** -0.5), 0.046875, ((0, 4), (1, 4), (2, 8))),
    }


EPSILON = 1e-06
EXACT = lax.Precision.HIGHEST

def mean_norm(values):
    return values * lax.rsqrt(lax.optimization_barrier(jnp.mean(values * values, axis=-1, keepdims=True)) + EPSILON)

def unit_norm(values):
    return values * lax.rsqrt(lax.optimization_barrier(jnp.sum(values * values, axis=-1, keepdims=True)) + EPSILON)

def unit_inverse(strict, repeats):
    negated = -strict
    result = jnp.eye(strict.shape[-1], dtype=jnp.float32) + negated
    raised = negated
    for _ in range(repeats):
        raised = jnp.einsum('...ij,...jk->...ik', raised, raised, precision=EXACT)
        result = result + jnp.einsum('...ij,...jk->...ik', result, raised, precision=EXACT)
    return result

def prepare(stream, qkv_weight, gate_weight, decay_rate):
    length = stream.shape[0]
    head_count = decay_rate.shape[0]
    head_dim = qkv_weight.shape[1] // (3 * head_count)
    blocks = length // BLOCK
    normed = mean_norm(stream.astype(jnp.float32)).astype(jnp.bfloat16)
    project = jnp.dot(normed, qkv_weight, preferred_element_type=jnp.float32)
    gating = jnp.dot(normed, gate_weight, preferred_element_type=jnp.float32)
    project = project.reshape(blocks, BLOCK, 3, head_count, head_dim).transpose(2, 0, 3, 1, 4)
    queries = unit_norm(project[0]) * head_dim ** (-0.5)
    key_rows = unit_norm(project[1])
    value_rows = project[2]
    gating = gating.reshape(blocks, BLOCK, 2, head_count).transpose(2, 0, 3, 1)
    strength = jax.nn.sigmoid(gating[0])
    log_decay = -decay_rate[None, :, None] * jax.nn.softplus(gating[1])
    cumulative = jnp.cumsum(log_decay, axis=-1)
    decay_gap = cumulative[..., :, None] - cumulative[..., None, :]
    row_index = lax.broadcasted_iota(jnp.int32, (BLOCK, BLOCK), 0)
    col_index = lax.broadcasted_iota(jnp.int32, (BLOCK, BLOCK), 1)
    strict_lower = row_index > col_index
    lower_diag = row_index >= col_index
    fading = jnp.exp(jnp.where(lower_diag, decay_gap, 0.0))
    key_gram = jnp.einsum('bhid,bhjd->bhij', key_rows, key_rows, precision=EXACT)
    strict = jnp.where(strict_lower, strength[..., :, None] * key_gram * fading, 0.0)
    inverse = unit_inverse(strict, BLOCK.bit_length() - 2) * strength[..., None, :]
    growth = jnp.exp(cumulative)[..., None]
    erase_rows = jnp.einsum('bhij,bhjd->bhid', inverse, key_rows * growth, precision=EXACT)
    target_rows = jnp.einsum('bhij,bhjd->bhid', inverse, value_rows, precision=EXACT)
    query_decay = queries * growth
    scores = jnp.where(lower_diag, jnp.einsum('bhid,bhjd->bhij', queries, key_rows, precision=EXACT) * fading, 0.0)
    last_decay = cumulative[..., -1:]
    key_tail = key_rows * jnp.exp(last_decay - cumulative)[..., None]
    block_fade = jnp.exp(last_decay)[..., None]
    return (erase_rows, target_rows, query_decay, scores, key_tail, block_fade)

def block_step(memory, pieces):
    erase_rows, target_rows, query_decay, scores, key_tail, block_fade = pieces
    new_values = target_rows - jnp.einsum('hcd,hde->hce', erase_rows, memory, precision=EXACT)
    output = jnp.einsum('hcd,hde->hce', query_decay, memory, precision=EXACT)
    output = output + jnp.einsum('hij,hje->hie', scores, new_values, precision=EXACT)
    memory = block_fade * memory + jnp.einsum('hcd,hce->hde', key_tail, new_values, precision=EXACT)
    return (memory, output)

def finish(stream, outputs, out_weight):
    blocks, head_count, block_len, head_dim = outputs.shape
    normed = mean_norm(outputs).transpose(0, 2, 1, 3).reshape(blocks * block_len, head_count * head_dim)
    normed = normed.astype(jnp.bfloat16)
    updated = stream.astype(jnp.float32) + jnp.dot(normed, out_weight, preferred_element_type=jnp.float32)
    return (updated.astype(jnp.bfloat16), normed)

def run_section(stream, qkv_weight, gate_weight, decay_rate, out_weight):

    def one_sequence(sequence):
        pieces = prepare(sequence, qkv_weight, gate_weight, decay_rate)
        head_count = decay_rate.shape[0]
        head_dim = pieces[0].shape[-1]
        memory = jnp.zeros((head_count, head_dim, head_dim), jnp.float32)
        memory, outputs = lax.scan(block_step, memory, pieces)
        return finish(sequence, outputs, out_weight)
    return lax.map(one_sequence, stream)

def token_sum(hidden, cotangent):
    flat_hidden = hidden.reshape(-1, hidden.shape[-1])
    flat_cot = cotangent.reshape(-1, cotangent.shape[-1])
    return lax.dot_general(flat_hidden, flat_cot, (((0,), (0,)), ((), ())), preferred_element_type=jnp.float32)

def reference(down_input, up_input, down_qkv, up_qkv, down_gates, up_gates, down_rates, up_rates, down_out, up_out, down_cotangent, up_cotangent):
    sections = down_qkv.shape[0]
    down_list = []
    down_hidden = []
    current = down_input
    for section_index in range(sections):
        current, hidden = run_section(current, down_qkv[section_index], down_gates[section_index], down_rates[section_index], down_out[section_index])
        down_list.append(current)
        down_hidden.append(hidden)
    up_list = [None] * sections
    up_hidden = [None] * sections
    current = up_input
    for section_index in reversed(range(sections)):
        current, hidden = run_section(current, up_qkv[section_index], up_gates[section_index], up_rates[section_index], up_out[section_index])
        up_list[section_index] = current
        up_hidden[section_index] = hidden
    gradients = []
    for section_index in range(sections):
        mirror = sections - 1 - section_index
        gradients.append(token_sum(down_hidden[section_index], down_cotangent[section_index]) + token_sum(up_hidden[mirror], up_cotangent[mirror]))
    return (jnp.stack(down_list), jnp.stack(up_list), jnp.stack(gradients))
```

```python
import functools

import jax
import jax.numpy as jnp
from jax import lax
from jax.experimental import pallas as pl
from jax.experimental.pallas import tpu as pltpu
from jax.sharding import PartitionSpec as P

MESH = pl.DeviceIdType.MESH
EPSILON = 1e-06
EXACT = lax.Precision.HIGHEST
BF = jnp.bfloat16
F32 = jnp.float32
HEADS = 8
DIM = 128
TOK = 256
WIDTH = 1024
CH = 4
COLS = WIDTH // CH
UNIT = 32
GROUP = 8


def mm(a, b):
    return jnp.dot(a, b, preferred_element_type=F32)


def mm_nt(a, b):
    return lax.dot_general(a, b, (((1,), (1,)), ((), ())), preferred_element_type=F32)


def level_mask(size):
    row = lax.broadcasted_iota(jnp.int32, (DIM, DIM), 0)
    col = lax.broadcasted_iota(jnp.int32, (DIM, DIM), 1)
    if size == 0:
        return (row == col).astype(F32)
    if size == DIM:
        return (row >= col).astype(F32)
    same = (row // (2 * size)) == (col // (2 * size))
    return (same & ((row // size) > (col // size))).astype(F32)


LEVELS = (1, 2, 4, 8, 16, 32, 64)


def block_inverses(parts, masks):
    eye = masks[0]
    results = [eye - a * masks[1] for a in parts]
    for level in range(2, 8):
        offs = [a * masks[level] for a in parts]
        inner = [mm(o, t).astype(BF) for o, t in zip(offs, results)]
        results = [t - mm(t, y).astype(BF) for t, y in zip(results, inner)]
    return results


def head_maps(heads, proj, rstd, beta, cum, cum_rows, masks, low, put):
    first, second = slice(0, DIM), slice(DIM, TOK)
    state = []
    for h in heads:
        q = proj[:, pl.ds(h * DIM, DIM)] * rstd
        k = proj[:, pl.ds(WIDTH + h * DIM, DIM)] * rstd
        v = proj[:, pl.ds(2 * WIDTH + h * DIM, DIM)] * rstd
        q = q * (lax.rsqrt(jnp.sum(q * q, axis=-1, keepdims=True) + EPSILON) * DIM ** -0.5)
        k = k * lax.rsqrt(jnp.sum(k * k, axis=-1, keepdims=True) + EPSILON)
        b = beta[:, h : h + 1]
        c = jnp.broadcast_to(cum[:, HEADS + h : HEADS + h + 1], (TOK, DIM))
        row = cum_rows[HEADS + h : HEADS + h + 1, :]
        growth = jnp.exp(c)
        last = c[TOK - 1 : TOK, :]
        qb, kb, kbeta = q.astype(BF), k.astype(BF), (k * b).astype(BF)
        d11 = jnp.exp(jnp.minimum(c[first] - row[:, first], 0.0))
        d21 = jnp.exp(jnp.minimum(c[second] - row[:, first], 0.0))
        d22 = jnp.exp(jnp.minimum(c[second] - row[:, second], 0.0))
        lhs = jnp.concatenate([kbeta, qb], axis=0)
        g1 = mm_nt(lhs, kb[first])
        g2 = mm_nt(jnp.concatenate([kbeta[second], qb[second]], axis=0), kb[second])
        a11 = (g1[0:128] * d11).astype(BF)
        a21 = (g1[128:256] * d21).astype(BF)
        s11 = (g1[256:384] * (d11 * low)).astype(BF)
        s21 = (g1[384:512] * d21).astype(BF)
        a22 = (g2[0:128] * d22).astype(BF)
        s22 = (g2[128:256] * (d22 * low)).astype(BF)
        rhs = jnp.concatenate([(k * (growth * b)).astype(BF), (v * b).astype(BF)], axis=1)
        tail = (k * jnp.exp(last - c)).T.astype(BF)
        state.append((a11, a22, a21, s11, s21, s22, rhs, tail, q * growth, jnp.exp(last)))
    inverses = block_inverses([s[0] for s in state] + [s[1] for s in state], masks)
    n = len(state)
    x1 = [mm(inverses[i], state[i][6][first]).astype(BF) for i in range(n)]
    r2 = [(state[i][6][second].astype(F32) - mm(state[i][2], x1[i])).astype(BF) for i in range(n)]
    x2 = [mm(inverses[n + i], r2[i]).astype(BF) for i in range(n)]
    for i, h in enumerate(heads):
        _, _, _, s11, s21, s22, _, tail, qg, fade = state[i]
        x = jnp.concatenate([x1[i], x2[i]], axis=0)
        z1 = mm(s11, x1[i])
        z2 = mm(jnp.concatenate([s21, s22], axis=1), x)
        kx = mm(tail, x)
        put(h, qg, z1, z2, kx, fade)


def kernel(
    dims,
    down_in, up_in, down_qkv, up_qkv, down_gates, up_gates, down_rates, up_rates,
    down_wo, up_wo, down_ct, up_ct,
    down_out, up_out, grad_out,
    wqkv, wo, wg, xbuf, ybuf, proj, hid, maskb, pmap, rmap, mmap, bmap, sin, sout,
    cot, ht, hg, part, gbuf, gsum,
    w_sem, wo_sem, x_recv, x_send, y_sem, s_recv, s_send, ct_recv, ct_send,
    h_recv, h_send, g_recv, g_send, go_sem,
):
    sections, spans, copies = dims
    p, c, d = lax.axis_index("pipe"), lax.axis_index("ctx"), lax.axis_index("dp")
    low_half = p < sections // 2
    share = WIDTH // (spans * copies)
    column = WIDTH // spans

    def is_down(t):
        return low_half == (t == 0)

    def at(pipe, ctx, dp):
        return (pipe, ctx, dp)

    def remote(src, dst, send, recv, where):
        return pltpu.make_async_remote_copy(
            src_ref=src, dst_ref=dst, send_sem=send, recv_sem=recv,
            device_id=where, device_id_type=MESH,
        )

    def weight_copy(t, n, qkv):
        rows = pl.ds(n * COLS, COLS)
        return pltpu.make_async_copy(qkv.at[0, rows], wqkv.at[t, rows], w_sem.at[t, n])

    def out_copy(t, out):
        return pltpu.make_async_copy(out.at[0], wo.at[t], wo_sem.at[t])

    def start_weights(t, qkv, out):
        for n in range(CH):
            weight_copy(t, n, qkv).start()
        out_copy(t, out).start()

    def input_copy(src, n):
        return pltpu.make_async_copy(
            src.at[0, :, pl.ds(n * COLS, COLS)], xbuf.at[0, n], x_recv.at[0, n]
        )

    @pl.when(p == 0)
    def _():
        for n in range(CH):
            input_copy(down_in, n).start()

    @pl.when(p == sections - 1)
    def _():
        for n in range(CH):
            input_copy(up_in, n).start()

    @pl.when(low_half)
    def _():
        start_weights(0, down_qkv, down_wo)
        start_weights(1, up_qkv, up_wo)

    @pl.when(jnp.logical_not(low_half))
    def _():
        start_weights(0, up_qkv, up_wo)
        start_weights(1, down_qkv, down_wo)

    barrier = pltpu.get_barrier_semaphore()
    mirror = sections - 1 - p
    pair = p + 1 - 2 * lax.rem(p, 2)
    peers = [at(pair, c, d), at(mirror, c, d)]
    for k in range(1, spans):
        other = lax.rem(c + k, spans)
        peers += [at(p, other, d), at(mirror, other, d)]
    for k in range(1, copies):
        peers.append(at(p, c, lax.rem(d + k, copies)))
    for peer in peers:
        pl.semaphore_signal(barrier, inc=1, device_id=peer, device_id_type=MESH)

    for level, size in enumerate((0,) + LEVELS + (DIM,)):
        maskb[level] = level_mask(size).astype(BF)
    for t in range(2):
        wg[t] = jnp.zeros_like(wg[t])
        wg[t, :, 0 : 2 * HEADS] = jnp.where(is_down(t), down_gates[0], up_gates[0])

    pl.semaphore_wait(barrier, len(peers))

    def cot_own(t, source):
        return pltpu.make_async_copy(source.at[0, 0], cot.at[t, d], ct_recv.at[t, d])

    def cot_copy(t, source, k):
        return remote(
            source.at[0, 0], cot.at[t, d], ct_send.at[t, k - 1], ct_recv.at[t, d],
            at(p, c, lax.rem(d + k, copies)),
        )

    def start_cot(t, source):
        cot_own(t, source).start()
        for k in range(1, copies):
            cot_copy(t, source, k).start()

    @pl.when(low_half)
    def _():
        start_cot(0, down_ct)
        start_cot(1, up_ct)

    @pl.when(jnp.logical_not(low_half))
    def _():
        start_cot(0, up_ct)
        start_cot(1, down_ct)

    def state_copy(t, h):
        return remote(
            sout.at[t, h], sin.at[t, h], s_send.at[t, h], s_recv.at[t, h],
            at(p, lax.rem(c + 1, spans), d),
        )

    def stage_of(t):
        early = jnp.where(low_half, p, sections - 1 - p)
        return jnp.where(t == 0, early, sections - 1 - early)

    def stream_copy(t, n):
        slot = jnp.where(stage_of(t) == 0, 0, 1)
        to = jnp.clip(jnp.where(is_down(t), p + 1, p - 1), 0, sections - 1)
        return remote(
            ybuf.at[t, n], xbuf.at[slot, n], x_send.at[t, n], x_recv.at[slot, n], at(to, c, d)
        )

    def result_copy(t, n, out):
        return pltpu.make_async_copy(
            ybuf.at[t, n], out.at[0, 0, :, pl.ds(n * COLS, COLS)], y_sem.at[t, n]
        )

    def hidden_own(t):
        return pltpu.make_async_copy(ht.at[t, d], hg.at[t, d], h_recv.at[t, d])

    def hidden_copy(t, k):
        to = lax.rem(d + k, copies)
        return remote(ht.at[t, to], hg.at[t, d], h_send.at[t, k - 1], h_recv.at[t, d], at(p, c, to))

    def grad_own(t):
        return pltpu.make_async_copy(part.at[t, c], gbuf.at[c], g_recv.at[c])

    def grad_copy(t, k):
        to = lax.rem(c + k, spans)
        slot = c + jnp.where(is_down(t), 0, spans)
        pipe = jnp.where(is_down(t), p, mirror)
        return remote(part.at[t, to], gbuf.at[slot], g_send.at[t, k], g_recv.at[slot], at(pipe, to, d))

    def section(t):
        square = jnp.zeros((TOK, 1), F32)
        logits = jnp.zeros((TOK, DIM), F32)
        for n in range(CH):
            pltpu.make_async_copy(xbuf.at[t, n], xbuf.at[t, n], x_recv.at[t, n]).wait()
            weight_copy(t, n, down_qkv).wait()
            x = xbuf[t, n]
            xf = x.astype(F32)
            square += jnp.sum(xf * xf, axis=-1, keepdims=True)
            logits += mm(x, wg[t, n * COLS : (n + 1) * COLS, :])
            for j in range(6):
                block = slice(512 * j, 512 * (j + 1))
                product = mm(x, wqkv[t, n * COLS : (n + 1) * COLS, block])
                if n == 0:
                    proj[:, block] = product
                else:
                    proj[:, block] += product
        rstd = lax.rsqrt(square * (1.0 / WIDTH) + EPSILON)
        logits = logits * rstd
        rates = jnp.where(is_down(t), down_rates[...], up_rates[...])
        rates = jnp.concatenate(
            [jnp.zeros((1, HEADS), F32), rates, jnp.zeros((1, DIM - 2 * HEADS), F32)], axis=1
        )
        beta = jax.nn.sigmoid(logits)
        log_decay = -rates * (jnp.maximum(logits, 0.0) + jnp.log1p(jnp.exp(-jnp.abs(logits))))
        row = lax.broadcasted_iota(jnp.int32, (TOK, TOK), 0)
        col = lax.broadcasted_iota(jnp.int32, (TOK, TOK), 1)
        cum = jnp.dot(
            (row >= col).astype(F32), log_decay, preferred_element_type=F32, precision=EXACT
        )
        cum_rows = cum.T
        masks = [maskb[level] for level in range(8)]
        low = maskb[8].astype(F32)
        eye = maskb[0].astype(F32)

        def put(h, qg, z1, z2, kx, fade):
            pmap[h, 0:DIM] = (qg[0:DIM] - z1[:, 0:DIM]).astype(BF)
            pmap[h, DIM:TOK] = (qg[DIM:TOK] - z2[:, 0:DIM]).astype(BF)
            rmap[h, 0:DIM] = z1[:, DIM:TOK]
            rmap[h, DIM:TOK] = z2[:, DIM:TOK]
            mmap[h] = (eye * fade - kx[:, 0:DIM]).astype(BF)
            bmap[h] = kx[:, DIM:TOK]

        for start in range(0, HEADS, GROUP):
            head_maps(
                range(start, start + GROUP), proj, rstd, beta, cum, cum_rows, masks, low, put
            )

        for h in range(HEADS):
            @pl.when(c == 0)
            def _():
                sin[t, h] = jnp.zeros((DIM, DIM), BF)

            @pl.when(c > 0)
            def _():
                state_copy(t, h).wait_recv()

            s = sin[t, h]
            sout[t, h] = (mm(mmap[h], s) + bmap[h]).astype(BF)

            @pl.when(c < spans - 1)
            def _():
                state_copy(t, h).start()

            o = mm(pmap[h], s) + rmap[h]
            o = o * lax.rsqrt(jnp.mean(o * o, axis=-1, keepdims=True) + EPSILON)
            hid[:, h * DIM : (h + 1) * DIM] = o.astype(BF)

        out_copy(t, down_wo).wait()
        for n in range(CH):
            block = slice(n * COLS, (n + 1) * COLS)
            y = xbuf[t, n].astype(F32) + mm(hid[...], wo[t, :, block])
            ybuf[t, n] = y.astype(BF)

            @pl.when(stage_of(t) < sections - 1)
            def _():
                stream_copy(t, n).start()

            @pl.when(is_down(t))
            def _():
                result_copy(t, n, down_out).start()

            @pl.when(jnp.logical_not(is_down(t)))
            def _():
                result_copy(t, n, up_out).start()

        for h in range(HEADS):
            flipped = hid[:, h * DIM : (h + 1) * DIM].T
            for u in range(DIM // UNIT):
                row0 = h * DIM + u * UNIT
                span, rest = row0 // column, row0 % column
                to, i = rest // share, rest % share
                ht[t, to, span * share + i : span * share + i + UNIT] = flipped[
                    u * UNIT : (u + 1) * UNIT
                ]
        hidden_own(t).start()
        for k in range(1, copies):
            hidden_copy(t, k).start()

    def gradient(t):
        for j in range(copies):
            pltpu.make_async_copy(cot.at[t, j], cot.at[t, j], ct_recv.at[t, j]).wait()
            pltpu.make_async_copy(hg.at[t, j], hg.at[t, j], h_recv.at[t, j]).wait()
        for n in range(CH):
            block = slice(n * COLS, (n + 1) * COLS)
            total = mm(hg[t, 0], cot[t, 0, :, block])
            for j in range(1, copies):
                total += mm(hg[t, j], cot[t, j, :, block])
            part[t, :, :, block] = total.astype(BF).reshape(spans, share, COLS)
        for k in range(1, spans):
            grad_copy(t, k).start()

        @pl.when(is_down(t))
        def _():
            grad_own(t).start()

        @pl.when(jnp.logical_not(is_down(t)))
        def _():
            grad_copy(t, 0).start()

    outer = (p == 0) | (p == sections - 1)

    def turn(i, carry):
        middle = jnp.where(outer, 2, 1)
        is_section = (i == 0) | (i == middle)

        @pl.when(is_section)
        def _():
            section(jnp.where(i == 0, 0, 1))

        @pl.when(jnp.logical_not(is_section))
        def _():
            gradient(jnp.where(i == 3, 1, 0))

        return carry

    lax.fori_loop(0, 4, turn, 0)

    for j in range(2 * spans):
        pltpu.make_async_copy(gbuf.at[j], gbuf.at[j], g_recv.at[j]).wait()
    total = gbuf[0].astype(F32)
    for j in range(1, 2 * spans):
        total += gbuf[j].astype(F32)
    gsum[...] = total
    final = pltpu.make_async_copy(gsum, grad_out.at[0], go_sem)
    final.start()

    for t in range(2):
        for n in range(CH):
            result_copy(t, n, down_out).wait()

            @pl.when(stage_of(t) < sections - 1)
            def _():
                stream_copy(t, n).wait_send()

        @pl.when(c < spans - 1)
        def _():
            for h in range(HEADS):
                state_copy(t, h).wait_send()

        for k in range(1, copies):
            cot_copy(t, down_ct, k).wait_send()
            hidden_copy(t, k).wait_send()
        for k in range(1, spans):
            grad_copy(t, k).wait_send()

        @pl.when(jnp.logical_not(is_down(t)))
        def _():
            grad_copy(t, 0).wait_send()

    final.wait()


def per_device(dims, *arrays):
    sections, spans, copies = dims
    share = WIDTH // (spans * copies)
    hbm = pl.BlockSpec(memory_space=pl.ANY)
    vmem = pl.BlockSpec(memory_space=pltpu.VMEM)
    dma = pltpu.SemaphoreType.DMA
    return pl.pallas_call(
        functools.partial(kernel, dims),
        out_shape=(
            jax.ShapeDtypeStruct((1, 1, TOK, WIDTH), BF),
            jax.ShapeDtypeStruct((1, 1, TOK, WIDTH), BF),
            jax.ShapeDtypeStruct((1, share, WIDTH), F32),
        ),
        in_specs=[hbm] * 4 + [vmem] * 4 + [hbm] * 4,
        out_specs=(hbm, hbm, hbm),
        scratch_shapes=[
            pltpu.VMEM((2, WIDTH, 3 * WIDTH), BF),
            pltpu.VMEM((2, WIDTH, WIDTH), BF),
            pltpu.VMEM((2, WIDTH, DIM), BF),
            pltpu.VMEM((2, CH, TOK, COLS), BF),
            pltpu.VMEM((2, CH, TOK, COLS), BF),
            pltpu.VMEM((TOK, 3 * WIDTH), F32),
            pltpu.VMEM((TOK, WIDTH), BF),
            pltpu.VMEM((9, DIM, DIM), BF),
            pltpu.VMEM((HEADS, TOK, DIM), BF),
            pltpu.VMEM((HEADS, TOK, DIM), F32),
            pltpu.VMEM((HEADS, DIM, DIM), BF),
            pltpu.VMEM((HEADS, DIM, DIM), F32),
            pltpu.VMEM((2, HEADS, DIM, DIM), BF),
            pltpu.VMEM((2, HEADS, DIM, DIM), BF),
            pltpu.VMEM((2, copies, TOK, WIDTH), BF),
            pltpu.VMEM((2, copies, spans * share, TOK), BF),
            pltpu.VMEM((2, copies, spans * share, TOK), BF),
            pltpu.VMEM((2, spans, share, WIDTH), BF),
            pltpu.VMEM((2 * spans, share, WIDTH), BF),
            pltpu.VMEM((share, WIDTH), F32),
            dma((2, CH)),
            dma((2,)),
            dma((2, CH)),
            dma((2, CH)),
            dma((2, CH)),
            dma((2, HEADS)),
            dma((2, HEADS)),
            dma((2, copies)),
            dma((2, copies)),
            dma((2, copies)),
            dma((2, copies)),
            dma((2 * spans,)),
            dma((2, spans)),
            dma,
        ],
        compiler_params=pltpu.CompilerParams(
            collective_id=0, has_side_effects=True, vmem_limit_bytes=60 * 1024 * 1024
        ),
    )(*arrays)


def solution(mesh):
    dims = (mesh.shape["pipe"], mesh.shape["ctx"], mesh.shape["dp"])
    return jax.shard_map(
        functools.partial(per_device, dims),
        mesh=mesh,
        in_specs=(
            P("dp", "ctx", None),
            P("dp", "ctx", None),
            P("pipe", None, None),
            P("pipe", None, None),
            P("pipe", None, None),
            P("pipe", None, None),
            P("pipe", None),
            P("pipe", None),
            P("pipe", None, None),
            P("pipe", None, None),
            P("pipe", "dp", "ctx", None),
            P("pipe", "dp", "ctx", None),
        ),
        out_specs=(
            P("pipe", "dp", "ctx", None),
            P("pipe", "dp", "ctx", None),
            P("pipe", ("ctx", "dp"), None),
        ),
        check_vma=False,
    )
```

```python
import functools

import jax
import jax.numpy as jnp
from jax import lax
from jax.experimental import pallas as pl
from jax.experimental.pallas import tpu as pltpu
from jax.sharding import PartitionSpec as P

MESH = pl.DeviceIdType.MESH
EPSILON = 1e-06
EXACT = lax.Precision.HIGHEST
BF = jnp.bfloat16
F32 = jnp.float32
HEADS = 8
DIM = 128
TOK = 256
WIDTH = 1024
CH = 4
COLS = WIDTH // CH
UNIT = 32
GROUP = 8
PIECES = 2
HANDS = 2


def mm(a, b):
    return jnp.dot(a, b, preferred_element_type=F32)


def mm_nt(a, b):
    return lax.dot_general(a, b, (((1,), (1,)), ((), ())), preferred_element_type=F32)


def level_mask(size):
    row = lax.broadcasted_iota(jnp.int32, (DIM, DIM), 0)
    col = lax.broadcasted_iota(jnp.int32, (DIM, DIM), 1)
    if size == 0:
        return (row == col).astype(F32)
    if size == DIM:
        return (row >= col).astype(F32)
    same = (row // (2 * size)) == (col // (2 * size))
    return (same & ((row // size) > (col // size))).astype(F32)


LEVELS = (1, 2, 4, 8, 16, 32, 64)


def block_inverses(parts, masks):
    eye = masks[0]
    results = [eye - a * masks[1] for a in parts]
    for level in range(2, 8):
        offs = [a * masks[level] for a in parts]
        inner = [mm(o, t).astype(BF) for o, t in zip(offs, results)]
        results = [t - mm(t, y).astype(BF) for t, y in zip(results, inner)]
    return results


def head_maps(heads, proj, rstd, beta, cum, cum_rows, masks, low, put):
    first, second = slice(0, DIM), slice(DIM, TOK)
    state = []
    for h in heads:
        q = proj[:, pl.ds(h * DIM, DIM)] * rstd
        k = proj[:, pl.ds(WIDTH + h * DIM, DIM)] * rstd
        v = proj[:, pl.ds(2 * WIDTH + h * DIM, DIM)] * rstd
        q = q * (lax.rsqrt(jnp.sum(q * q, axis=-1, keepdims=True) + EPSILON) * DIM ** -0.5)
        k = k * lax.rsqrt(jnp.sum(k * k, axis=-1, keepdims=True) + EPSILON)
        b = beta[:, h : h + 1]
        c = jnp.broadcast_to(cum[:, HEADS + h : HEADS + h + 1], (TOK, DIM))
        row = cum_rows[HEADS + h : HEADS + h + 1, :]
        growth = jnp.exp(c)
        last = c[TOK - 1 : TOK, :]
        qb, kb, kbeta = q.astype(BF), k.astype(BF), (k * b).astype(BF)
        d11 = jnp.exp(jnp.minimum(c[first] - row[:, first], 0.0))
        d21 = jnp.exp(jnp.minimum(c[second] - row[:, first], 0.0))
        d22 = jnp.exp(jnp.minimum(c[second] - row[:, second], 0.0))
        lhs = jnp.concatenate([kbeta, qb], axis=0)
        g1 = mm_nt(lhs, kb[first])
        g2 = mm_nt(jnp.concatenate([kbeta[second], qb[second]], axis=0), kb[second])
        a11 = (g1[0:128] * d11).astype(BF)
        a21 = (g1[128:256] * d21).astype(BF)
        s11 = (g1[256:384] * (d11 * low)).astype(BF)
        s21 = (g1[384:512] * d21).astype(BF)
        a22 = (g2[0:128] * d22).astype(BF)
        s22 = (g2[128:256] * (d22 * low)).astype(BF)
        rhs = jnp.concatenate([(k * (growth * b)).astype(BF), (v * b).astype(BF)], axis=1)
        tail = (k * jnp.exp(last - c)).T.astype(BF)
        state.append((a11, a22, a21, s11, s21, s22, rhs, tail, q * growth, jnp.exp(last)))
    inverses = block_inverses([s[0] for s in state] + [s[1] for s in state], masks)
    n = len(state)
    x1 = [mm(inverses[i], state[i][6][first]).astype(BF) for i in range(n)]
    r2 = [(state[i][6][second].astype(F32) - mm(state[i][2], x1[i])).astype(BF) for i in range(n)]
    x2 = [mm(inverses[n + i], r2[i]).astype(BF) for i in range(n)]
    for i, h in enumerate(heads):
        _, _, _, s11, s21, s22, _, tail, qg, fade = state[i]
        x = jnp.concatenate([x1[i], x2[i]], axis=0)
        z1 = mm(s11, x1[i])
        z2 = mm(jnp.concatenate([s21, s22], axis=1), x)
        kx = mm(tail, x)
        put(h, qg, z1, z2, kx, fade)


def kernel(
    dims,
    down_in, up_in, down_qkv, up_qkv, down_gates, up_gates, down_rates, up_rates,
    down_wo, up_wo, down_ct, up_ct,
    down_out, up_out, grad_out,
    wqkv, wo, wg, xbuf, ybuf, proj, hid, maskb, pmap, rmap, mmap, bmap, sin, sout,
    cot, ht, hg, part, gbuf, gsum,
    w_sem, wo_sem, x_recv, x_send, y_sem, s_recv, s_send, ct_recv, ct_send,
    h_recv, h_send, g_recv, g_send, go_sem,
):
    sections, spans, copies = dims
    p, c, d = lax.axis_index("pipe"), lax.axis_index("ctx"), lax.axis_index("dp")
    low_half = p < sections // 2
    share = WIDTH // (spans * copies)
    column = WIDTH // spans

    def is_down(t):
        return low_half == (t == 0)

    def at(pipe, ctx, dp):
        return (pipe, ctx, dp)

    def remote(src, dst, send, recv, where):
        return pltpu.make_async_remote_copy(
            src_ref=src, dst_ref=dst, send_sem=send, recv_sem=recv,
            device_id=where, device_id_type=MESH,
        )

    def weight_copy(t, n, qkv):
        rows = pl.ds(n * COLS, COLS)
        return pltpu.make_async_copy(qkv.at[0, rows], wqkv.at[t, rows], w_sem.at[t, n])

    def out_copy(t, out):
        return pltpu.make_async_copy(out.at[0], wo.at[t], wo_sem.at[t])

    def start_weights(t, qkv, out):
        for n in range(CH):
            weight_copy(t, n, qkv).start()
        out_copy(t, out).start()

    def input_copy(src, n):
        return pltpu.make_async_copy(
            src.at[0, :, pl.ds(n * COLS, COLS)], xbuf.at[0, n], x_recv.at[0, n]
        )

    @pl.when(p == 0)
    def _():
        for n in range(CH):
            input_copy(down_in, n).start()

    @pl.when(p == sections - 1)
    def _():
        for n in range(CH):
            input_copy(up_in, n).start()

    def load(t):
        @pl.when(is_down(t))
        def _():
            start_weights(t, down_qkv, down_wo)

        @pl.when(jnp.logical_not(is_down(t)))
        def _():
            start_weights(t, up_qkv, up_wo)

    load(0)

    barrier = pltpu.get_barrier_semaphore()
    mirror = sections - 1 - p
    pair = p + 1 - 2 * lax.rem(p, 2)
    peers = [at(pair, c, d), at(mirror, c, d)]
    for k in range(1, spans):
        other = lax.rem(c + k, spans)
        peers += [at(p, other, d), at(mirror, other, d)]
    for k in range(1, copies):
        peers.append(at(p, c, lax.rem(d + k, copies)))
    for peer in peers:
        pl.semaphore_signal(barrier, inc=1, device_id=peer, device_id_type=MESH)

    for level, size in enumerate((0,) + LEVELS + (DIM,)):
        maskb[level] = level_mask(size).astype(BF)
    for t in range(2):
        wg[t, 2 * HEADS :, :] = jnp.zeros((DIM - 2 * HEADS, WIDTH), BF)
        wg[t, 0 : 2 * HEADS, :] = jnp.where(is_down(t), down_gates[0], up_gates[0])

    def cot_own(t, source):
        return pltpu.make_async_copy(source.at[0, 0], cot.at[t, d], ct_recv.at[t, d])

    def cot_copy(t, source, k):
        return remote(
            source.at[0, 0], cot.at[t, d], ct_send.at[t, k - 1], ct_recv.at[t, d],
            at(p, c, lax.rem(d + k, copies)),
        )

    def start_cot(t, source):
        cot_own(t, source).start()
        for k in range(1, copies):
            cot_copy(t, source, k).start()

    def start_cots(t):
        @pl.when(is_down(t))
        def _():
            start_cot(t, down_ct)

        @pl.when(jnp.logical_not(is_down(t)))
        def _():
            start_cot(t, up_ct)

    def meet():
        pl.semaphore_wait(barrier, len(peers))
        start_cots(0)

    outer = (p == 0) | (p == sections - 1)

    @pl.when(jnp.logical_not(outer))
    def _():
        meet()

    def state_copy(t, h):
        return remote(
            sout.at[t, h], sin.at[t, h], s_send.at[t, h], s_recv.at[t, h],
            at(p, lax.rem(c + 1, spans), d),
        )

    def stage_of(t):
        early = jnp.where(low_half, p, sections - 1 - p)
        return jnp.where(t == 0, early, sections - 1 - early)

    def stream_copy(t, n):
        slot = jnp.where(stage_of(t) == 0, 0, 1)
        to = jnp.clip(jnp.where(is_down(t), p + 1, p - 1), 0, sections - 1)
        return remote(
            ybuf.at[t, n], xbuf.at[slot, n], x_send.at[t, n], x_recv.at[slot, n], at(to, c, d)
        )

    def result_copy(t, n, out):
        return pltpu.make_async_copy(
            ybuf.at[t, n], out.at[0, 0, :, pl.ds(n * COLS, COLS)], y_sem.at[t, n]
        )

    def hidden_own(t, piece):
        rows = pl.ds(piece * (spans * share // PIECES), spans * share // PIECES)
        return pltpu.make_async_copy(
            ht.at[t, d, rows], hg.at[t, d, rows], h_recv.at[t, d, piece]
        )

    def hidden_copy(t, k, piece):
        to = lax.rem(d + k, copies)
        rows = pl.ds(piece * (spans * share // PIECES), spans * share // PIECES)
        return remote(
            ht.at[t, to, rows], hg.at[t, d, rows], h_send.at[t, k - 1, piece],
            h_recv.at[t, d, piece], at(p, c, to),
        )

    def grad_own(t):
        return pltpu.make_async_copy(part.at[t, c], gbuf.at[c], g_recv.at[c])

    def grad_copy(t, k):
        to = lax.rem(c + k, spans)
        slot = c + jnp.where(is_down(t), 0, spans)
        pipe = jnp.where(is_down(t), p, mirror)
        return remote(part.at[t, to], gbuf.at[slot], g_send.at[t, k], g_recv.at[slot], at(pipe, to, d))

    def rates_of(t):
        rates = jnp.where(is_down(t), down_rates[...], up_rates[...])
        return jnp.concatenate(
            [jnp.zeros((1, HEADS), F32), rates, jnp.zeros((1, DIM - 2 * HEADS), F32)], axis=1
        )

    def gate_values(logits, rates):
        beta = jax.nn.sigmoid(logits)
        log_decay = -rates * (jnp.maximum(logits, 0.0) + jnp.log1p(jnp.exp(-jnp.abs(logits))))
        row = lax.broadcasted_iota(jnp.int32, (TOK, TOK), 0)
        col = lax.broadcasted_iota(jnp.int32, (TOK, TOK), 1)
        cum = jnp.dot(
            (row >= col).astype(F32), log_decay, preferred_element_type=F32, precision=EXACT
        )
        return beta, cum, cum.T

    def section(t):
        square = jnp.zeros((TOK, 1), F32)
        logits = jnp.zeros((TOK, DIM), F32)
        for n in range(CH):
            pltpu.make_async_copy(xbuf.at[t, n], xbuf.at[t, n], x_recv.at[t, n]).wait()
            weight_copy(t, n, down_qkv).wait()
            x = xbuf[t, n]
            xf = x.astype(F32)
            square += jnp.sum(xf * xf, axis=-1, keepdims=True)
            logits += mm_nt(x, wg[t, :, n * COLS : (n + 1) * COLS])
            if n == CH - 1:
                rstd = lax.rsqrt(square * (1.0 / WIDTH) + EPSILON)
                beta, cum, cum_rows = gate_values(logits * rstd, rates_of(t))
            for j in range(6):
                block = slice(512 * j, 512 * (j + 1))
                product = mm(x, wqkv[t, n * COLS : (n + 1) * COLS, block])
                if n == 0:
                    proj[:, block] = product
                else:
                    proj[:, block] += product

        @pl.when(t == 0)
        def _():
            load(1)

        masks = [maskb[level] for level in range(8)]
        low = maskb[8].astype(F32)
        eye = maskb[0].astype(F32)

        def put(h, qg, z1, z2, kx, fade):
            pmap[h, 0:DIM] = (qg[0:DIM] - z1[:, 0:DIM]).astype(BF)
            pmap[h, DIM:TOK] = (qg[DIM:TOK] - z2[:, 0:DIM]).astype(BF)
            rmap[h, 0:DIM] = z1[:, DIM:TOK]
            rmap[h, DIM:TOK] = z2[:, DIM:TOK]
            mmap[h] = (eye * fade - kx[:, 0:DIM]).astype(BF)
            bmap[h] = kx[:, DIM:TOK]

        for start in range(0, HEADS, GROUP):
            head_maps(
                range(start, start + GROUP), proj, rstd, beta, cum, cum_rows, masks, low, put
            )

        @pl.when((t == 0) & outer)
        def _():
            meet()

        for h in range(HEADS):
            @pl.when(c == 0)
            def _():
                sin[t, h] = jnp.zeros((DIM, DIM), BF)

            @pl.when(c > 0)
            def _():
                state_copy(t, h).wait_recv()

            s = sin[t, h]
            sout[t, h] = (mm(mmap[h], s) + bmap[h]).astype(BF)

            @pl.when(c < spans - 1)
            def _():
                state_copy(t, h).start()

            o = mm(pmap[h], s) + rmap[h]
            o = o * lax.rsqrt(jnp.mean(o * o, axis=-1, keepdims=True) + EPSILON)
            o = o.astype(BF)
            hid[:, h * DIM : (h + 1) * DIM] = o
            flipped = o.T
            for u in range(DIM // UNIT):
                row0 = h * DIM + u * UNIT
                span, rest = row0 // column, row0 % column
                to, i = rest // share, rest % share
                ht[t, to, span * share + i : span * share + i + UNIT] = flipped[
                    u * UNIT : (u + 1) * UNIT
                ]
            if h % (HEADS // PIECES) == HEADS // PIECES - 1:
                piece = h // (HEADS // PIECES)
                hidden_own(t, piece).start()
                for k in range(1, copies):
                    hidden_copy(t, k, piece).start()

        out_copy(t, down_wo).wait()
        for n in range(CH):
            block = slice(n * COLS, (n + 1) * COLS)
            y = xbuf[t, n].astype(F32) + mm(hid[...], wo[t, :, block])
            ybuf[t, n] = y.astype(BF)

            @pl.when(stage_of(t) < sections - 1)
            def _():
                stream_copy(t, n).start()

            @pl.when(is_down(t))
            def _():
                result_copy(t, n, down_out).start()

            @pl.when(jnp.logical_not(is_down(t)))
            def _():
                result_copy(t, n, up_out).start()

        @pl.when(t == 0)
        def _():
            start_cots(1)

    def gradient(t):
        for j in range(copies):
            pltpu.make_async_copy(cot.at[t, j], cot.at[t, j], ct_recv.at[t, j]).wait()
            for piece in range(PIECES):
                rows = pl.ds(piece * (spans * share // PIECES), spans * share // PIECES)
                pltpu.make_async_copy(
                    hg.at[t, j, rows], hg.at[t, j, rows], h_recv.at[t, j, piece]
                ).wait()
        for n in range(CH):
            block = slice(n * COLS, (n + 1) * COLS)
            total = mm(hg[t, 0], cot[t, 0, :, block])
            for j in range(1, copies):
                total += mm(hg[t, j], cot[t, j, :, block])
            part[t, :, :, block] = total.astype(BF).reshape(spans, share, COLS)
        for k in range(1, spans):
            grad_copy(t, k).start()

        @pl.when(is_down(t))
        def _():
            grad_own(t).start()

        @pl.when(jnp.logical_not(is_down(t)))
        def _():
            grad_copy(t, 0).start()

    def turn(i, carry):
        middle = jnp.where(outer, 2, 1)
        is_section = (i == 0) | (i == middle)

        @pl.when(is_section)
        def _():
            section(jnp.where(i == 0, 0, 1))

        @pl.when(jnp.logical_not(is_section))
        def _():
            gradient(jnp.where(i == 3, 1, 0))

        return carry

    lax.fori_loop(0, 4, turn, 0)

    for j in range(2 * spans):
        pltpu.make_async_copy(gbuf.at[j], gbuf.at[j], g_recv.at[j]).wait()
    total = gbuf[0].astype(F32)
    for j in range(1, 2 * spans):
        total += gbuf[j].astype(F32)
    gsum[...] = total
    final = pltpu.make_async_copy(gsum, grad_out.at[0], go_sem)
    final.start()

    for t in range(2):
        for n in range(CH):
            result_copy(t, n, down_out).wait()

            @pl.when(stage_of(t) < sections - 1)
            def _():
                stream_copy(t, n).wait_send()

        @pl.when(c < spans - 1)
        def _():
            for h in range(HEADS):
                state_copy(t, h).wait_send()

        for k in range(1, copies):
            cot_copy(t, down_ct, k).wait_send()
            for piece in range(PIECES):
                hidden_copy(t, k, piece).wait_send()
        for k in range(1, spans):
            grad_copy(t, k).wait_send()

        @pl.when(jnp.logical_not(is_down(t)))
        def _():
            grad_copy(t, 0).wait_send()

    final.wait()


def hand_over(down_in, up_in, grad_in, down_out, up_out, grad_out, sems):
    rows = TOK // HANDS
    moves = []
    for i, (src, dst) in enumerate(((down_in, down_out), (up_in, up_out))):
        for n in range(HANDS):
            part = (0, 0, pl.ds(n * rows, rows))
            moves.append(
                pltpu.make_async_copy(src.at[part], dst.at[part], sems.at[i * HANDS + n])
            )
    moves.append(pltpu.make_async_copy(grad_in, grad_out, sems.at[2 * HANDS]))
    for move in moves:
        move.start()
    for move in moves:
        move.wait()


def per_device(dims, *arrays):
    sections, spans, copies = dims
    share = WIDTH // (spans * copies)
    hbm = pl.BlockSpec(memory_space=pl.ANY)
    vmem = pl.BlockSpec(memory_space=pltpu.VMEM)
    dma = pltpu.SemaphoreType.DMA
    down_acts, up_acts, grad = pl.pallas_call(
        functools.partial(kernel, dims),
        out_shape=(
            jax.ShapeDtypeStruct((1, 1, TOK, WIDTH), BF),
            jax.ShapeDtypeStruct((1, 1, TOK, WIDTH), BF),
            jax.ShapeDtypeStruct((1, share, WIDTH), F32),
        ),
        in_specs=[hbm] * 4 + [vmem] * 4 + [hbm] * 4,
        out_specs=(hbm, hbm, hbm),
        scratch_shapes=[
            pltpu.VMEM((2, WIDTH, 3 * WIDTH), BF),
            pltpu.VMEM((2, WIDTH, WIDTH), BF),
            pltpu.VMEM((2, DIM, WIDTH), BF),
            pltpu.VMEM((2, CH, TOK, COLS), BF),
            pltpu.VMEM((2, CH, TOK, COLS), BF),
            pltpu.VMEM((TOK, 3 * WIDTH), F32),
            pltpu.VMEM((TOK, WIDTH), BF),
            pltpu.VMEM((9, DIM, DIM), BF),
            pltpu.VMEM((HEADS, TOK, DIM), BF),
            pltpu.VMEM((HEADS, TOK, DIM), F32),
            pltpu.VMEM((HEADS, DIM, DIM), BF),
            pltpu.VMEM((HEADS, DIM, DIM), F32),
            pltpu.VMEM((2, HEADS, DIM, DIM), BF),
            pltpu.VMEM((2, HEADS, DIM, DIM), BF),
            pltpu.VMEM((2, copies, TOK, WIDTH), BF),
            pltpu.VMEM((2, copies, spans * share, TOK), BF),
            pltpu.VMEM((2, copies, spans * share, TOK), BF),
            pltpu.VMEM((2, spans, share, WIDTH), BF),
            pltpu.VMEM((2 * spans, share, WIDTH), BF),
            pltpu.VMEM((share, WIDTH), F32),
            dma((2, CH)),
            dma((2,)),
            dma((2, CH)),
            dma((2, CH)),
            dma((2, CH)),
            dma((2, HEADS)),
            dma((2, HEADS)),
            dma((2, copies)),
            dma((2, copies)),
            dma((2, copies, PIECES)),
            dma((2, copies, PIECES)),
            dma((2 * spans,)),
            dma((2, spans)),
            dma,
        ],
        compiler_params=pltpu.CompilerParams(
            collective_id=0, has_side_effects=True, vmem_limit_bytes=60 * 1024 * 1024
        ),
    )(*arrays[:4], *(jnp.swapaxes(gates, 1, 2) for gates in arrays[4:6]), *arrays[6:])
    return pl.pallas_call(
        hand_over,
        out_shape=tuple(jax.ShapeDtypeStruct(a.shape, a.dtype) for a in (down_acts, up_acts, grad)),
        in_specs=[hbm] * 3,
        out_specs=(hbm, hbm, hbm),
        scratch_shapes=[dma((2 * HANDS + 1,))],
    )(down_acts, up_acts, grad)


def solution(mesh):
    dims = (mesh.shape["pipe"], mesh.shape["ctx"], mesh.shape["dp"])
    return jax.shard_map(
        functools.partial(per_device, dims),
        mesh=mesh,
        in_specs=(
            P("dp", "ctx", None),
            P("dp", "ctx", None),
            P("pipe", None, None),
            P("pipe", None, None),
            P("pipe", None, None),
            P("pipe", None, None),
            P("pipe", None),
            P("pipe", None),
            P("pipe", None, None),
            P("pipe", None, None),
            P("pipe", "dp", "ctx", None),
            P("pipe", "dp", "ctx", None),
        ),
        out_specs=(
            P("pipe", "dp", "ctx", None),
            P("pipe", "dp", "ctx", None),
            P("pipe", ("ctx", "dp"), None),
        ),
        check_vma=False,
    )
```

```python
import functools

import jax
import jax.numpy as jnp
from jax import lax
from jax.experimental import pallas as pl
from jax.experimental.pallas import tpu as pltpu
from jax.sharding import PartitionSpec as P

MESH = pl.DeviceIdType.MESH
EPSILON = 1e-06
EXACT = lax.Precision.HIGHEST
BF = jnp.bfloat16
F32 = jnp.float32
HEADS = 8
DIM = 128
TOK = 256
WIDTH = 1024
CH = 4
COLS = WIDTH // CH
UNIT = 32
GROUP = 8
PIECES = 2
HANDS = 2


def mm(a, b):
    return jnp.dot(a, b, preferred_element_type=F32)


def mm_nt(a, b):
    return lax.dot_general(a, b, (((1,), (1,)), ((), ())), preferred_element_type=F32)


def level_mask(size):
    row = lax.broadcasted_iota(jnp.int32, (DIM, DIM), 0)
    col = lax.broadcasted_iota(jnp.int32, (DIM, DIM), 1)
    if size == 0:
        return (row == col).astype(F32)
    if size == DIM:
        return (row >= col).astype(F32)
    same = (row // (2 * size)) == (col // (2 * size))
    return (same & ((row // size) > (col // size))).astype(F32)


LEVELS = (1, 2, 4, 8, 16, 32, 64)


def block_inverses(parts, masks):
    eye = masks[0]
    results = [eye - a * masks[1] for a in parts]
    for level in range(2, 8):
        offs = [a * masks[level] for a in parts]
        inner = [mm(o, t).astype(BF) for o, t in zip(offs, results)]
        results = [t - mm(t, y).astype(BF) for t, y in zip(results, inner)]
    return results


def head_maps(heads, proj, rstd, beta, cum, cum_rows, masks, low, put):
    first, second = slice(0, DIM), slice(DIM, TOK)
    state = []
    for h in heads:
        q = proj[:, pl.ds(h * DIM, DIM)] * rstd
        k = proj[:, pl.ds(WIDTH + h * DIM, DIM)] * rstd
        v = proj[:, pl.ds(2 * WIDTH + h * DIM, DIM)] * rstd
        q = q * (lax.rsqrt(jnp.sum(q * q, axis=-1, keepdims=True) + EPSILON) * DIM ** -0.5)
        k = k * lax.rsqrt(jnp.sum(k * k, axis=-1, keepdims=True) + EPSILON)
        b = beta[:, h : h + 1]
        c = jnp.broadcast_to(cum[:, HEADS + h : HEADS + h + 1], (TOK, DIM))
        row = cum_rows[HEADS + h : HEADS + h + 1, :]
        growth = jnp.exp(c)
        last = c[TOK - 1 : TOK, :]
        qb, kb, kbeta = q.astype(BF), k.astype(BF), (k * b).astype(BF)
        d11 = jnp.exp(jnp.minimum(c[first] - row[:, first], 0.0))
        d21 = jnp.exp(jnp.minimum(c[second] - row[:, first], 0.0))
        d22 = jnp.exp(jnp.minimum(c[second] - row[:, second], 0.0))
        lhs = jnp.concatenate([kbeta, qb], axis=0)
        g1 = mm_nt(lhs, kb[first])
        g2 = mm_nt(jnp.concatenate([kbeta[second], qb[second]], axis=0), kb[second])
        a11 = (g1[0:128] * d11).astype(BF)
        a21 = (g1[128:256] * d21).astype(BF)
        s11 = (g1[256:384] * (d11 * low)).astype(BF)
        s21 = (g1[384:512] * d21).astype(BF)
        a22 = (g2[0:128] * d22).astype(BF)
        s22 = (g2[128:256] * (d22 * low)).astype(BF)
        rhs = jnp.concatenate([(k * (growth * b)).astype(BF), (v * b).astype(BF)], axis=1)
        tail = (k * jnp.exp(last - c)).T.astype(BF)
        state.append((a11, a22, a21, s11, s21, s22, rhs, tail, q * growth, jnp.exp(last)))
    inverses = block_inverses([s[0] for s in state] + [s[1] for s in state], masks)
    n = len(state)
    x1 = [mm(inverses[i], state[i][6][first]).astype(BF) for i in range(n)]
    r2 = [(state[i][6][second].astype(F32) - mm(state[i][2], x1[i])).astype(BF) for i in range(n)]
    x2 = [mm(inverses[n + i], r2[i]).astype(BF) for i in range(n)]
    for i, h in enumerate(heads):
        _, _, _, s11, s21, s22, _, tail, qg, fade = state[i]
        x = jnp.concatenate([x1[i], x2[i]], axis=0)
        z1 = mm(s11, x1[i])
        z2 = mm(jnp.concatenate([s21, s22], axis=1), x)
        kx = mm(tail, x)
        put(h, qg, z1, z2, kx, fade)


def kernel(
    dims,
    down_in, up_in, down_qkv, up_qkv, down_gates, up_gates, down_rates, up_rates,
    down_wo, up_wo, down_ct, up_ct,
    down_out, up_out, grad_out,
    wqkv, wo, wg, xbuf, ybuf, proj, hid, maskb, pmap, rmap, mmap, bmap, sin, sout,
    cot, ht, hg, part, gbuf, gsum,
    w_sem, wo_sem, x_recv, x_send, y_sem, s_recv, s_send, ct_recv, ct_send,
    h_recv, h_send, g_recv, g_send, go_sem,
):
    sections, spans, copies = dims
    p, c, d = lax.axis_index("pipe"), lax.axis_index("ctx"), lax.axis_index("dp")
    low_half = p < sections // 2
    share = WIDTH // (spans * copies)
    column = WIDTH // spans

    def is_down(t):
        return low_half == (t == 0)

    def at(pipe, ctx, dp):
        return (pipe, ctx, dp)

    def remote(src, dst, send, recv, where):
        return pltpu.make_async_remote_copy(
            src_ref=src, dst_ref=dst, send_sem=send, recv_sem=recv,
            device_id=where, device_id_type=MESH,
        )

    def weight_copy(t, n, qkv):
        rows = pl.ds(n * COLS, COLS)
        return pltpu.make_async_copy(qkv.at[0, rows], wqkv.at[t, rows], w_sem.at[t, n])

    def out_copy(t, out):
        return pltpu.make_async_copy(out.at[0], wo.at[t], wo_sem.at[t])

    def start_weights(t, qkv, out):
        for n in range(CH):
            weight_copy(t, n, qkv).start()
        out_copy(t, out).start()

    def input_copy(src, n):
        return pltpu.make_async_copy(
            src.at[0, :, pl.ds(n * COLS, COLS)], xbuf.at[0, n], x_recv.at[0, n]
        )

    @pl.when(p == 0)
    def _():
        for n in range(CH):
            input_copy(down_in, n).start()

    @pl.when(p == sections - 1)
    def _():
        for n in range(CH):
            input_copy(up_in, n).start()

    def load(t):
        @pl.when(is_down(t))
        def _():
            start_weights(t, down_qkv, down_wo)

        @pl.when(jnp.logical_not(is_down(t)))
        def _():
            start_weights(t, up_qkv, up_wo)

    load(0)

    barrier = pltpu.get_barrier_semaphore()
    mirror = sections - 1 - p
    pair = p + 1 - 2 * lax.rem(p, 2)
    peers = [at(pair, c, d), at(mirror, c, d)]
    for k in range(1, spans):
        other = lax.rem(c + k, spans)
        peers += [at(p, other, d), at(mirror, other, d)]
    for k in range(1, copies):
        peers.append(at(p, c, lax.rem(d + k, copies)))
    for peer in peers:
        pl.semaphore_signal(barrier, inc=1, device_id=peer, device_id_type=MESH)

    for level, size in enumerate((0,) + LEVELS + (DIM,)):
        maskb[level] = level_mask(size).astype(BF)
    for t in range(2):
        wg[t, 2 * HEADS :, :] = jnp.zeros((DIM - 2 * HEADS, WIDTH), BF)
        wg[t, 0 : 2 * HEADS, :] = jnp.where(is_down(t), down_gates[0], up_gates[0])

    def cot_own(t, source):
        return pltpu.make_async_copy(source.at[0, 0], cot.at[t, d], ct_recv.at[t, d])

    def cot_copy(t, source, k):
        return remote(
            source.at[0, 0], cot.at[t, d], ct_send.at[t, k - 1], ct_recv.at[t, d],
            at(p, c, lax.rem(d + k, copies)),
        )

    def start_cot(t, source):
        cot_own(t, source).start()
        for k in range(1, copies):
            cot_copy(t, source, k).start()

    def start_cots(t):
        @pl.when(is_down(t))
        def _():
            start_cot(t, down_ct)

        @pl.when(jnp.logical_not(is_down(t)))
        def _():
            start_cot(t, up_ct)

    def meet():
        pl.semaphore_wait(barrier, len(peers))
        start_cots(0)

    outer = (p == 0) | (p == sections - 1)

    @pl.when(jnp.logical_not(outer))
    def _():
        meet()

    def state_copy(t, h):
        return remote(
            sout.at[t, h], sin.at[t, h], s_send.at[t, h], s_recv.at[t, h],
            at(p, lax.rem(c + 1, spans), d),
        )

    def stage_of(t):
        early = jnp.where(low_half, p, sections - 1 - p)
        return jnp.where(t == 0, early, sections - 1 - early)

    def stream_copy(t, n):
        slot = jnp.where(stage_of(t) == 0, 0, 1)
        to = jnp.clip(jnp.where(is_down(t), p + 1, p - 1), 0, sections - 1)
        return remote(
            ybuf.at[t, n], xbuf.at[slot, n], x_send.at[t, n], x_recv.at[slot, n], at(to, c, d)
        )

    def result_copy(t, n, out):
        return pltpu.make_async_copy(
            ybuf.at[t, n], out.at[0, 0, :, pl.ds(n * COLS, COLS)], y_sem.at[t, n]
        )

    def hidden_own(t, piece):
        rows = pl.ds(piece * (spans * share // PIECES), spans * share // PIECES)
        return pltpu.make_async_copy(
            ht.at[t, d, rows], hg.at[t, d, rows], h_recv.at[t, d, piece]
        )

    def hidden_copy(t, k, piece):
        to = lax.rem(d + k, copies)
        rows = pl.ds(piece * (spans * share // PIECES), spans * share // PIECES)
        return remote(
            ht.at[t, to, rows], hg.at[t, d, rows], h_send.at[t, k - 1, piece],
            h_recv.at[t, d, piece], at(p, c, to),
        )

    def grad_own(t):
        return pltpu.make_async_copy(part.at[t, c], gbuf.at[c], g_recv.at[c])

    def grad_copy(t, k):
        to = lax.rem(c + k, spans)
        slot = c + jnp.where(is_down(t), 0, spans)
        pipe = jnp.where(is_down(t), p, mirror)
        return remote(part.at[t, to], gbuf.at[slot], g_send.at[t, k], g_recv.at[slot], at(pipe, to, d))

    def rates_of(t):
        rates = jnp.where(is_down(t), down_rates[...], up_rates[...])
        return jnp.concatenate(
            [jnp.zeros((1, HEADS), F32), rates, jnp.zeros((1, DIM - 2 * HEADS), F32)], axis=1
        )

    def gate_values(logits, rates):
        beta = jax.nn.sigmoid(logits)
        log_decay = -rates * (jnp.maximum(logits, 0.0) + jnp.log1p(jnp.exp(-jnp.abs(logits))))
        row = lax.broadcasted_iota(jnp.int32, (TOK, TOK), 0)
        col = lax.broadcasted_iota(jnp.int32, (TOK, TOK), 1)
        cum = jnp.dot(
            (row >= col).astype(F32), log_decay, preferred_element_type=F32, precision=EXACT
        )
        return beta, cum, cum.T

    def section(t):
        square = jnp.zeros((TOK, 1), F32)
        logits = jnp.zeros((TOK, DIM), F32)
        for n in range(CH):
            pltpu.make_async_copy(xbuf.at[t, n], xbuf.at[t, n], x_recv.at[t, n]).wait()
            weight_copy(t, n, down_qkv).wait()
            x = xbuf[t, n]
            xf = x.astype(F32)
            square += jnp.sum(xf * xf, axis=-1, keepdims=True)
            logits += mm_nt(x, wg[t, :, n * COLS : (n + 1) * COLS])
            if n == CH - 1:
                rstd = lax.rsqrt(square * (1.0 / WIDTH) + EPSILON)
                beta, cum, cum_rows = gate_values(logits * rstd, rates_of(t))
            for j in range(6):
                block = slice(512 * j, 512 * (j + 1))
                product = mm(x, wqkv[t, n * COLS : (n + 1) * COLS, block])
                if n == 0:
                    proj[:, block] = product
                else:
                    proj[:, block] += product

        @pl.when(t == 0)
        def _():
            load(1)

        masks = [maskb[level] for level in range(8)]
        low = maskb[8].astype(F32)
        eye = maskb[0].astype(F32)

        def put(h, qg, z1, z2, kx, fade):
            pmap[h, 0:DIM] = (qg[0:DIM] - z1[:, 0:DIM]).astype(BF)
            pmap[h, DIM:TOK] = (qg[DIM:TOK] - z2[:, 0:DIM]).astype(BF)
            rmap[h, 0:DIM] = z1[:, DIM:TOK]
            rmap[h, DIM:TOK] = z2[:, DIM:TOK]
            mmap[h] = (eye * fade - kx[:, 0:DIM]).astype(BF)
            bmap[h] = kx[:, DIM:TOK]

        for start in range(0, HEADS, GROUP):
            head_maps(
                range(start, start + GROUP), proj, rstd, beta, cum, cum_rows, masks, low, put
            )

        @pl.when((t == 0) & outer)
        def _():
            meet()

        for h in range(HEADS):
            @pl.when(c == 0)
            def _():
                sin[t, h] = jnp.zeros((DIM, DIM), BF)

            @pl.when(c > 0)
            def _():
                state_copy(t, h).wait_recv()

            s = sin[t, h]
            sout[t, h] = (mm(mmap[h], s) + bmap[h]).astype(BF)

            @pl.when(c < spans - 1)
            def _():
                state_copy(t, h).start()

            o = mm(pmap[h], s) + rmap[h]
            o = o * lax.rsqrt(jnp.mean(o * o, axis=-1, keepdims=True) + EPSILON)
            o = o.astype(BF)
            hid[:, h * DIM : (h + 1) * DIM] = o
            flipped = o.T
            for u in range(DIM // UNIT):
                row0 = h * DIM + u * UNIT
                span, rest = row0 // column, row0 % column
                to, i = rest // share, rest % share
                ht[t, to, span * share + i : span * share + i + UNIT] = flipped[
                    u * UNIT : (u + 1) * UNIT
                ]
            if h % (HEADS // PIECES) == HEADS // PIECES - 1:
                piece = h // (HEADS // PIECES)
                hidden_own(t, piece).start()
                for k in range(1, copies):
                    hidden_copy(t, k, piece).start()

        out_copy(t, down_wo).wait()
        for n in range(CH):
            block = slice(n * COLS, (n + 1) * COLS)
            y = xbuf[t, n].astype(F32) + mm(hid[...], wo[t, :, block])
            ybuf[t, n] = y.astype(BF)

            @pl.when(stage_of(t) < sections - 1)
            def _():
                stream_copy(t, n).start()

            @pl.when(is_down(t))
            def _():
                result_copy(t, n, down_out).start()

            @pl.when(jnp.logical_not(is_down(t)))
            def _():
                result_copy(t, n, up_out).start()

        @pl.when(t == 0)
        def _():
            start_cots(1)

    def gradient(t):
        for j in range(copies):
            pltpu.make_async_copy(cot.at[t, j], cot.at[t, j], ct_recv.at[t, j]).wait()
            for piece in range(PIECES):
                rows = pl.ds(piece * (spans * share // PIECES), spans * share // PIECES)
                pltpu.make_async_copy(
                    hg.at[t, j, rows], hg.at[t, j, rows], h_recv.at[t, j, piece]
                ).wait()
        for n in range(CH):
            block = slice(n * COLS, (n + 1) * COLS)
            total = mm(hg[t, 0], cot[t, 0, :, block])
            for j in range(1, copies):
                total += mm(hg[t, j], cot[t, j, :, block])
            part[t, :, :, block] = total.astype(BF).reshape(spans, share, COLS)
        for k in range(1, spans):
            grad_copy(t, k).start()

        @pl.when(is_down(t))
        def _():
            grad_own(t).start()

        @pl.when(jnp.logical_not(is_down(t)))
        def _():
            grad_copy(t, 0).start()

    def turn(i, carry):
        middle = jnp.where(outer, 2, 1)
        is_section = (i == 0) | (i == middle)

        @pl.when(is_section)
        def _():
            section(jnp.where(i == 0, 0, 1))

        @pl.when(jnp.logical_not(is_section))
        def _():
            gradient(jnp.where(i == 3, 1, 0))

        return carry

    lax.fori_loop(0, 4, turn, 0)

    for j in range(2 * spans):
        pltpu.make_async_copy(gbuf.at[j], gbuf.at[j], g_recv.at[j]).wait()
    total = gbuf[0].astype(F32)
    for j in range(1, 2 * spans):
        total += gbuf[j].astype(F32)
    gsum[...] = total
    final = pltpu.make_async_copy(gsum, grad_out.at[0], go_sem)
    final.start()

    for t in range(2):
        for n in range(CH):
            result_copy(t, n, down_out).wait()

            @pl.when(stage_of(t) < sections - 1)
            def _():
                stream_copy(t, n).wait_send()

        @pl.when(c < spans - 1)
        def _():
            for h in range(HEADS):
                state_copy(t, h).wait_send()

        for k in range(1, copies):
            cot_copy(t, down_ct, k).wait_send()
            for piece in range(PIECES):
                hidden_copy(t, k, piece).wait_send()
        for k in range(1, spans):
            grad_copy(t, k).wait_send()

        @pl.when(jnp.logical_not(is_down(t)))
        def _():
            grad_copy(t, 0).wait_send()

    final.wait()


def hand_over(down_in, up_in, grad_in, down_out, up_out, grad_out, acts, grad, in_sems, out_sems):
    rows = TOK // HANDS
    moves = []
    for i, (src, dst) in enumerate(((down_in, down_out), (up_in, up_out))):
        for n in range(HANDS):
            part = (0, 0, pl.ds(n * rows, rows))
            moves.append((src.at[part], acts.at[i, pl.ds(n * rows, rows)], dst.at[part]))
    moves.append((grad_in.at[0], grad, grad_out.at[0]))
    loads, stores = [], []
    for i, (src, here, dst) in enumerate(moves):
        loads.append(pltpu.make_async_copy(src, here, in_sems.at[i]))
        stores.append(pltpu.make_async_copy(here, dst, out_sems.at[i]))
        loads[i].start()
    for load, store in zip(loads, stores):
        load.wait()
        store.start()
    for store in stores:
        store.wait()


def per_device(dims, *arrays):
    sections, spans, copies = dims
    share = WIDTH // (spans * copies)
    hbm = pl.BlockSpec(memory_space=pl.ANY)
    vmem = pl.BlockSpec(memory_space=pltpu.VMEM)
    dma = pltpu.SemaphoreType.DMA
    down_acts, up_acts, grad = pl.pallas_call(
        functools.partial(kernel, dims),
        out_shape=(
            jax.ShapeDtypeStruct((1, 1, TOK, WIDTH), BF),
            jax.ShapeDtypeStruct((1, 1, TOK, WIDTH), BF),
            jax.ShapeDtypeStruct((1, share, WIDTH), F32),
        ),
        in_specs=[hbm] * 4 + [vmem] * 4 + [hbm] * 4,
        out_specs=(hbm, hbm, hbm),
        scratch_shapes=[
            pltpu.VMEM((2, WIDTH, 3 * WIDTH), BF),
            pltpu.VMEM((2, WIDTH, WIDTH), BF),
            pltpu.VMEM((2, DIM, WIDTH), BF),
            pltpu.VMEM((2, CH, TOK, COLS), BF),
            pltpu.VMEM((2, CH, TOK, COLS), BF),
            pltpu.VMEM((TOK, 3 * WIDTH), F32),
            pltpu.VMEM((TOK, WIDTH), BF),
            pltpu.VMEM((9, DIM, DIM), BF),
            pltpu.VMEM((HEADS, TOK, DIM), BF),
            pltpu.VMEM((HEADS, TOK, DIM), F32),
            pltpu.VMEM((HEADS, DIM, DIM), BF),
            pltpu.VMEM((HEADS, DIM, DIM), F32),
            pltpu.VMEM((2, HEADS, DIM, DIM), BF),
            pltpu.VMEM((2, HEADS, DIM, DIM), BF),
            pltpu.VMEM((2, copies, TOK, WIDTH), BF),
            pltpu.VMEM((2, copies, spans * share, TOK), BF),
            pltpu.VMEM((2, copies, spans * share, TOK), BF),
            pltpu.VMEM((2, spans, share, WIDTH), BF),
            pltpu.VMEM((2 * spans, share, WIDTH), BF),
            pltpu.VMEM((share, WIDTH), F32),
            dma((2, CH)),
            dma((2,)),
            dma((2, CH)),
            dma((2, CH)),
            dma((2, CH)),
            dma((2, HEADS)),
            dma((2, HEADS)),
            dma((2, copies)),
            dma((2, copies)),
            dma((2, copies, PIECES)),
            dma((2, copies, PIECES)),
            dma((2 * spans,)),
            dma((2, spans)),
            dma,
        ],
        compiler_params=pltpu.CompilerParams(
            collective_id=0, has_side_effects=True, vmem_limit_bytes=60 * 1024 * 1024
        ),
    )(*arrays[:4], *(jnp.swapaxes(gates, 1, 2) for gates in arrays[4:6]), *arrays[6:])
    return pl.pallas_call(
        hand_over,
        out_shape=tuple(jax.ShapeDtypeStruct(a.shape, a.dtype) for a in (down_acts, up_acts, grad)),
        in_specs=[hbm] * 3,
        out_specs=(hbm, hbm, hbm),
        scratch_shapes=[
            pltpu.VMEM((2, TOK, WIDTH), BF),
            pltpu.VMEM((share, WIDTH), F32),
            dma((2 * HANDS + 1,)),
            dma((2 * HANDS + 1,)),
        ],
    )(down_acts, up_acts, grad)


def solution(mesh):
    dims = (mesh.shape["pipe"], mesh.shape["ctx"], mesh.shape["dp"])
    return jax.shard_map(
        functools.partial(per_device, dims),
        mesh=mesh,
        in_specs=(
            P("dp", "ctx", None),
            P("dp", "ctx", None),
            P("pipe", None, None),
            P("pipe", None, None),
            P("pipe", None, None),
            P("pipe", None, None),
            P("pipe", None),
            P("pipe", None),
            P("pipe", None, None),
            P("pipe", None, None),
            P("pipe", "dp", "ctx", None),
            P("pipe", "dp", "ctx", None),
        ),
        out_specs=(
            P("pipe", "dp", "ctx", None),
            P("pipe", "dp", "ctx", None),
            P("pipe", ("ctx", "dp"), None),
        ),
        check_vma=False,
    )
```

```python
import functools

import jax
import jax.numpy as jnp
from jax import lax
from jax.experimental import pallas as pl
from jax.experimental.pallas import tpu as pltpu
from jax.sharding import PartitionSpec as P

MESH = pl.DeviceIdType.MESH
EPSILON = 1e-06
EXACT = lax.Precision.HIGHEST
BF = jnp.bfloat16
F32 = jnp.float32
HEADS = 8
DIM = 128
TOK = 256
WIDTH = 1024
CH = 4
COLS = WIDTH // CH
UNIT = 32
PIECES = 4
CHAIN = ((0, 1, 2, 3), (4, 5), (6, 7))
HANDS = 2


def mm(a, b):
    return jnp.dot(a, b, preferred_element_type=F32)


def mm_nt(a, b):
    return lax.dot_general(a, b, (((1,), (1,)), ((), ())), preferred_element_type=F32)


def level_mask(size):
    row = lax.broadcasted_iota(jnp.int32, (DIM, DIM), 0)
    col = lax.broadcasted_iota(jnp.int32, (DIM, DIM), 1)
    if size == 0:
        return (row == col).astype(F32)
    if size == DIM:
        return (row >= col).astype(F32)
    same = (row // (2 * size)) == (col // (2 * size))
    return (same & ((row // size) > (col // size))).astype(F32)


LEVELS = (1, 2, 4, 8, 16, 32, 64)


def block_inverses(parts, masks):
    eye = masks[0]
    results = [eye - a * masks[1] for a in parts]
    for level in range(2, 8):
        offs = [a * masks[level] for a in parts]
        inner = [mm(o, t).astype(BF) for o, t in zip(offs, results)]
        results = [t - mm(t, y).astype(BF) for t, y in zip(results, inner)]
    return results


def decay_of(gap):
    return jnp.exp(jnp.minimum(gap, 0.0)).astype(BF)


def lane_of(compact, lane):
    return jnp.broadcast_to(compact[:, lane : lane + 1], (TOK, DIM))


def head_maps(heads, proj, rstd, power, beta, cum, select, masks, low, eye, put):
    first, second = slice(0, DIM), slice(DIM, TOK)
    lanes = lax.broadcasted_iota(jnp.int32, (TOK, DIM), 1)
    tail = jnp.exp(cum[TOK - 1 : TOK, :] - cum)
    fade = jnp.exp(cum[TOK - 1 : TOK, :])
    rows = jnp.where(lanes < HEADS, beta, cum).T
    brows = rows.astype(BF)
    tail_rows = tail.T

    def square_sums(start):
        raw = proj[:, start : start + WIDTH]
        return mm((raw * raw).astype(BF), select)

    floor = (EPSILON * DIM) * (square_sums(0) + EPSILON * power)
    nk = rstd * lax.rsqrt(square_sums(WIDTH) * (rstd * rstd) + EPSILON)
    rstd_all = jnp.broadcast_to(rstd, (TOK, DIM))
    state = []
    for h in heads:
        lane = HEADS + h
        q = proj[:, h * DIM : (h + 1) * DIM]
        k = proj[:, WIDTH + h * DIM : WIDTH + (h + 1) * DIM] * lane_of(nk, lane)
        v = proj[:, 2 * WIDTH + h * DIM : 2 * WIDTH + (h + 1) * DIM]
        c = lane_of(cum, lane)
        growth = jnp.exp(c)
        qb, kb = q.astype(BF), k.astype(BF)
        rhs = jnp.concatenate([(k * growth).astype(BF), (v * rstd_all).astype(BF)], axis=1)
        weight = (tail_rows[lane : lane + 1, :] * rows[h : h + 1, :]).astype(BF)
        flipped = kb.T * weight
        qg = q * growth
        crow, brow = rows[lane : lane + 1, :], brows[h : h + 1, :]
        d11 = decay_of(c[first] - crow[:, first]) * brow[:, first]
        d21 = decay_of(c[second] - crow[:, first]) * brow[:, first]
        d22 = decay_of(c[second] - crow[:, second]) * brow[:, second]
        g1 = mm_nt(jnp.concatenate([kb, qb], axis=0), kb[first]).astype(BF)
        g2 = mm_nt(jnp.concatenate([kb[second], qb[second]], axis=0), kb[second]).astype(BF)
        a11 = g1[0:128] * d11
        a21 = g1[128:256] * d21
        s11 = g1[256:384] * (d11 * low)
        s21 = g1[384:512] * d21
        a22 = g2[0:128] * d22
        s22 = g2[128:256] * (d22 * low)
        state.append((a11, a22, a21, s11, s21, s22, rhs, flipped, qg))
    inverses = block_inverses([s[0] for s in state] + [s[1] for s in state], masks)
    n = len(state)
    x1 = [mm(inverses[i], state[i][6][first]).astype(BF) for i in range(n)]
    r2 = [state[i][6][second] - mm(state[i][2], x1[i]).astype(BF) for i in range(n)]
    x2 = [mm(inverses[n + i], r2[i]).astype(BF) for i in range(n)]
    for i, h in enumerate(heads):
        _, _, _, s11, s21, s22, _, flipped, qg = state[i]
        x = jnp.concatenate([x1[i], x2[i]], axis=0)
        z1 = mm(s11, x1[i])
        z2 = mm(jnp.concatenate([s21, s22], axis=1), x)
        kx = mm(flipped, x)
        put(h, qg, z1, z2, kx, eye * fade[:, HEADS + h : HEADS + h + 1])
    return floor


def kernel(
    dims,
    down_in, up_in, down_qkv, up_qkv, down_gates, up_gates, down_rates, up_rates,
    down_wo, up_wo, down_ct, up_ct,
    down_out, up_out, grad_out,
    wqkv, wo, wg, xbuf, ybuf, proj, hid, maskb, select, floor, pmap, rmap, mmap, bmap, sin, sout,
    cot, ht, hg, part, gbuf, gsum,
    w_sem, wo_sem, x_recv, x_send, y_sem, s_recv, s_send, ct_recv, ct_send,
    h_recv, h_send, g_recv, g_send, go_sem,
):
    sections, spans, copies = dims
    p, c, d = lax.axis_index("pipe"), lax.axis_index("ctx"), lax.axis_index("dp")
    low_half = p < sections // 2
    share = WIDTH // (spans * copies)
    column = WIDTH // spans

    def is_down(t):
        return low_half == (t == 0)

    def at(pipe, ctx, dp):
        return (pipe, ctx, dp)

    def remote(src, dst, send, recv, where):
        return pltpu.make_async_remote_copy(
            src_ref=src, dst_ref=dst, send_sem=send, recv_sem=recv,
            device_id=where, device_id_type=MESH,
        )

    def weight_copy(t, n, qkv):
        rows = pl.ds(n * COLS, COLS)
        return pltpu.make_async_copy(qkv.at[0, rows], wqkv.at[t, rows], w_sem.at[t, n])

    def out_copy(t, out):
        return pltpu.make_async_copy(out.at[0], wo.at[t], wo_sem.at[t])

    def start_weights(t, qkv, out):
        for n in range(CH):
            weight_copy(t, n, qkv).start()
        out_copy(t, out).start()

    def input_copy(src, n):
        return pltpu.make_async_copy(
            src.at[0, :, pl.ds(n * COLS, COLS)], xbuf.at[0, n], x_recv.at[0, n]
        )

    @pl.when(p == 0)
    def _():
        for n in range(CH):
            input_copy(down_in, n).start()

    @pl.when(p == sections - 1)
    def _():
        for n in range(CH):
            input_copy(up_in, n).start()

    def load(t):
        @pl.when(is_down(t))
        def _():
            start_weights(t, down_qkv, down_wo)

        @pl.when(jnp.logical_not(is_down(t)))
        def _():
            start_weights(t, up_qkv, up_wo)

    load(0)

    barrier = pltpu.get_barrier_semaphore()
    mirror = sections - 1 - p
    pair = p + 1 - 2 * lax.rem(p, 2)
    peers = [at(pair, c, d), at(mirror, c, d)]
    for k in range(1, spans):
        other = lax.rem(c + k, spans)
        peers += [at(p, other, d), at(mirror, other, d)]
    for k in range(1, copies):
        peers.append(at(p, c, lax.rem(d + k, copies)))
    for peer in peers:
        pl.semaphore_signal(barrier, inc=1, device_id=peer, device_id_type=MESH)

    for level, size in enumerate((0,) + LEVELS + (DIM,)):
        maskb[level] = level_mask(size).astype(BF)
    for h in range(HEADS):
        lanes = lax.broadcasted_iota(jnp.int32, (DIM, DIM), 1)
        select[h * DIM : (h + 1) * DIM] = (lanes == HEADS + h).astype(F32).astype(BF)
    for t in range(2):
        wg[t, 2 * HEADS :, :] = jnp.zeros((DIM - 2 * HEADS, WIDTH), BF)
        wg[t, 0 : 2 * HEADS, :] = jnp.where(is_down(t), down_gates[0], up_gates[0])

    def cot_own(t, source):
        return pltpu.make_async_copy(source.at[0, 0], cot.at[t, d], ct_recv.at[t, d])

    def cot_copy(t, source, k):
        return remote(
            source.at[0, 0], cot.at[t, d], ct_send.at[t, k - 1], ct_recv.at[t, d],
            at(p, c, lax.rem(d + k, copies)),
        )

    def start_cot(t, source):
        cot_own(t, source).start()
        for k in range(1, copies):
            cot_copy(t, source, k).start()

    def start_cots(t):
        @pl.when(is_down(t))
        def _():
            start_cot(t, down_ct)

        @pl.when(jnp.logical_not(is_down(t)))
        def _():
            start_cot(t, up_ct)

    def meet():
        pl.semaphore_wait(barrier, len(peers))
        start_cots(0)

    outer = (p == 0) | (p == sections - 1)

    @pl.when(jnp.logical_not(outer))
    def _():
        meet()

    def state_copy(t, h):
        return remote(
            sout.at[t, h], sin.at[t, h], s_send.at[t, h], s_recv.at[t, h],
            at(p, lax.rem(c + 1, spans), d),
        )

    def stage_of(t):
        early = jnp.where(low_half, p, sections - 1 - p)
        return jnp.where(t == 0, early, sections - 1 - early)

    def stream_copy(t, n):
        slot = jnp.where(stage_of(t) == 0, 0, 1)
        to = jnp.clip(jnp.where(is_down(t), p + 1, p - 1), 0, sections - 1)
        return remote(
            ybuf.at[t, n], xbuf.at[slot, n], x_send.at[t, n], x_recv.at[slot, n], at(to, c, d)
        )

    def result_copy(t, n, out):
        return pltpu.make_async_copy(
            ybuf.at[t, n], out.at[0, 0, :, pl.ds(n * COLS, COLS)], y_sem.at[t, n]
        )

    def hidden_own(t, piece):
        rows = pl.ds(piece * (spans * share // PIECES), spans * share // PIECES)
        return pltpu.make_async_copy(
            ht.at[t, d, rows], hg.at[t, d, rows], h_recv.at[t, d, piece]
        )

    def hidden_copy(t, k, piece):
        to = lax.rem(d + k, copies)
        rows = pl.ds(piece * (spans * share // PIECES), spans * share // PIECES)
        return remote(
            ht.at[t, to, rows], hg.at[t, d, rows], h_send.at[t, k - 1, piece],
            h_recv.at[t, d, piece], at(p, c, to),
        )

    def grad_own(t, to):
        return pltpu.make_async_copy(part.at[t, to], gbuf.at[to], g_recv.at[to])

    def grad_copy(t, to):
        slot = c + jnp.where(is_down(t), 0, spans)
        pipe = jnp.where(is_down(t), p, mirror)
        return remote(
            part.at[t, to], gbuf.at[slot], g_send.at[t, to], g_recv.at[slot], at(pipe, to, d)
        )

    def stays(t, to):
        return (c == to) & is_down(t)

    def rates_of(t):
        rates = jnp.where(is_down(t), down_rates[...], up_rates[...])
        return jnp.concatenate(
            [jnp.zeros((1, HEADS), F32), rates, jnp.zeros((1, DIM - 2 * HEADS), F32)], axis=1
        )

    def gate_values(logits, rates):
        beta = jax.nn.sigmoid(logits)
        log_decay = -rates * (jnp.maximum(logits, 0.0) + jnp.log1p(jnp.exp(-jnp.abs(logits))))
        row = lax.broadcasted_iota(jnp.int32, (TOK, TOK), 0)
        col = lax.broadcasted_iota(jnp.int32, (TOK, TOK), 1)
        cum = jnp.dot(
            (row >= col).astype(F32), log_decay, preferred_element_type=F32, precision=EXACT
        )
        return beta, cum

    def section(t):
        square = jnp.zeros((TOK, 1), F32)
        logits = jnp.zeros((TOK, DIM), F32)
        for n in range(CH):
            pltpu.make_async_copy(xbuf.at[t, n], xbuf.at[t, n], x_recv.at[t, n]).wait()
            weight_copy(t, n, down_qkv).wait()
            x = xbuf[t, n]
            xf = x.astype(F32)
            square += jnp.sum(xf * xf, axis=-1, keepdims=True)
            logits += mm_nt(x, wg[t, :, n * COLS : (n + 1) * COLS])
            if n == CH - 1:
                power = square * (1.0 / WIDTH) + EPSILON
                rstd = lax.rsqrt(power)
                beta, cum = gate_values(logits * rstd, rates_of(t))
            for j in range(6):
                block = slice(512 * j, 512 * (j + 1))
                product = mm(x, wqkv[t, n * COLS : (n + 1) * COLS, block])
                if n == 0:
                    proj[:, block] = product
                else:
                    proj[:, block] += product

        @pl.when(t == 0)
        def _():
            load(1)

        masks = [maskb[level] for level in range(8)]
        low = maskb[8]
        eye = maskb[0].astype(F32)

        def put(h, qg, z1, z2, kx, fade):
            pmap[h, 0:DIM] = (qg[0:DIM] - z1[:, 0:DIM]).astype(BF)
            pmap[h, DIM:TOK] = (qg[DIM:TOK] - z2[:, 0:DIM]).astype(BF)
            rmap[h, 0:DIM] = z1[:, DIM:TOK]
            rmap[h, DIM:TOK] = z2[:, DIM:TOK]
            mmap[h] = (fade - kx[:, 0:DIM]).astype(BF)
            bmap[h] = kx[:, DIM:TOK]

        floor[...] = head_maps(
            range(HEADS), proj, rstd, power, beta, cum, select[...], masks, low, eye, put
        )

        @pl.when((t == 0) & outer)
        def _():
            meet()

        @pl.when(c == 0)
        def _():
            for h in range(HEADS):
                sout[t, h] = bmap[h].astype(BF)
                state_copy(t, h).start()
                sin[t, h] = jnp.zeros((DIM, DIM), BF)

        for group in CHAIN:
            @pl.when(c > 0)
            def _():
                for h in group:
                    state_copy(t, h).wait_recv()

                    @pl.when(c < spans - 1)
                    def _():
                        sout[t, h] = (mm(mmap[h], sin[t, h]) + bmap[h]).astype(BF)
                        state_copy(t, h).start()

            for h in group:
                o = mm(pmap[h], sin[t, h]) + rmap[h]
                level = jnp.mean(o * o, axis=-1, keepdims=True)
                o = o * lax.rsqrt(level + floor[:, HEADS + h : HEADS + h + 1])
                o = o.astype(BF)
                hid[:, h * DIM : (h + 1) * DIM] = o
                flipped = o.T
                for u in range(DIM // UNIT):
                    row0 = h * DIM + u * UNIT
                    span, rest = row0 // column, row0 % column
                    to, i = rest // share, rest % share
                    ht[t, to, span * share + i : span * share + i + UNIT] = flipped[
                        u * UNIT : (u + 1) * UNIT
                    ]
            for piece in range(PIECES):
                last = HEADS // PIECES * (piece + 1) - 1 if spans == HEADS else HEADS - 1
                if last in group:
                    hidden_own(t, piece).start()
                    for k in range(1, copies):
                        hidden_copy(t, k, piece).start()

        out_copy(t, down_wo).wait()
        for n in range(CH):
            block = slice(n * COLS, (n + 1) * COLS)
            y = xbuf[t, n].astype(F32) + mm(hid[...], wo[t, :, block])
            ybuf[t, n] = y.astype(BF)

            @pl.when(stage_of(t) < sections - 1)
            def _():
                stream_copy(t, n).start()

            @pl.when(is_down(t))
            def _():
                result_copy(t, n, down_out).start()

            @pl.when(jnp.logical_not(is_down(t)))
            def _():
                result_copy(t, n, up_out).start()

        @pl.when(t == 0)
        def _():
            start_cots(1)

    def gradient(t):
        for j in range(copies):
            pltpu.make_async_copy(cot.at[t, j], cot.at[t, j], ct_recv.at[t, j]).wait()
        size = spans * share // PIECES
        for piece in range(PIECES):
            rows = pl.ds(piece * size, size)
            for j in range(copies):
                pltpu.make_async_copy(
                    hg.at[t, j, rows], hg.at[t, j, rows], h_recv.at[t, j, piece]
                ).wait()
            total = mm(hg[t, 0, piece * size : (piece + 1) * size], cot[t, 0])
            for j in range(1, copies):
                total += mm(hg[t, j, piece * size : (piece + 1) * size], cot[t, j])
            total = total.astype(BF)
            for row0 in range(0, size, UNIT):
                to, at_row = divmod(piece * size + row0, share)
                part[t, to, at_row : at_row + UNIT] = total[row0 : row0 + UNIT]
                if at_row + UNIT == share:
                    @pl.when(stays(t, to))
                    def _():
                        grad_own(t, to).start()

                    @pl.when(jnp.logical_not(stays(t, to)))
                    def _():
                        grad_copy(t, to).start()

    def turn(i, carry):
        middle = jnp.where(outer, 2, 1)
        is_section = (i == 0) | (i == middle)

        @pl.when(is_section)
        def _():
            section(jnp.where(i == 0, 0, 1))

        @pl.when(jnp.logical_not(is_section))
        def _():
            gradient(jnp.where(i == 3, 1, 0))

        return carry

    lax.fori_loop(0, 4, turn, 0)

    for j in range(2 * spans):
        pltpu.make_async_copy(gbuf.at[j], gbuf.at[j], g_recv.at[j]).wait()
    total = gbuf[0].astype(F32)
    for j in range(1, 2 * spans):
        total += gbuf[j].astype(F32)
    gsum[...] = total
    final = pltpu.make_async_copy(gsum, grad_out.at[0], go_sem)
    final.start()

    for t in range(2):
        for n in range(CH):
            result_copy(t, n, down_out).wait()

            @pl.when(stage_of(t) < sections - 1)
            def _():
                stream_copy(t, n).wait_send()

        @pl.when(c < spans - 1)
        def _():
            for h in range(HEADS):
                state_copy(t, h).wait_send()

        for k in range(1, copies):
            cot_copy(t, down_ct, k).wait_send()
            for piece in range(PIECES):
                hidden_copy(t, k, piece).wait_send()
        for to in range(spans):
            @pl.when(jnp.logical_not(stays(t, to)))
            def _():
                grad_copy(t, to).wait_send()

    final.wait()


def hand_over(down_in, up_in, grad_in, down_out, up_out, grad_out, acts, grad, in_sems, out_sems):
    rows = TOK // HANDS
    moves = []
    for i, (src, dst) in enumerate(((down_in, down_out), (up_in, up_out))):
        for n in range(HANDS):
            part = (0, 0, pl.ds(n * rows, rows))
            moves.append((src.at[part], acts.at[i, pl.ds(n * rows, rows)], dst.at[part]))
    moves.append((grad_in.at[0], grad, grad_out.at[0]))
    loads, stores = [], []
    for i, (src, here, dst) in enumerate(moves):
        loads.append(pltpu.make_async_copy(src, here, in_sems.at[i]))
        stores.append(pltpu.make_async_copy(here, dst, out_sems.at[i]))
        loads[i].start()
    for load, store in zip(loads, stores):
        load.wait()
        store.start()
    for store in stores:
        store.wait()


def per_device(dims, *arrays):
    sections, spans, copies = dims
    share = WIDTH // (spans * copies)
    hbm = pl.BlockSpec(memory_space=pl.ANY)
    vmem = pl.BlockSpec(memory_space=pltpu.VMEM)
    dma = pltpu.SemaphoreType.DMA
    down_acts, up_acts, grad = pl.pallas_call(
        functools.partial(kernel, dims),
        out_shape=(
            jax.ShapeDtypeStruct((1, 1, TOK, WIDTH), BF),
            jax.ShapeDtypeStruct((1, 1, TOK, WIDTH), BF),
            jax.ShapeDtypeStruct((1, share, WIDTH), F32),
        ),
        in_specs=[hbm] * 4 + [vmem] * 4 + [hbm] * 4,
        out_specs=(hbm, hbm, hbm),
        scratch_shapes=[
            pltpu.VMEM((2, WIDTH, 3 * WIDTH), BF),
            pltpu.VMEM((2, WIDTH, WIDTH), BF),
            pltpu.VMEM((2, DIM, WIDTH), BF),
            pltpu.VMEM((2, CH, TOK, COLS), BF),
            pltpu.VMEM((2, CH, TOK, COLS), BF),
            pltpu.VMEM((TOK, 3 * WIDTH), F32),
            pltpu.VMEM((TOK, WIDTH), BF),
            pltpu.VMEM((9, DIM, DIM), BF),
            pltpu.VMEM((WIDTH, DIM), BF),
            pltpu.VMEM((TOK, DIM), F32),
            pltpu.VMEM((HEADS, TOK, DIM), BF),
            pltpu.VMEM((HEADS, TOK, DIM), F32),
            pltpu.VMEM((HEADS, DIM, DIM), BF),
            pltpu.VMEM((HEADS, DIM, DIM), F32),
            pltpu.VMEM((2, HEADS, DIM, DIM), BF),
            pltpu.VMEM((2, HEADS, DIM, DIM), BF),
            pltpu.VMEM((2, copies, TOK, WIDTH), BF),
            pltpu.VMEM((2, copies, spans * share, TOK), BF),
            pltpu.VMEM((2, copies, spans * share, TOK), BF),
            pltpu.VMEM((2, spans, share, WIDTH), BF),
            pltpu.VMEM((2 * spans, share, WIDTH), BF),
            pltpu.VMEM((share, WIDTH), F32),
            dma((2, CH)),
            dma((2,)),
            dma((2, CH)),
            dma((2, CH)),
            dma((2, CH)),
            dma((2, HEADS)),
            dma((2, HEADS)),
            dma((2, copies)),
            dma((2, copies)),
            dma((2, copies, PIECES)),
            dma((2, copies, PIECES)),
            dma((2 * spans,)),
            dma((2, spans)),
            dma,
        ],
        compiler_params=pltpu.CompilerParams(
            collective_id=0, has_side_effects=True, vmem_limit_bytes=60 * 1024 * 1024
        ),
    )(*arrays[:4], *(jnp.swapaxes(gates, 1, 2) for gates in arrays[4:6]), *arrays[6:])
    return pl.pallas_call(
        hand_over,
        out_shape=tuple(jax.ShapeDtypeStruct(a.shape, a.dtype) for a in (down_acts, up_acts, grad)),
        in_specs=[hbm] * 3,
        out_specs=(hbm, hbm, hbm),
        scratch_shapes=[
            pltpu.VMEM((2, TOK, WIDTH), BF),
            pltpu.VMEM((share, WIDTH), F32),
            dma((2 * HANDS + 1,)),
            dma((2 * HANDS + 1,)),
        ],
    )(down_acts, up_acts, grad)


def solution(mesh):
    dims = (mesh.shape["pipe"], mesh.shape["ctx"], mesh.shape["dp"])
    return jax.shard_map(
        functools.partial(per_device, dims),
        mesh=mesh,
        in_specs=(
            P("dp", "ctx", None),
            P("dp", "ctx", None),
            P("pipe", None, None),
            P("pipe", None, None),
            P("pipe", None, None),
            P("pipe", None, None),
            P("pipe", None),
            P("pipe", None),
            P("pipe", None, None),
            P("pipe", None, None),
            P("pipe", "dp", "ctx", None),
            P("pipe", "dp", "ctx", None),
        ),
        out_specs=(
            P("pipe", "dp", "ctx", None),
            P("pipe", "dp", "ctx", None),
            P("pipe", ("ctx", "dp"), None),
        ),
        check_vma=False,
    )
```

```python
import functools

import jax
import jax.numpy as jnp
from jax import lax
from jax.experimental import pallas as pl
from jax.experimental.pallas import tpu as pltpu
from jax.sharding import PartitionSpec as P

MESH = pl.DeviceIdType.MESH
EPSILON = 1e-06
EXACT = lax.Precision.HIGHEST
BF = jnp.bfloat16
F32 = jnp.float32
HEADS = 8
DIM = 128
TOK = 256
WIDTH = 1024
CH = 4
COLS = WIDTH // CH
UNIT = 32
PIECES = 4
HANDS = 2


def mm(a, b):
    return jnp.dot(a, b, preferred_element_type=F32)


def mm_nt(a, b):
    return lax.dot_general(a, b, (((1,), (1,)), ((), ())), preferred_element_type=F32)


def band_mask(inner, outer):
    row = lax.broadcasted_iota(jnp.int32, (DIM, DIM), 0)
    col = lax.broadcasted_iota(jnp.int32, (DIM, DIM), 1)
    if outer == 1:
        return (row == col).astype(F32)
    if inner == 0:
        return (row >= col).astype(F32)
    same = (row // outer) == (col // outer)
    return (same & ((row // inner) > (col // inner))).astype(F32)


MASKS = ((1, 1), (1, 8), (8, 64), (64, 128), (0, 128))


def eightfold(starts, powers):
    squares = [mm(n, n).astype(BF) for n in powers]
    halves = [t + mm(n, t).astype(BF) for t, n in zip(starts, squares)]
    fourths = [mm(n, n).astype(BF) for n in squares]
    return [t + mm(n, t).astype(BF) for t, n in zip(halves, fourths)]


def block_inverses(parts, masks):
    inner = [a * masks[1] for a in parts]
    results = eightfold([masks[0] - a for a in inner], inner)
    steps = [mm(t, a * masks[2]).astype(BF) for t, a in zip(results, parts)]
    results = [t - mm(n, t).astype(BF) for t, n in zip(results, steps)]
    results = eightfold(results, steps)
    steps = [mm(a * masks[3], t).astype(BF) for t, a in zip(results, parts)]
    return [t - mm(t, y).astype(BF) for t, y in zip(results, steps)]


def decay_of(gap):
    return jnp.exp(jnp.minimum(gap, 0.0)).astype(BF)


def lane_of(compact, lane):
    return jnp.broadcast_to(compact[:, lane : lane + 1], (TOK, DIM))


def head_maps(heads, proj, rstd, power, beta, cum, select, masks, low, eye, put):
    first, second = slice(0, DIM), slice(DIM, TOK)
    lanes = lax.broadcasted_iota(jnp.int32, (TOK, DIM), 1)
    tail = jnp.exp(cum[TOK - 1 : TOK, :] - cum)
    fade = jnp.exp(cum[TOK - 1 : TOK, :])
    rows = jnp.where(lanes < HEADS, beta, cum).T
    brows = rows.astype(BF)
    tail_rows = tail.T

    def square_sums(start):
        raw = proj[:, start : start + WIDTH]
        return mm((raw * raw).astype(BF), select)

    floor = (EPSILON * DIM) * (square_sums(0) + EPSILON * power)
    nk = rstd * lax.rsqrt(square_sums(WIDTH) * (rstd * rstd) + EPSILON)
    rstd_all = jnp.broadcast_to(rstd, (TOK, DIM))
    state = []
    for h in heads:
        lane = HEADS + h
        q = proj[:, h * DIM : (h + 1) * DIM]
        k = proj[:, WIDTH + h * DIM : WIDTH + (h + 1) * DIM] * lane_of(nk, lane)
        v = proj[:, 2 * WIDTH + h * DIM : 2 * WIDTH + (h + 1) * DIM]
        c = lane_of(cum, lane)
        growth = jnp.exp(c)
        qb, kb = q.astype(BF), k.astype(BF)
        rhs = jnp.concatenate([(k * growth).astype(BF), (v * rstd_all).astype(BF)], axis=1)
        weight = (tail_rows[lane : lane + 1, :] * rows[h : h + 1, :]).astype(BF)
        flipped = kb.T * weight
        qg = q * growth
        crow, brow = rows[lane : lane + 1, :], brows[h : h + 1, :]
        d11 = decay_of(c[first] - crow[:, first]) * brow[:, first]
        d21 = decay_of(c[second] - crow[:, first]) * brow[:, first]
        d22 = decay_of(c[second] - crow[:, second]) * brow[:, second]
        g1 = mm_nt(jnp.concatenate([kb, qb], axis=0), kb[first]).astype(BF)
        g2 = mm_nt(jnp.concatenate([kb[second], qb[second]], axis=0), kb[second]).astype(BF)
        a11 = g1[0:128] * d11
        a21 = g1[128:256] * d21
        s11 = g1[256:384] * (d11 * low)
        s21 = g1[384:512] * d21
        a22 = g2[0:128] * d22
        s22 = g2[128:256] * (d22 * low)
        state.append((a11, a22, a21, s11, s21, s22, rhs, flipped, qg))
    inverses = block_inverses([s[0] for s in state] + [s[1] for s in state], masks)
    n = len(state)
    x1 = [mm(inverses[i], state[i][6][first]).astype(BF) for i in range(n)]
    r2 = [state[i][6][second] - mm(state[i][2], x1[i]).astype(BF) for i in range(n)]
    x2 = [mm(inverses[n + i], r2[i]).astype(BF) for i in range(n)]
    for i, h in enumerate(heads):
        _, _, _, s11, s21, s22, _, flipped, qg = state[i]
        x = jnp.concatenate([x1[i], x2[i]], axis=0)
        z1 = mm(s11, x1[i])
        z2 = mm(jnp.concatenate([s21, s22], axis=1), x)
        kx = mm(flipped, x)
        put(h, qg, z1, z2, kx, eye * fade[:, HEADS + h : HEADS + h + 1])
    return floor


def kernel(
    dims,
    down_in, up_in, down_qkv, up_qkv, down_gates, up_gates, down_rates, up_rates,
    down_wo, up_wo, down_ct, up_ct,
    down_out, up_out, grad_out,
    wqkv, wo, wg, xbuf, ybuf, proj, hid, obuf, maskb, select, floor, pmap, rmap, mmap, bmap, bsend, sin, sout,
    cot, ht, hg, part, gbuf, gsum,
    w_sem, wo_sem, x_recv, x_send, y_sem, s_recv, s_send, ct_recv, ct_send,
    ct_own, h_recv, h_send, g_recv, g_send, go_sem,
):
    sections, spans, copies = dims
    p, c, d = lax.axis_index("pipe"), lax.axis_index("ctx"), lax.axis_index("dp")
    low_half = p < sections // 2
    share = WIDTH // (spans * copies)
    column = WIDTH // spans

    def is_down(t):
        return low_half == (t == 0)

    def at(pipe, ctx, dp):
        return (pipe, ctx, dp)

    def remote(src, dst, send, recv, where):
        return pltpu.make_async_remote_copy(
            src_ref=src, dst_ref=dst, send_sem=send, recv_sem=recv,
            device_id=where, device_id_type=MESH,
        )

    def weight_copy(t, n, qkv):
        rows = pl.ds(n * COLS, COLS)
        return pltpu.make_async_copy(qkv.at[0, rows], wqkv.at[t, rows], w_sem.at[t, n])

    def out_copy(t, out):
        return pltpu.make_async_copy(out.at[0], wo.at[t], wo_sem.at[t])

    def start_weights(t, qkv, out):
        for n in range(CH):
            weight_copy(t, n, qkv).start()
        out_copy(t, out).start()

    def input_copy(src, n):
        return pltpu.make_async_copy(
            src.at[0, :, pl.ds(n * COLS, COLS)], xbuf.at[0, n], x_recv.at[0, n]
        )

    @pl.when(p == 0)
    def _():
        for n in range(CH):
            input_copy(down_in, n).start()

    @pl.when(p == sections - 1)
    def _():
        for n in range(CH):
            input_copy(up_in, n).start()

    def load(t):
        @pl.when(is_down(t))
        def _():
            start_weights(t, down_qkv, down_wo)

        @pl.when(jnp.logical_not(is_down(t)))
        def _():
            start_weights(t, up_qkv, up_wo)

    load(0)

    barrier = pltpu.get_barrier_semaphore()
    mirror = sections - 1 - p
    pair = p + 1 - 2 * lax.rem(p, 2)
    peers = [at(pair, c, d), at(mirror, c, d)]
    for k in range(1, spans):
        other = lax.rem(c + k, spans)
        peers += [at(p, other, d), at(mirror, other, d)]
    for k in range(1, copies):
        peers.append(at(p, c, lax.rem(d + k, copies)))
    for peer in peers:
        pl.semaphore_signal(barrier, inc=1, device_id=peer, device_id_type=MESH)

    for level, (inner, outer_size) in enumerate(MASKS):
        maskb[level] = band_mask(inner, outer_size).astype(BF)
    for h in range(HEADS):
        lanes = lax.broadcasted_iota(jnp.int32, (DIM, DIM), 1)
        select[h * DIM : (h + 1) * DIM] = (lanes == HEADS + h).astype(F32).astype(BF)
    for t in range(2):
        wg[t, 2 * HEADS :, :] = jnp.zeros((DIM - 2 * HEADS, WIDTH), BF)
        wg[t, 0 : 2 * HEADS, :] = jnp.where(is_down(t), down_gates[0], up_gates[0])

    half = TOK // 2
    before, after = lax.rem(d + copies - 1, copies), lax.rem(d + 1, copies)
    ways = ((0, after),) if copies == 2 else ((0, after), (1, before))

    def cot_own(t, source):
        return pltpu.make_async_copy(source.at[0, 0], cot.at[t, d], ct_own.at[t])

    def cot_copy(t, source, way, to):
        return remote(
            source.at[0, 0], cot.at[t, d], ct_send.at[t, way], ct_recv.at[t, way], at(p, c, to)
        )

    def cot_relay(t, way, to):
        owner = before if way == 0 else after
        part_rows = pl.ds(way * half, half)
        return remote(
            cot.at[t, owner, part_rows], cot.at[t, owner, part_rows], ct_send.at[t, 2 + way],
            ct_recv.at[t, 2 + way], at(p, c, to),
        )

    def start_cot(t, source):
        cot_own(t, source).start()
        for way, to in ways:
            cot_copy(t, source, way, to).start()

    def relay_cots(t):
        for way, to in ways:
            cot_copy(t, down_ct, way, to).wait_recv()
        if copies == 4:
            for way, to in ways:
                cot_relay(t, way, to).start()

    def wait_cots(t):
        cot_own(t, down_ct).wait()
        if copies == 4:
            for way, to in ways:
                cot_relay(t, way, to).wait_recv()

    def start_cots(t):
        @pl.when(is_down(t))
        def _():
            start_cot(t, down_ct)

        @pl.when(jnp.logical_not(is_down(t)))
        def _():
            start_cot(t, up_ct)

    def meet():
        pl.semaphore_wait(barrier, len(peers))
        start_cots(0)

        @pl.when(jnp.logical_not(outer))
        def _():
            start_cots(1)

    outer = (p == 0) | (p == sections - 1)

    @pl.when(jnp.logical_not(outer))
    def _():
        meet()

    def state_copy(t, h):
        return remote(
            sout.at[t, h], sin.at[t, h], s_send.at[t, h], s_recv.at[t, h],
            at(p, lax.rem(c + 1, spans), d),
        )

    def first_copy(t, h):
        return remote(
            bsend.at[t, h], sin.at[t, h], s_send.at[t, h], s_recv.at[t, h],
            at(p, lax.rem(c + 1, spans), d),
        )

    def stage_of(t):
        early = jnp.where(low_half, p, sections - 1 - p)
        return jnp.where(t == 0, early, sections - 1 - early)

    def stream_copy(t, n):
        slot = jnp.where(stage_of(t) == 0, 0, 1)
        to = jnp.clip(jnp.where(is_down(t), p + 1, p - 1), 0, sections - 1)
        return remote(
            ybuf.at[t, n], xbuf.at[slot, n], x_send.at[t, n], x_recv.at[slot, n], at(to, c, d)
        )

    def result_copy(t, n, out):
        return pltpu.make_async_copy(
            ybuf.at[t, n], out.at[0, 0, :, pl.ds(n * COLS, COLS)], y_sem.at[t, n]
        )

    def hidden_own(t, piece):
        rows = pl.ds(piece * (spans * share // PIECES), spans * share // PIECES)
        return pltpu.make_async_copy(
            ht.at[t, d, rows], hg.at[t, d, rows], h_recv.at[t, d, piece]
        )

    def hidden_copy(t, k, piece):
        to = lax.rem(d + k, copies)
        rows = pl.ds(piece * (spans * share // PIECES), spans * share // PIECES)
        return remote(
            ht.at[t, to, rows], hg.at[t, d, rows], h_send.at[t, k - 1, piece],
            h_recv.at[t, d, piece], at(p, c, to),
        )

    def grad_own(t, to):
        return pltpu.make_async_copy(part.at[t, to], gbuf.at[to], g_recv.at[to])

    def grad_copy(t, to):
        slot = c + jnp.where(is_down(t), 0, spans)
        pipe = jnp.where(is_down(t), p, mirror)
        return remote(
            part.at[t, to], gbuf.at[slot], g_send.at[t, to], g_recv.at[slot], at(pipe, to, d)
        )

    def stays(t, to):
        return (c == to) & is_down(t)

    def rates_of(t):
        rates = jnp.where(is_down(t), down_rates[...], up_rates[...])
        return jnp.concatenate(
            [jnp.zeros((1, HEADS), F32), rates, jnp.zeros((1, DIM - 2 * HEADS), F32)], axis=1
        )

    def gate_values(logits, rates):
        beta = jax.nn.sigmoid(logits)
        log_decay = -rates * (jnp.maximum(logits, 0.0) + jnp.log1p(jnp.exp(-jnp.abs(logits))))
        row = lax.broadcasted_iota(jnp.int32, (TOK, TOK), 0)
        col = lax.broadcasted_iota(jnp.int32, (TOK, TOK), 1)
        cum = jnp.dot(
            (row >= col).astype(F32), log_decay, preferred_element_type=F32, precision=EXACT
        )
        return beta, cum

    def section(t):
        square = jnp.zeros((TOK, 1), F32)
        logits = jnp.zeros((TOK, DIM), F32)
        for n in range(CH):
            pltpu.make_async_copy(xbuf.at[t, n], xbuf.at[t, n], x_recv.at[t, n]).wait()
            weight_copy(t, n, down_qkv).wait()
            x = xbuf[t, n]
            xf = x.astype(F32)
            square += jnp.sum(xf * xf, axis=-1, keepdims=True)
            logits += mm_nt(x, wg[t, :, n * COLS : (n + 1) * COLS])
            if n == CH - 1:
                power = square * (1.0 / WIDTH) + EPSILON
                rstd = lax.rsqrt(power)
                beta, cum = gate_values(logits * rstd, rates_of(t))
            for j in range(6):
                block = slice(512 * j, 512 * (j + 1))
                product = mm(x, wqkv[t, n * COLS : (n + 1) * COLS, block])
                if n == 0:
                    proj[:, block] = product
                else:
                    proj[:, block] += product

        @pl.when(t == 0)
        def _():
            load(1)

        masks = [maskb[level] for level in range(4)]
        low = maskb[4]
        eye = maskb[0].astype(F32)

        def put(h, qg, z1, z2, kx, fade):
            pmap[h, 0:DIM] = (qg[0:DIM] - z1[:, 0:DIM]).astype(BF)
            pmap[h, DIM:TOK] = (qg[DIM:TOK] - z2[:, 0:DIM]).astype(BF)
            rmap[h, 0:DIM] = z1[:, DIM:TOK]
            rmap[h, DIM:TOK] = z2[:, DIM:TOK]
            mmap[h] = (fade - kx[:, 0:DIM]).astype(BF)
            bmap[h] = kx[:, DIM:TOK]
            bsend[t, h] = kx[:, DIM:TOK].astype(BF)

        floor[...] = head_maps(
            range(HEADS), proj, rstd, power, beta, cum, select[...], masks, low, eye, put
        )

        @pl.when((t == 0) & outer)
        def _():
            meet()

        @pl.when(c == 0)
        def _():
            for h in range(HEADS):
                first_copy(t, h).start()
                sin[t, h] = jnp.zeros((DIM, DIM), BF)

        def finish_head(h):
            o = obuf[h % 2]
            level = jnp.mean(o * o, axis=-1, keepdims=True)
            o = o * lax.rsqrt(level + floor[:, HEADS + h : HEADS + h + 1])
            o = o.astype(BF)
            hid[:, h * DIM : (h + 1) * DIM] = o
            flipped = o.T
            for u in range(DIM // UNIT):
                row0 = h * DIM + u * UNIT
                span, rest = row0 // column, row0 % column
                to, i = rest // share, rest % share
                ht[t, to, span * share + i : span * share + i + UNIT] = flipped[
                    u * UNIT : (u + 1) * UNIT
                ]

        def send_pieces(h):
            for piece in range(PIECES):
                last = HEADS // PIECES * (piece + 1) - 1 if spans == HEADS else HEADS - 1
                if last == h:
                    hidden_own(t, piece).start()
                    for k in range(1, copies):
                        hidden_copy(t, k, piece).start()

        for h in range(HEADS):
            @pl.when(c > 0)
            def _():
                state_copy(t, h).wait_recv()

            s = sin[t, h]
            sout[t, h] = (mm(mmap[h], s) + bmap[h]).astype(BF)
            obuf[h % 2] = mm(pmap[h], s) + rmap[h]
            if h > 0:
                finish_head(h - 1)

            @pl.when((c > 0) & (c < spans - 1))
            def _():
                state_copy(t, h).start()

            if h > 0:
                send_pieces(h - 1)
        finish_head(HEADS - 1)
        send_pieces(HEADS - 1)

        out_copy(t, down_wo).wait()
        for n in range(CH):
            block = slice(n * COLS, (n + 1) * COLS)
            y = xbuf[t, n].astype(F32) + mm(hid[...], wo[t, :, block])
            ybuf[t, n] = y.astype(BF)

            @pl.when(stage_of(t) < sections - 1)
            def _():
                stream_copy(t, n).start()

            @pl.when(is_down(t))
            def _():
                result_copy(t, n, down_out).start()

            @pl.when(jnp.logical_not(is_down(t)))
            def _():
                result_copy(t, n, up_out).start()

        @pl.when(t == 0)
        def _():
            relay_cots(0)

            @pl.when(outer)
            def _():
                start_cots(1)

            @pl.when(jnp.logical_not(outer))
            def _():
                relay_cots(1)

    def gradient(t):
        wait_cots(t)
        size = spans * share // PIECES
        for piece in range(PIECES):
            rows = pl.ds(piece * size, size)
            for j in range(copies):
                pltpu.make_async_copy(
                    hg.at[t, j, rows], hg.at[t, j, rows], h_recv.at[t, j, piece]
                ).wait()
            total = mm(hg[t, 0, piece * size : (piece + 1) * size], cot[t, 0])
            for j in range(1, copies):
                total += mm(hg[t, j, piece * size : (piece + 1) * size], cot[t, j])
            total = total.astype(BF)
            for row0 in range(0, size, UNIT):
                to, at_row = divmod(piece * size + row0, share)
                part[t, to, at_row : at_row + UNIT] = total[row0 : row0 + UNIT]
                if at_row + UNIT == share:
                    @pl.when(stays(t, to))
                    def _():
                        grad_own(t, to).start()

                    @pl.when(jnp.logical_not(stays(t, to)))
                    def _():
                        grad_copy(t, to).start()

    def turn(i, carry):
        middle = jnp.where(outer, 2, 1)
        is_section = (i == 0) | (i == middle)

        @pl.when(is_section)
        def _():
            section(jnp.where(i == 0, 0, 1))

        @pl.when(jnp.logical_not(is_section))
        def _():
            gradient(jnp.where(i == 3, 1, 0))

            @pl.when(outer & (i == 1))
            def _():
                relay_cots(1)

        return carry

    lax.fori_loop(0, 4, turn, 0)

    for j in range(2 * spans):
        pltpu.make_async_copy(gbuf.at[j], gbuf.at[j], g_recv.at[j]).wait()
    total = gbuf[0].astype(F32)
    for j in range(1, 2 * spans):
        total += gbuf[j].astype(F32)
    gsum[...] = total
    final = pltpu.make_async_copy(gsum, grad_out.at[0], go_sem)
    final.start()

    for t in range(2):
        for n in range(CH):
            result_copy(t, n, down_out).wait()

            @pl.when(stage_of(t) < sections - 1)
            def _():
                stream_copy(t, n).wait_send()

        @pl.when(c < spans - 1)
        def _():
            for h in range(HEADS):
                state_copy(t, h).wait_send()

        for way, to in ways:
            cot_copy(t, down_ct, way, to).wait_send()
            if copies == 4:
                cot_relay(t, way, to).wait_send()
        for k in range(1, copies):
            for piece in range(PIECES):
                hidden_copy(t, k, piece).wait_send()
        for to in range(spans):
            @pl.when(jnp.logical_not(stays(t, to)))
            def _():
                grad_copy(t, to).wait_send()

    final.wait()


def hand_over(down_in, up_in, grad_in, down_out, up_out, grad_out, acts, grad, in_sems, out_sems):
    rows = TOK // HANDS
    moves = []
    for i, (src, dst) in enumerate(((down_in, down_out), (up_in, up_out))):
        for n in range(HANDS):
            part = (0, 0, pl.ds(n * rows, rows))
            moves.append((src.at[part], acts.at[i, pl.ds(n * rows, rows)], dst.at[part]))
    moves.append((grad_in.at[0], grad, grad_out.at[0]))
    loads, stores = [], []
    for i, (src, here, dst) in enumerate(moves):
        loads.append(pltpu.make_async_copy(src, here, in_sems.at[i]))
        stores.append(pltpu.make_async_copy(here, dst, out_sems.at[i]))
        loads[i].start()
    for load, store in zip(loads, stores):
        load.wait()
        store.start()
    for store in stores:
        store.wait()


def per_device(dims, *arrays):
    sections, spans, copies = dims
    share = WIDTH // (spans * copies)
    hbm = pl.BlockSpec(memory_space=pl.ANY)
    vmem = pl.BlockSpec(memory_space=pltpu.VMEM)
    dma = pltpu.SemaphoreType.DMA
    down_acts, up_acts, grad = pl.pallas_call(
        functools.partial(kernel, dims),
        out_shape=(
            jax.ShapeDtypeStruct((1, 1, TOK, WIDTH), BF),
            jax.ShapeDtypeStruct((1, 1, TOK, WIDTH), BF),
            jax.ShapeDtypeStruct((1, share, WIDTH), F32),
        ),
        in_specs=[hbm] * 4 + [vmem] * 4 + [hbm] * 4,
        out_specs=(hbm, hbm, hbm),
        scratch_shapes=[
            pltpu.VMEM((2, WIDTH, 3 * WIDTH), BF),
            pltpu.VMEM((2, WIDTH, WIDTH), BF),
            pltpu.VMEM((2, DIM, WIDTH), BF),
            pltpu.VMEM((2, CH, TOK, COLS), BF),
            pltpu.VMEM((2, CH, TOK, COLS), BF),
            pltpu.VMEM((TOK, 3 * WIDTH), F32),
            pltpu.VMEM((TOK, WIDTH), BF),
            pltpu.VMEM((2, TOK, DIM), F32),
            pltpu.VMEM((len(MASKS), DIM, DIM), BF),
            pltpu.VMEM((WIDTH, DIM), BF),
            pltpu.VMEM((TOK, DIM), F32),
            pltpu.VMEM((HEADS, TOK, DIM), BF),
            pltpu.VMEM((HEADS, TOK, DIM), F32),
            pltpu.VMEM((HEADS, DIM, DIM), BF),
            pltpu.VMEM((HEADS, DIM, DIM), F32),
            pltpu.VMEM((2, HEADS, DIM, DIM), BF),
            pltpu.VMEM((2, HEADS, DIM, DIM), BF),
            pltpu.VMEM((2, HEADS, DIM, DIM), BF),
            pltpu.VMEM((2, copies, TOK, WIDTH), BF),
            pltpu.VMEM((2, copies, spans * share, TOK), BF),
            pltpu.VMEM((2, copies, spans * share, TOK), BF),
            pltpu.VMEM((2, spans, share, WIDTH), BF),
            pltpu.VMEM((2 * spans, share, WIDTH), BF),
            pltpu.VMEM((share, WIDTH), F32),
            dma((2, CH)),
            dma((2,)),
            dma((2, CH)),
            dma((2, CH)),
            dma((2, CH)),
            dma((2, HEADS)),
            dma((2, HEADS)),
            dma((2, 4)),
            dma((2, 4)),
            dma((2,)),
            dma((2, copies, PIECES)),
            dma((2, copies, PIECES)),
            dma((2 * spans,)),
            dma((2, spans)),
            dma,
        ],
        compiler_params=pltpu.CompilerParams(
            collective_id=0, has_side_effects=True, vmem_limit_bytes=60 * 1024 * 1024
        ),
    )(*arrays[:4], *(jnp.swapaxes(gates, 1, 2) for gates in arrays[4:6]), *arrays[6:])
    return pl.pallas_call(
        hand_over,
        out_shape=tuple(jax.ShapeDtypeStruct(a.shape, a.dtype) for a in (down_acts, up_acts, grad)),
        in_specs=[hbm] * 3,
        out_specs=(hbm, hbm, hbm),
        scratch_shapes=[
            pltpu.VMEM((2, TOK, WIDTH), BF),
            pltpu.VMEM((share, WIDTH), F32),
            dma((2 * HANDS + 1,)),
            dma((2 * HANDS + 1,)),
        ],
    )(down_acts, up_acts, grad)


def solution(mesh):
    dims = (mesh.shape["pipe"], mesh.shape["ctx"], mesh.shape["dp"])
    return jax.shard_map(
        functools.partial(per_device, dims),
        mesh=mesh,
        in_specs=(
            P("dp", "ctx", None),
            P("dp", "ctx", None),
            P("pipe", None, None),
            P("pipe", None, None),
            P("pipe", None, None),
            P("pipe", None, None),
            P("pipe", None),
            P("pipe", None),
            P("pipe", None, None),
            P("pipe", None, None),
            P("pipe", "dp", "ctx", None),
            P("pipe", "dp", "ctx", None),
        ),
        out_specs=(
            P("pipe", "dp", "ctx", None),
            P("pipe", "dp", "ctx", None),
            P("pipe", ("ctx", "dp"), None),
        ),
        check_vma=False,
    )
```

```python
import functools

import jax
import jax.numpy as jnp
from jax import lax
from jax.experimental import pallas as pl
from jax.experimental.pallas import tpu as pltpu
from jax.sharding import PartitionSpec as P

MESH = pl.DeviceIdType.MESH
EPSILON = 1e-06
EXACT = lax.Precision.HIGHEST
BF = jnp.bfloat16
F32 = jnp.float32
HEADS = 8
DIM = 128
TOK = 256
WIDTH = 1024
CH = 4
COLS = WIDTH // CH
UNIT = 32
PIECES = 4
HANDS = 2


def mm(a, b):
    return jnp.dot(a, b, preferred_element_type=F32)


def mm_nt(a, b):
    return lax.dot_general(a, b, (((1,), (1,)), ((), ())), preferred_element_type=F32)


def band_mask(inner, outer):
    row = lax.broadcasted_iota(jnp.int32, (DIM, DIM), 0)
    col = lax.broadcasted_iota(jnp.int32, (DIM, DIM), 1)
    if outer == 1:
        return (row == col).astype(F32)
    if inner == 0:
        return (row >= col).astype(F32)
    same = (row // outer) == (col // outer)
    return (same & ((row // inner) > (col // inner))).astype(F32)


MASKS = ((1, 1), (1, 8), (8, 64), (64, 128), (0, 128))


def eightfold(starts, powers):
    squares = [mm(n, n).astype(BF) for n in powers]
    halves = [t + mm(n, t).astype(BF) for t, n in zip(starts, squares)]
    fourths = [mm(n, n).astype(BF) for n in squares]
    return [t + mm(n, t).astype(BF) for t, n in zip(halves, fourths)]


def block_inverses(parts, masks):
    inner = [a * masks[1] for a in parts]
    results = eightfold([masks[0] - a for a in inner], inner)
    steps = [mm(t, a * masks[2]).astype(BF) for t, a in zip(results, parts)]
    results = [t - mm(n, t).astype(BF) for t, n in zip(results, steps)]
    results = eightfold(results, steps)
    steps = [mm(a * masks[3], t).astype(BF) for t, a in zip(results, parts)]
    results = [t - mm(t, y).astype(BF) for t, y in zip(results, steps)]
    return results


def decay_of(gap):
    return jnp.exp(jnp.minimum(gap, 0.0)).astype(BF)


def lane_of(compact, lane):
    return jnp.broadcast_to(compact[:, lane : lane + 1], (TOK, DIM))


def gate_rows(logits, rates, triangle):
    row = lax.broadcasted_iota(jnp.int32, (2 * HEADS, TOK), 0)
    decay = -rates * (jnp.maximum(logits, 0.0) + jnp.log1p(jnp.exp(-jnp.abs(logits))))
    high = decay.astype(BF)
    rest = decay - high.astype(F32)
    middle = rest.astype(BF)
    low = (rest - middle.astype(F32)).astype(BF)
    sums = mm(jnp.concatenate([high, middle, low], axis=0), triangle)
    total = sums[0:16] + sums[16:32] + sums[32:48]
    return jnp.where(row < HEADS, jax.nn.sigmoid(logits), total)


def head_maps(proj, power, gates, select, masks, low, eye, put):
    first, second = slice(0, DIM), slice(DIM, TOK)
    rstd = lax.rsqrt(power)
    columns = jnp.concatenate([gates, jnp.zeros((DIM - 2 * HEADS, TOK), F32)], axis=0).T
    beta, cum = gates[0:HEADS], gates[HEADS : 2 * HEADS]
    last = jnp.broadcast_to(cum[:, TOK - 1 : TOK], (HEADS, TOK))
    weights = (beta * jnp.exp(last - cum)).astype(BF)
    fades = jnp.exp(last[:, 0:DIM])
    strengths = beta.astype(BF)

    def square_sums(start):
        raw = proj[:, start : start + WIDTH]
        return mm((raw * raw).astype(BF), select)

    nk = rstd * lax.rsqrt(square_sums(WIDTH) * (rstd * rstd) + EPSILON)

    def prepare(h):
        lane = HEADS + h
        q = proj[:, h * DIM : (h + 1) * DIM]
        k = proj[:, WIDTH + h * DIM : WIDTH + (h + 1) * DIM] * lane_of(nk, lane)
        v = proj[:, 2 * WIDTH + h * DIM : 2 * WIDTH + (h + 1) * DIM]
        c = lane_of(columns, lane)
        growth = jnp.exp(c)
        qb, kb = q.astype(BF), k.astype(BF)
        rhs = jnp.concatenate([(k * growth).astype(BF), (v * rstd).astype(BF)], axis=1)
        flipped = kb.T * weights[h : h + 1, :]
        qg = q * growth
        crow, brow = cum[h : h + 1, :], strengths[h : h + 1, :]
        d11 = decay_of(c[first] - crow[:, first]) * brow[:, first]
        d21 = decay_of(c[second] - crow[:, first]) * brow[:, first]
        d22 = decay_of(c[second] - crow[:, second]) * brow[:, second]
        g1 = mm_nt(jnp.concatenate([kb, qb], axis=0), kb[first]).astype(BF)
        g2 = mm_nt(jnp.concatenate([kb[second], qb[second]], axis=0), kb[second]).astype(BF)
        a11 = g1[0:128] * d11
        a21 = g1[128:256] * d21
        s11 = g1[256:384] * (d11 * low)
        s21 = g1[384:512] * d21
        a22 = g2[0:128] * d22
        s22 = g2[128:256] * (d22 * low)
        return h, a11, a22, a21, s11, s21, s22, rhs, flipped, qg

    def complete(state, inverses):
        n = len(state)
        x1 = [mm(inverses[i], state[i][7][first]).astype(BF) for i in range(n)]
        r2 = [state[i][7][second] - mm(state[i][3], x1[i]).astype(BF) for i in range(n)]
        x2 = [mm(inverses[n + i], r2[i]).astype(BF) for i in range(n)]
        for i in range(n):
            h, _, _, _, s11, s21, s22, _, flipped, qg = state[i]
            x = jnp.concatenate([x1[i], x2[i]], axis=0)
            z1 = mm(s11, x1[i])
            z2 = mm(jnp.concatenate([s21, s22], axis=1), x)
            kx = mm(flipped, x)
            put(h, qg, z1, z2, kx, eye * fades[h : h + 1, :])

    state = [prepare(h) for h in range(HEADS)]
    inverses = block_inverses([s[1] for s in state] + [s[2] for s in state], masks)
    complete(state, inverses)
    return (EPSILON * DIM) * (square_sums(0) + EPSILON * power)


def kernel(
    dims,
    down_in, up_in, down_qkv, up_qkv, down_gates, up_gates, down_rates, up_rates,
    down_wo, up_wo, down_ct, up_ct,
    down_out, up_out, grad_out,
    wqkv, wo, wg, rates, triangle, xbuf, ybuf, proj, hid, obuf, maskb, select, floor, pmap, rmap, mmap, bmap, bsend, sin, sout,
    cot, ht, hg, part, gbuf, gsum,
    w_sem, wo_sem, x_recv, x_send, y_sem, s_recv, s_send, ct_recv, ct_send,
    ct_own, h_recv, h_send, g_recv, g_send, go_sem,
):
    sections, spans, copies = dims
    p, c, d = lax.axis_index("pipe"), lax.axis_index("ctx"), lax.axis_index("dp")
    low_half = p < sections // 2
    share = WIDTH // (spans * copies)
    column = WIDTH // spans

    def is_down(t):
        return low_half == (t == 0)

    def at(pipe, ctx, dp):
        return (pipe, ctx, dp)

    def remote(src, dst, send, recv, where):
        return pltpu.make_async_remote_copy(
            src_ref=src, dst_ref=dst, send_sem=send, recv_sem=recv,
            device_id=where, device_id_type=MESH,
        )

    def weight_copy(t, n, qkv):
        rows = pl.ds(n * COLS, COLS)
        return pltpu.make_async_copy(qkv.at[0, rows], wqkv.at[t, rows], w_sem.at[t, n])

    def out_copy(t, out):
        return pltpu.make_async_copy(out.at[0], wo.at[t], wo_sem.at[t])

    def start_weights(t, qkv, out):
        for n in range(CH):
            weight_copy(t, n, qkv).start()
        out_copy(t, out).start()

    def input_copy(src, n):
        return pltpu.make_async_copy(
            src.at[0, :, pl.ds(n * COLS, COLS)], xbuf.at[0, n], x_recv.at[0, n]
        )

    @pl.when(p == 0)
    def _():
        for n in range(CH):
            input_copy(down_in, n).start()

    @pl.when(p == sections - 1)
    def _():
        for n in range(CH):
            input_copy(up_in, n).start()

    def load(t):
        @pl.when(is_down(t))
        def _():
            start_weights(t, down_qkv, down_wo)

        @pl.when(jnp.logical_not(is_down(t)))
        def _():
            start_weights(t, up_qkv, up_wo)

    load(0)

    barrier = pltpu.get_barrier_semaphore()
    mirror = sections - 1 - p
    pair = p + 1 - 2 * lax.rem(p, 2)
    peers = [at(pair, c, d), at(mirror, c, d)]
    for k in range(1, spans):
        other = lax.rem(c + k, spans)
        peers += [at(p, other, d), at(mirror, other, d)]
    for k in range(1, copies):
        peers.append(at(p, c, lax.rem(d + k, copies)))
    for peer in peers:
        pl.semaphore_signal(barrier, inc=1, device_id=peer, device_id_type=MESH)

    for level, (inner, outer_size) in enumerate(MASKS):
        maskb[level] = band_mask(inner, outer_size).astype(BF)
    for h in range(HEADS):
        lanes = lax.broadcasted_iota(jnp.int32, (DIM, DIM), 1)
        select[h * DIM : (h + 1) * DIM] = (lanes == HEADS + h).astype(F32).astype(BF)
    for t in range(2):
        wg[t] = jnp.where(is_down(t), down_gates[0], up_gates[0])
        rate = jnp.where(is_down(t), down_rates[...], up_rates[...])
        rate = jnp.concatenate(
            [jnp.zeros((1, HEADS), F32), rate, jnp.zeros((1, DIM - 2 * HEADS), F32)], axis=1
        )
        rate = jnp.broadcast_to(rate, (TOK, DIM)).T
        rates[t] = rate[0 : 2 * HEADS]
    token = lax.broadcasted_iota(jnp.int32, (TOK, TOK), 0)
    until = lax.broadcasted_iota(jnp.int32, (TOK, TOK), 1)
    triangle[...] = (token <= until).astype(F32).astype(BF)

    half = TOK // 2
    before, after = lax.rem(d + copies - 1, copies), lax.rem(d + 1, copies)
    ways = ((0, after),) if copies == 2 else ((0, after), (1, before))

    def cot_own(t, source):
        return pltpu.make_async_copy(source.at[0, 0], cot.at[t, d], ct_own.at[t])

    def cot_copy(t, source, way, to):
        return remote(
            source.at[0, 0], cot.at[t, d], ct_send.at[t, way], ct_recv.at[t, way], at(p, c, to)
        )

    def cot_relay(t, way, to):
        owner = before if way == 0 else after
        part_rows = pl.ds(way * half, half)
        return remote(
            cot.at[t, owner, part_rows], cot.at[t, owner, part_rows], ct_send.at[t, 2 + way],
            ct_recv.at[t, 2 + way], at(p, c, to),
        )

    def start_cot(t, source):
        cot_own(t, source).start()
        for way, to in ways:
            cot_copy(t, source, way, to).start()

    def relay_cots(t):
        for way, to in ways:
            cot_copy(t, down_ct, way, to).wait_recv()
        if copies == 4:
            for way, to in ways:
                cot_relay(t, way, to).start()

    def wait_cots(t):
        cot_own(t, down_ct).wait()
        if copies == 4:
            for way, to in ways:
                cot_relay(t, way, to).wait_recv()

    def start_cots(t):
        @pl.when(is_down(t))
        def _():
            start_cot(t, down_ct)

        @pl.when(jnp.logical_not(is_down(t)))
        def _():
            start_cot(t, up_ct)

    def meet():
        pl.semaphore_wait(barrier, len(peers))
        start_cots(0)

        @pl.when(jnp.logical_not(outer))
        def _():
            start_cots(1)

    outer = (p == 0) | (p == sections - 1)

    @pl.when(jnp.logical_not(outer))
    def _():
        meet()

    def state_copy(t, h):
        return remote(
            sout.at[t, h], sin.at[t, h], s_send.at[t, h], s_recv.at[t, h],
            at(p, lax.rem(c + 1, spans), d),
        )

    def first_copy(t, h):
        return remote(
            bsend.at[t, h], sin.at[t, h], s_send.at[t, h], s_recv.at[t, h],
            at(p, lax.rem(c + 1, spans), d),
        )

    def stage_of(t):
        early = jnp.where(low_half, p, sections - 1 - p)
        return jnp.where(t == 0, early, sections - 1 - early)

    def stream_copy(t, n):
        slot = jnp.where(stage_of(t) == 0, 0, 1)
        to = jnp.clip(jnp.where(is_down(t), p + 1, p - 1), 0, sections - 1)
        return remote(
            ybuf.at[t, n], xbuf.at[slot, n], x_send.at[t, n], x_recv.at[slot, n], at(to, c, d)
        )

    def result_copy(t, n, out):
        return pltpu.make_async_copy(
            ybuf.at[t, n], out.at[0, 0, :, pl.ds(n * COLS, COLS)], y_sem.at[t, n]
        )

    def hidden_own(t, piece):
        rows = pl.ds(piece * (spans * share // PIECES), spans * share // PIECES)
        return pltpu.make_async_copy(
            ht.at[t, d, rows], hg.at[t, d, rows], h_recv.at[t, d, piece]
        )

    def hidden_copy(t, k, piece):
        to = lax.rem(d + k, copies)
        rows = pl.ds(piece * (spans * share // PIECES), spans * share // PIECES)
        return remote(
            ht.at[t, to, rows], hg.at[t, d, rows], h_send.at[t, k - 1, piece],
            h_recv.at[t, d, piece], at(p, c, to),
        )

    def grad_own(t, to):
        return pltpu.make_async_copy(part.at[t, to], gbuf.at[to], g_recv.at[to])

    def grad_copy(t, to):
        slot = c + jnp.where(is_down(t), 0, spans)
        pipe = jnp.where(is_down(t), p, mirror)
        return remote(
            part.at[t, to], gbuf.at[slot], g_send.at[t, to], g_recv.at[slot], at(pipe, to, d)
        )

    def stays(t, to):
        return (c == to) & is_down(t)

    def section(t):
        ones = jnp.ones((COLS, DIM), BF)
        square = jnp.zeros((TOK, DIM), F32)
        square_row = jnp.zeros((2 * HEADS, TOK), F32)
        logits = jnp.zeros((2 * HEADS, TOK), F32)
        for n in range(CH):
            pltpu.make_async_copy(xbuf.at[t, n], xbuf.at[t, n], x_recv.at[t, n]).wait()
            weight_copy(t, n, down_qkv).wait()
            x = xbuf[t, n]
            xf = x.astype(F32)
            x2 = (xf * xf).astype(BF)
            square += mm(x2, ones)
            square_row += mm_nt(ones[0 : 2 * HEADS, 0:DIM], x2[:, 0:DIM])
            square_row += mm_nt(ones[0 : 2 * HEADS, 0:DIM], x2[:, DIM:COLS])
            logits += mm_nt(wg[t, :, n * COLS : (n + 1) * COLS], x)
            for j in range(6):
                block = slice(512 * j, 512 * (j + 1))
                product = mm(x, wqkv[t, n * COLS : (n + 1) * COLS, block])
                if n == 0:
                    proj[:, block] = product
                else:
                    proj[:, block] += product

        power = square * (1.0 / WIDTH) + EPSILON
        scale = lax.rsqrt(square_row * (1.0 / WIDTH) + EPSILON)
        gates = gate_rows(logits * scale, rates[t], triangle[...])


        masks = [maskb[level] for level in range(4)]
        low = maskb[4]
        eye = maskb[0].astype(F32)

        def put(h, qg, z1, z2, kx, fade):
            pmap[h, 0:DIM] = (qg[0:DIM] - z1[:, 0:DIM]).astype(BF)
            pmap[h, DIM:TOK] = (qg[DIM:TOK] - z2[:, 0:DIM]).astype(BF)
            rmap[h, 0:DIM] = z1[:, DIM:TOK]
            rmap[h, DIM:TOK] = z2[:, DIM:TOK]
            mmap[h] = (fade - kx[:, 0:DIM]).astype(BF)
            bmap[h] = kx[:, DIM:TOK]
            bsend[t, h] = kx[:, DIM:TOK].astype(BF)

        floor[...] = head_maps(
            proj, power, gates, select[...], masks, low, eye, put
        )

        @pl.when(t == 0)
        def _():
            load(1)

        @pl.when((t == 0) & outer)
        def _():
            meet()

        @pl.when(c == 0)
        def _():
            for h in range(HEADS):
                first_copy(t, h).start()
                sin[t, h] = jnp.zeros((DIM, DIM), BF)

        def finish_head(h):
            o = obuf[h % 2]
            level = jnp.mean(o * o, axis=-1, keepdims=True)
            o = o * lax.rsqrt(level + floor[:, HEADS + h : HEADS + h + 1])
            o = o.astype(BF)
            hid[:, h * DIM : (h + 1) * DIM] = o
            flipped = o.T
            for u in range(DIM // UNIT):
                row0 = h * DIM + u * UNIT
                span, rest = row0 // column, row0 % column
                to, i = rest // share, rest % share
                ht[t, to, span * share + i : span * share + i + UNIT] = flipped[
                    u * UNIT : (u + 1) * UNIT
                ]

        def send_pieces(h):
            for piece in range(PIECES):
                last = HEADS // PIECES * (piece + 1) - 1 if spans == HEADS else HEADS - 1
                if last == h:
                    hidden_own(t, piece).start()
                    for k in range(1, copies):
                        hidden_copy(t, k, piece).start()

        for h in range(HEADS):
            @pl.when(c > 0)
            def _():
                state_copy(t, h).wait_recv()

            s = sin[t, h]
            sout[t, h] = (mm(mmap[h], s) + bmap[h]).astype(BF)
            if h < HEADS - 1:
                obuf[h % 2] = mm(pmap[h], s) + rmap[h]
                if h > 0:
                    finish_head(h - 1)

            @pl.when((c > 0) & (c < spans - 1))
            def _():
                state_copy(t, h).start()

            if h == HEADS - 1:
                obuf[h % 2] = mm(pmap[h], s) + rmap[h]
                finish_head(h - 1)

            if h > 0:
                send_pieces(h - 1)
        finish_head(HEADS - 1)
        send_pieces(HEADS - 1)

        out_copy(t, down_wo).wait()
        for n in range(CH):
            block = slice(n * COLS, (n + 1) * COLS)
            y = xbuf[t, n].astype(F32) + mm(hid[...], wo[t, :, block])
            ybuf[t, n] = y.astype(BF)

            @pl.when(stage_of(t) < sections - 1)
            def _():
                stream_copy(t, n).start()

            @pl.when(is_down(t))
            def _():
                result_copy(t, n, down_out).start()

            @pl.when(jnp.logical_not(is_down(t)))
            def _():
                result_copy(t, n, up_out).start()

        @pl.when(t == 0)
        def _():
            relay_cots(0)

            @pl.when(outer)
            def _():
                start_cots(1)

            @pl.when(jnp.logical_not(outer))
            def _():
                relay_cots(1)

    def gradient(t):
        wait_cots(t)
        size = spans * share // PIECES
        for piece in range(PIECES):
            rows = pl.ds(piece * size, size)
            for j in range(copies):
                pltpu.make_async_copy(
                    hg.at[t, j, rows], hg.at[t, j, rows], h_recv.at[t, j, piece]
                ).wait()
            total = mm(hg[t, 0, piece * size : (piece + 1) * size], cot[t, 0])
            for j in range(1, copies):
                total += mm(hg[t, j, piece * size : (piece + 1) * size], cot[t, j])
            total = total.astype(BF)
            for row0 in range(0, size, UNIT):
                to, at_row = divmod(piece * size + row0, share)
                part[t, to, at_row : at_row + UNIT] = total[row0 : row0 + UNIT]
                if at_row + UNIT == share:
                    @pl.when(stays(t, to))
                    def _():
                        grad_own(t, to).start()

                    @pl.when(jnp.logical_not(stays(t, to)))
                    def _():
                        grad_copy(t, to).start()

    def turn(i, carry):
        middle = jnp.where(outer, 2, 1)
        is_section = (i == 0) | (i == middle)

        @pl.when(is_section)
        def _():
            section(jnp.where(i == 0, 0, 1))

        @pl.when(jnp.logical_not(is_section))
        def _():
            gradient(jnp.where(i == 3, 1, 0))

            @pl.when(outer & (i == 1))
            def _():
                relay_cots(1)

        return carry

    lax.fori_loop(0, 4, turn, 0)

    for j in range(2 * spans):
        pltpu.make_async_copy(gbuf.at[j], gbuf.at[j], g_recv.at[j]).wait()
    total = gbuf[0].astype(F32)
    for j in range(1, 2 * spans):
        total += gbuf[j].astype(F32)
    gsum[...] = total
    final = pltpu.make_async_copy(gsum, grad_out.at[0], go_sem)
    final.start()

    for t in range(2):
        for n in range(CH):
            result_copy(t, n, down_out).wait()

            @pl.when(stage_of(t) < sections - 1)
            def _():
                stream_copy(t, n).wait_send()

        @pl.when(c < spans - 1)
        def _():
            for h in range(HEADS):
                state_copy(t, h).wait_send()

        for way, to in ways:
            cot_copy(t, down_ct, way, to).wait_send()
            if copies == 4:
                cot_relay(t, way, to).wait_send()
        for k in range(1, copies):
            for piece in range(PIECES):
                hidden_copy(t, k, piece).wait_send()
        for to in range(spans):
            @pl.when(jnp.logical_not(stays(t, to)))
            def _():
                grad_copy(t, to).wait_send()

    final.wait()


def hand_over(down_in, up_in, grad_in, down_out, up_out, grad_out, acts, grad, in_sems, out_sems):
    rows = TOK // HANDS
    moves = []
    for i, (src, dst) in enumerate(((down_in, down_out), (up_in, up_out))):
        for n in range(HANDS):
            part = (0, 0, pl.ds(n * rows, rows))
            moves.append((src.at[part], acts.at[i, pl.ds(n * rows, rows)], dst.at[part]))
    moves.append((grad_in.at[0], grad, grad_out.at[0]))
    loads, stores = [], []
    for i, (src, here, dst) in enumerate(moves):
        loads.append(pltpu.make_async_copy(src, here, in_sems.at[i]))
        stores.append(pltpu.make_async_copy(here, dst, out_sems.at[i]))
        loads[i].start()
    for load, store in zip(loads, stores):
        load.wait()
        store.start()
    for store in stores:
        store.wait()


def per_device(dims, *arrays):
    sections, spans, copies = dims
    share = WIDTH // (spans * copies)
    hbm = pl.BlockSpec(memory_space=pl.ANY)
    vmem = pl.BlockSpec(memory_space=pltpu.VMEM)
    dma = pltpu.SemaphoreType.DMA
    down_acts, up_acts, grad = pl.pallas_call(
        functools.partial(kernel, dims),
        out_shape=(
            jax.ShapeDtypeStruct((1, 1, TOK, WIDTH), BF),
            jax.ShapeDtypeStruct((1, 1, TOK, WIDTH), BF),
            jax.ShapeDtypeStruct((1, share, WIDTH), F32),
        ),
        in_specs=[hbm] * 4 + [vmem] * 4 + [hbm] * 4,
        out_specs=(hbm, hbm, hbm),
        scratch_shapes=[
            pltpu.VMEM((2, WIDTH, 3 * WIDTH), BF),
            pltpu.VMEM((2, WIDTH, WIDTH), BF),
            pltpu.VMEM((2, 2 * HEADS, WIDTH), BF),
            pltpu.VMEM((2, 2 * HEADS, TOK), F32),
            pltpu.VMEM((TOK, TOK), BF),
            pltpu.VMEM((2, CH, TOK, COLS), BF),
            pltpu.VMEM((2, CH, TOK, COLS), BF),
            pltpu.VMEM((TOK, 3 * WIDTH), F32),
            pltpu.VMEM((TOK, WIDTH), BF),
            pltpu.VMEM((2, TOK, DIM), F32),
            pltpu.VMEM((len(MASKS), DIM, DIM), BF),
            pltpu.VMEM((WIDTH, DIM), BF),
            pltpu.VMEM((TOK, DIM), F32),
            pltpu.VMEM((HEADS, TOK, DIM), BF),
            pltpu.VMEM((HEADS, TOK, DIM), F32),
            pltpu.VMEM((HEADS, DIM, DIM), BF),
            pltpu.VMEM((HEADS, DIM, DIM), F32),
            pltpu.VMEM((2, HEADS, DIM, DIM), BF),
            pltpu.VMEM((2, HEADS, DIM, DIM), BF),
            pltpu.VMEM((2, HEADS, DIM, DIM), BF),
            pltpu.VMEM((2, copies, TOK, WIDTH), BF),
            pltpu.VMEM((2, copies, spans * share, TOK), BF),
            pltpu.VMEM((2, copies, spans * share, TOK), BF),
            pltpu.VMEM((2, spans, share, WIDTH), BF),
            pltpu.VMEM((2 * spans, share, WIDTH), BF),
            pltpu.VMEM((share, WIDTH), F32),
            dma((2, CH)),
            dma((2,)),
            dma((2, CH)),
            dma((2, CH)),
            dma((2, CH)),
            dma((2, HEADS)),
            dma((2, HEADS)),
            dma((2, 4)),
            dma((2, 4)),
            dma((2,)),
            dma((2, copies, PIECES)),
            dma((2, copies, PIECES)),
            dma((2 * spans,)),
            dma((2, spans)),
            dma,
        ],
        compiler_params=pltpu.CompilerParams(
            collective_id=0, has_side_effects=True, vmem_limit_bytes=60 * 1024 * 1024
        ),
    )(*arrays[:4], *(jnp.swapaxes(gates, 1, 2) for gates in arrays[4:6]), *arrays[6:])
    return pl.pallas_call(
        hand_over,
        out_shape=tuple(jax.ShapeDtypeStruct(a.shape, a.dtype) for a in (down_acts, up_acts, grad)),
        in_specs=[hbm] * 3,
        out_specs=(hbm, hbm, hbm),
        scratch_shapes=[
            pltpu.VMEM((2, TOK, WIDTH), BF),
            pltpu.VMEM((share, WIDTH), F32),
            dma((2 * HANDS + 1,)),
            dma((2 * HANDS + 1,)),
        ],
    )(down_acts, up_acts, grad)


def solution(mesh):
    dims = (mesh.shape["pipe"], mesh.shape["ctx"], mesh.shape["dp"])
    return jax.shard_map(
        functools.partial(per_device, dims),
        mesh=mesh,
        in_specs=(
            P("dp", "ctx", None),
            P("dp", "ctx", None),
            P("pipe", None, None),
            P("pipe", None, None),
            P("pipe", None, None),
            P("pipe", None, None),
            P("pipe", None),
            P("pipe", None),
            P("pipe", None, None),
            P("pipe", None, None),
            P("pipe", "dp", "ctx", None),
            P("pipe", "dp", "ctx", None),
        ),
        out_specs=(
            P("pipe", "dp", "ctx", None),
            P("pipe", "dp", "ctx", None),
            P("pipe", ("ctx", "dp"), None),
        ),
        check_vma=False,
    )
```

```python
import functools

import jax
import jax.numpy as jnp
from jax import lax
from jax.experimental import pallas as pl
from jax.experimental.pallas import tpu as pltpu
from jax.sharding import PartitionSpec as P

MESH = pl.DeviceIdType.MESH
EPSILON = 1e-06
EXACT = lax.Precision.HIGHEST
BF = jnp.bfloat16
F32 = jnp.float32
HEADS = 8
DIM = 128
TOK = 256
WIDTH = 1024
CH = 4
COLS = WIDTH // CH
UNIT = 32
PIECES = ((0, 2), (2, 4), (4, 6), (6, 7), (7, 8))
HANDS = 2


def mm(a, b):
    return jnp.dot(a, b, preferred_element_type=F32)


def mm_nt(a, b):
    return lax.dot_general(a, b, (((1,), (1,)), ((), ())), preferred_element_type=F32)


def band_mask(inner, outer):
    row = lax.broadcasted_iota(jnp.int32, (DIM, DIM), 0)
    col = lax.broadcasted_iota(jnp.int32, (DIM, DIM), 1)
    if outer == 1:
        return (row == col).astype(F32)
    if inner == 0:
        return (row >= col).astype(F32)
    same = (row // outer) == (col // outer)
    return (same & ((row // inner) > (col // inner))).astype(F32)


MASKS = ((1, 1), (1, 8), (8, 64), (64, 128), (0, 128))


def eightfold(starts, powers):
    squares = [mm(n, n).astype(BF) for n in powers]
    halves = [t + mm(n, t).astype(BF) for t, n in zip(starts, squares)]
    fourths = [mm(n, n).astype(BF) for n in squares]
    return [t + mm(n, t).astype(BF) for t, n in zip(halves, fourths)]


def block_inverses(parts, masks):
    inner = [a * masks[1] for a in parts]
    results = eightfold([masks[0] - a for a in inner], inner)
    steps = [mm(t, a * masks[2]).astype(BF) for t, a in zip(results, parts)]
    results = [t - mm(n, t).astype(BF) for t, n in zip(results, steps)]
    results = eightfold(results, steps)
    steps = [mm(a * masks[3], t).astype(BF) for t, a in zip(results, parts)]
    results = [t - mm(t, y).astype(BF) for t, y in zip(results, steps)]
    return results


def decay_of(gap):
    return jnp.exp(jnp.minimum(gap, 0.0)).astype(BF)


def lane_of(compact, lane):
    return jnp.broadcast_to(compact[:, lane : lane + 1], (TOK, DIM))


def gate_rows(logits, rates, triangle):
    row = lax.broadcasted_iota(jnp.int32, (2 * HEADS, TOK), 0)
    decay = -rates * (jnp.maximum(logits, 0.0) + jnp.log1p(jnp.exp(-jnp.abs(logits))))
    high = decay.astype(BF)
    rest = decay - high.astype(F32)
    middle = rest.astype(BF)
    low = (rest - middle.astype(F32)).astype(BF)
    sums = mm(jnp.concatenate([high, middle, low], axis=0), triangle)
    total = sums[0:16] + sums[16:32] + sums[32:48]
    return jnp.where(row < HEADS, jax.nn.sigmoid(logits), total)


def head_maps(proj, power, gates, select, masks, low, eye, put):
    first, second = slice(0, DIM), slice(DIM, TOK)
    rstd = lax.rsqrt(power)
    columns = jnp.concatenate([gates, jnp.zeros((DIM - 2 * HEADS, TOK), F32)], axis=0).T
    beta, cum = gates[0:HEADS], gates[HEADS : 2 * HEADS]
    last = jnp.broadcast_to(cum[:, TOK - 1 : TOK], (HEADS, TOK))
    weights = (beta * jnp.exp(last - cum)).astype(BF)
    fades = jnp.exp(last[:, 0:DIM])
    strengths = beta.astype(BF)

    def square_sums(start):
        raw = proj[:, start : start + WIDTH]
        return mm((raw * raw).astype(BF), select)

    nk = rstd * lax.rsqrt(square_sums(WIDTH) * (rstd * rstd) + EPSILON)

    def prepare(h):
        lane = HEADS + h
        q = proj[:, h * DIM : (h + 1) * DIM]
        k = proj[:, WIDTH + h * DIM : WIDTH + (h + 1) * DIM] * lane_of(nk, lane)
        v = proj[:, 2 * WIDTH + h * DIM : 2 * WIDTH + (h + 1) * DIM]
        c = lane_of(columns, lane)
        growth = jnp.exp(c)
        qb, kb = q.astype(BF), k.astype(BF)
        rhs = jnp.concatenate([(k * growth).astype(BF), (v * rstd).astype(BF)], axis=1)
        flipped = kb.T * weights[h : h + 1, :]
        qg = q * growth
        crow, brow = cum[h : h + 1, :], strengths[h : h + 1, :]
        d11 = decay_of(c[first] - crow[:, first]) * brow[:, first]
        d21 = decay_of(c[second] - crow[:, first]) * brow[:, first]
        d22 = decay_of(c[second] - crow[:, second]) * brow[:, second]
        g1 = mm_nt(jnp.concatenate([kb, qb], axis=0), kb[first]).astype(BF)
        g2 = mm_nt(jnp.concatenate([kb[second], qb[second]], axis=0), kb[second]).astype(BF)
        a11 = g1[0:128] * d11
        a21 = g1[128:256] * d21
        s11 = g1[256:384] * (d11 * low)
        s21 = g1[384:512] * d21
        a22 = g2[0:128] * d22
        s22 = g2[128:256] * (d22 * low)
        return h, a11, a22, a21, s11, s21, s22, rhs, flipped, qg

    def complete(state, inverses):
        n = len(state)
        x1 = [mm(inverses[i], state[i][7][first]).astype(BF) for i in range(n)]
        r2 = [state[i][7][second] - mm(state[i][3], x1[i]).astype(BF) for i in range(n)]
        x2 = [mm(inverses[n + i], r2[i]).astype(BF) for i in range(n)]
        for i in range(n):
            h, _, _, _, s11, s21, s22, _, flipped, qg = state[i]
            x = jnp.concatenate([x1[i], x2[i]], axis=0)
            z1 = mm(s11, x1[i])
            z2 = mm(jnp.concatenate([s21, s22], axis=1), x)
            kx = mm(flipped, x)
            put(h, qg, z1, z2, kx, eye * fades[h : h + 1, :])

    state = [prepare(h) for h in range(HEADS)]
    inverses = block_inverses([s[1] for s in state] + [s[2] for s in state], masks)
    complete(state, inverses)
    return (EPSILON * DIM) * (square_sums(0) + EPSILON * power)


def kernel(
    dims,
    down_in, up_in, down_qkv, up_qkv, down_gates, up_gates, down_rates, up_rates,
    down_wo, up_wo, down_ct, up_ct,
    down_out, up_out, grad_out,
    wqkv, wo, wg, rate_in, rates, triangle, xbuf, ybuf, proj, hid, obuf, maskb, select, floor, pmap, rmap, mmap, bmap, bsend, sin, sout,
    cot, ht, hg, part, gbuf, gsum,
    gate_sem, w_sem, wo_sem, x_recv, x_send, y_sem, s_recv, s_send, ct_recv, ct_send,
    ct_own, h_recv, h_send, g_recv, g_send, go_sem,
):
    sections, spans, copies = dims
    p, c, d = lax.axis_index("pipe"), lax.axis_index("ctx"), lax.axis_index("dp")
    low_half = p < sections // 2
    share = WIDTH // (spans * copies)
    column = WIDTH // spans

    def is_down(t):
        return low_half == (t == 0)

    def at(pipe, ctx, dp):
        return (pipe, ctx, dp)

    def remote(src, dst, send, recv, where):
        return pltpu.make_async_remote_copy(
            src_ref=src, dst_ref=dst, send_sem=send, recv_sem=recv,
            device_id=where, device_id_type=MESH,
        )

    def weight_copy(t, n, qkv):
        rows = pl.ds(n * COLS, COLS)
        return pltpu.make_async_copy(qkv.at[0, rows], wqkv.at[t, rows], w_sem.at[t, n])

    def out_copy(t, out):
        return pltpu.make_async_copy(out.at[0], wo.at[t], wo_sem.at[t])

    def start_weights(t, qkv, out):
        for n in range(CH):
            weight_copy(t, n, qkv).start()
        out_copy(t, out).start()

    def input_copy(src, n):
        return pltpu.make_async_copy(
            src.at[0, :, pl.ds(n * COLS, COLS)], xbuf.at[0, n], x_recv.at[0, n]
        )

    @pl.when(p == 0)
    def _():
        for n in range(CH):
            input_copy(down_in, n).start()

    @pl.when(p == sections - 1)
    def _():
        for n in range(CH):
            input_copy(up_in, n).start()

    def load(t):
        @pl.when(is_down(t))
        def _():
            start_weights(t, down_qkv, down_wo)

        @pl.when(jnp.logical_not(is_down(t)))
        def _():
            start_weights(t, up_qkv, up_wo)

    def gate_copies(t, gates, rate):
        return (
            pltpu.make_async_copy(gates.at[0], wg.at[t], gate_sem.at[t, 0]),
            pltpu.make_async_copy(rate, rate_in.at[t], gate_sem.at[t, 1]),
        )

    for t in range(2):
        @pl.when(is_down(t))
        def _():
            for copy in gate_copies(t, down_gates, down_rates):
                copy.start()

        @pl.when(jnp.logical_not(is_down(t)))
        def _():
            for copy in gate_copies(t, up_gates, up_rates):
                copy.start()

    load(0)

    barrier = pltpu.get_barrier_semaphore()
    mirror = sections - 1 - p
    pair = p + 1 - 2 * lax.rem(p, 2)
    peers = [at(pair, c, d), at(mirror, c, d)]
    for k in range(1, spans):
        other = lax.rem(c + k, spans)
        peers += [at(p, other, d), at(mirror, other, d)]
    for k in range(1, copies):
        peers.append(at(p, c, lax.rem(d + k, copies)))
    for peer in peers:
        pl.semaphore_signal(barrier, inc=1, device_id=peer, device_id_type=MESH)

    for level, (inner, outer_size) in enumerate(MASKS):
        maskb[level] = band_mask(inner, outer_size).astype(BF)
    for h in range(HEADS):
        lanes = lax.broadcasted_iota(jnp.int32, (DIM, DIM), 1)
        select[h * DIM : (h + 1) * DIM] = (lanes == HEADS + h).astype(F32).astype(BF)
    token = lax.broadcasted_iota(jnp.int32, (TOK, TOK), 0)
    until = lax.broadcasted_iota(jnp.int32, (TOK, TOK), 1)
    triangle[...] = (token <= until).astype(F32).astype(BF)
    for t in range(2):
        for copy in gate_copies(t, down_gates, down_rates):
            copy.wait()
        rate = jnp.concatenate(
            [jnp.zeros((1, HEADS), F32), rate_in[t], jnp.zeros((1, DIM - 2 * HEADS), F32)], axis=1
        )
        rates[t] = jnp.broadcast_to(rate, (TOK, DIM)).T[0 : 2 * HEADS]

    half = TOK // 2
    before, after = lax.rem(d + copies - 1, copies), lax.rem(d + 1, copies)
    ways = ((0, after),) if copies == 2 else ((0, after), (1, before))

    def cot_own(t, source):
        return pltpu.make_async_copy(source.at[0, 0], cot.at[t, d], ct_own.at[t])

    def cot_copy(t, source, way, to):
        return remote(
            source.at[0, 0], cot.at[t, d], ct_send.at[t, way], ct_recv.at[t, way], at(p, c, to)
        )

    def cot_relay(t, way, to):
        owner = before if way == 0 else after
        part_rows = pl.ds(way * half, half)
        return remote(
            cot.at[t, owner, part_rows], cot.at[t, owner, part_rows], ct_send.at[t, 2 + way],
            ct_recv.at[t, 2 + way], at(p, c, to),
        )

    def start_cot(t, source):
        cot_own(t, source).start()
        for way, to in ways:
            cot_copy(t, source, way, to).start()

    def relay_cots(t):
        for way, to in ways:
            cot_copy(t, down_ct, way, to).wait_recv()
        if copies == 4:
            for way, to in ways:
                cot_relay(t, way, to).start()

    def wait_cots(t):
        cot_own(t, down_ct).wait()
        if copies == 4:
            for way, to in ways:
                cot_relay(t, way, to).wait_recv()

    def start_cots(t):
        @pl.when(is_down(t))
        def _():
            start_cot(t, down_ct)

        @pl.when(jnp.logical_not(is_down(t)))
        def _():
            start_cot(t, up_ct)

    def meet():
        pl.semaphore_wait(barrier, len(peers))
        start_cots(0)

        @pl.when(jnp.logical_not(outer))
        def _():
            start_cots(1)

    outer = (p == 0) | (p == sections - 1)

    @pl.when(jnp.logical_not(outer))
    def _():
        meet()

    def state_copy(t, h):
        return remote(
            sout.at[t, h], sin.at[t, h], s_send.at[t, h], s_recv.at[t, h],
            at(p, lax.rem(c + 1, spans), d),
        )

    def first_copy(t, h):
        return remote(
            bsend.at[t, h], sin.at[t, h], s_send.at[t, h], s_recv.at[t, h],
            at(p, lax.rem(c + 1, spans), d),
        )

    def stage_of(t):
        early = jnp.where(low_half, p, sections - 1 - p)
        return jnp.where(t == 0, early, sections - 1 - early)

    def stream_copy(t, n):
        slot = jnp.where(stage_of(t) == 0, 0, 1)
        to = jnp.clip(jnp.where(is_down(t), p + 1, p - 1), 0, sections - 1)
        return remote(
            ybuf.at[t, n], xbuf.at[slot, n], x_send.at[t, n], x_recv.at[slot, n], at(to, c, d)
        )

    def result_copy(t, n, out):
        return pltpu.make_async_copy(
            ybuf.at[t, n], out.at[0, 0, :, pl.ds(n * COLS, COLS)], y_sem.at[t, n]
        )

    def piece_rows(piece):
        first, end = (spans * share // HEADS * head for head in PIECES[piece])
        return pl.ds(first, end - first)

    def hidden_own(t, piece):
        rows = piece_rows(piece)
        return pltpu.make_async_copy(
            ht.at[t, d, rows], hg.at[t, d, rows], h_recv.at[t, d, piece]
        )

    def hidden_copy(t, k, piece):
        to = lax.rem(d + k, copies)
        rows = piece_rows(piece)
        return remote(
            ht.at[t, to, rows], hg.at[t, d, rows], h_send.at[t, k - 1, piece],
            h_recv.at[t, d, piece], at(p, c, to),
        )

    def grad_own(t, to):
        return pltpu.make_async_copy(part.at[t, to], gbuf.at[to], g_recv.at[to])

    def grad_copy(t, to):
        slot = c + jnp.where(is_down(t), 0, spans)
        pipe = jnp.where(is_down(t), p, mirror)
        return remote(
            part.at[t, to], gbuf.at[slot], g_send.at[t, to], g_recv.at[slot], at(pipe, to, d)
        )

    def stays(t, to):
        return (c == to) & is_down(t)

    def section(t):
        ones = jnp.ones((COLS, DIM), BF)
        square = jnp.zeros((TOK, DIM), F32)
        square_row = jnp.zeros((2 * HEADS, TOK), F32)
        logits = jnp.zeros((2 * HEADS, TOK), F32)
        for n in range(CH):
            pltpu.make_async_copy(xbuf.at[t, n], xbuf.at[t, n], x_recv.at[t, n]).wait()
            weight_copy(t, n, down_qkv).wait()
            x = xbuf[t, n]
            xf = x.astype(F32)
            x2 = (xf * xf).astype(BF)
            square += mm(x2, ones)
            square_row += mm_nt(ones[0 : 2 * HEADS, 0:DIM], x2[:, 0:DIM])
            square_row += mm_nt(ones[0 : 2 * HEADS, 0:DIM], x2[:, DIM:COLS])
            logits += mm_nt(wg[t, :, n * COLS : (n + 1) * COLS], x)
            for j in range(6):
                block = slice(512 * j, 512 * (j + 1))
                product = mm(x, wqkv[t, n * COLS : (n + 1) * COLS, block])
                if n == 0:
                    proj[:, block] = product
                else:
                    proj[:, block] += product

        power = square * (1.0 / WIDTH) + EPSILON
        scale = lax.rsqrt(square_row * (1.0 / WIDTH) + EPSILON)
        gates = gate_rows(logits * scale, rates[t], triangle[...])


        masks = [maskb[level] for level in range(4)]
        low = maskb[4]
        eye = maskb[0].astype(F32)

        def put(h, qg, z1, z2, kx, fade):
            pmap[h, 0:DIM] = (qg[0:DIM] - z1[:, 0:DIM]).astype(BF)
            pmap[h, DIM:TOK] = (qg[DIM:TOK] - z2[:, 0:DIM]).astype(BF)
            rmap[h, 0:DIM] = z1[:, DIM:TOK]
            rmap[h, DIM:TOK] = z2[:, DIM:TOK]
            mmap[h] = (fade - kx[:, 0:DIM]).astype(BF)
            bmap[h] = kx[:, DIM:TOK]
            bsend[t, h] = kx[:, DIM:TOK].astype(BF)

        floor[...] = head_maps(
            proj, power, gates, select[...], masks, low, eye, put
        )

        @pl.when(t == 0)
        def _():
            load(1)

        @pl.when((t == 0) & outer)
        def _():
            meet()

        @pl.when(c == 0)
        def _():
            for h in range(HEADS):
                first_copy(t, h).start()
                sin[t, h] = jnp.zeros((DIM, DIM), BF)

        def finish_head(h):
            o = obuf[h % 2]
            level = jnp.mean(o * o, axis=-1, keepdims=True)
            o = o * lax.rsqrt(level + floor[:, HEADS + h : HEADS + h + 1])
            o = o.astype(BF)
            hid[:, h * DIM : (h + 1) * DIM] = o
            flipped = o.T
            for u in range(DIM // UNIT):
                row0 = h * DIM + u * UNIT
                span, rest = row0 // column, row0 % column
                to, i = rest // share, rest % share
                ht[t, to, span * share + i : span * share + i + UNIT] = flipped[
                    u * UNIT : (u + 1) * UNIT
                ]

        def send_pieces(h):
            for piece, (_, end) in enumerate(PIECES):
                if h == (end - 1 if spans == HEADS else HEADS - 1):
                    hidden_own(t, piece).start()
                    for k in range(1, copies):
                        hidden_copy(t, k, piece).start()

        for h in range(HEADS):
            @pl.when(c > 0)
            def _():
                state_copy(t, h).wait_recv()

            s = sin[t, h]
            sout[t, h] = (mm(mmap[h], s) + bmap[h]).astype(BF)
            if h < HEADS - 1:
                obuf[h % 2] = mm(pmap[h], s) + rmap[h]
                if h > 0:
                    finish_head(h - 1)

            @pl.when((c > 0) & (c < spans - 1))
            def _():
                state_copy(t, h).start()

            if h == HEADS - 1:
                obuf[h % 2] = mm(pmap[h], s) + rmap[h]
                finish_head(h - 1)

            if h > 0:
                send_pieces(h - 1)
        finish_head(HEADS - 1)
        send_pieces(HEADS - 1)

        out_copy(t, down_wo).wait()
        for n in range(CH):
            block = slice(n * COLS, (n + 1) * COLS)
            y = xbuf[t, n].astype(F32) + mm(hid[...], wo[t, :, block])
            ybuf[t, n] = y.astype(BF)

            @pl.when(stage_of(t) < sections - 1)
            def _():
                stream_copy(t, n).start()

        @pl.when(is_down(t))
        def _():
            for n in range(CH):
                result_copy(t, n, down_out).start()

        @pl.when(jnp.logical_not(is_down(t)))
        def _():
            for n in range(CH):
                result_copy(t, n, up_out).start()

        @pl.when(t == 0)
        def _():
            relay_cots(0)

            @pl.when(outer)
            def _():
                start_cots(1)

            @pl.when(jnp.logical_not(outer))
            def _():
                relay_cots(1)

    def gradient(t):
        wait_cots(t)
        for piece in range(len(PIECES)):
            rows = piece_rows(piece)
            start, size = rows.start, rows.size
            for j in range(copies):
                pltpu.make_async_copy(
                    hg.at[t, j, rows], hg.at[t, j, rows], h_recv.at[t, j, piece]
                ).wait()
            total = mm(hg[t, 0, start : start + size], cot[t, 0])
            for j in range(1, copies):
                total += mm(hg[t, j, start : start + size], cot[t, j])
            total = total.astype(BF)
            for row0 in range(0, size, UNIT):
                to, at_row = divmod(start + row0, share)
                part[t, to, at_row : at_row + UNIT] = total[row0 : row0 + UNIT]
                if at_row + UNIT == share:
                    @pl.when(stays(t, to))
                    def _():
                        grad_own(t, to).start()

                    @pl.when(jnp.logical_not(stays(t, to)))
                    def _():
                        grad_copy(t, to).start()

    def turn(i, carry):
        middle = jnp.where(outer, 2, 1)
        is_section = (i == 0) | (i == middle)

        @pl.when(is_section)
        def _():
            section(jnp.where(i == 0, 0, 1))

        @pl.when(jnp.logical_not(is_section))
        def _():
            gradient(jnp.where(i == 3, 1, 0))

            @pl.when(outer & (i == 1))
            def _():
                relay_cots(1)

        return carry

    lax.fori_loop(0, 4, turn, 0)

    for j in range(2 * spans):
        pltpu.make_async_copy(gbuf.at[j], gbuf.at[j], g_recv.at[j]).wait()
    total = gbuf[0].astype(F32)
    for j in range(1, 2 * spans):
        total += gbuf[j].astype(F32)
    gsum[...] = total
    final = pltpu.make_async_copy(gsum, grad_out.at[0], go_sem)
    final.start()

    for t in range(2):
        for n in range(CH):
            result_copy(t, n, down_out).wait()

            @pl.when(stage_of(t) < sections - 1)
            def _():
                stream_copy(t, n).wait_send()

        @pl.when(c < spans - 1)
        def _():
            for h in range(HEADS):
                state_copy(t, h).wait_send()

        for way, to in ways:
            cot_copy(t, down_ct, way, to).wait_send()
            if copies == 4:
                cot_relay(t, way, to).wait_send()
        for k in range(1, copies):
            for piece in range(len(PIECES)):
                hidden_copy(t, k, piece).wait_send()
        for to in range(spans):
            @pl.when(jnp.logical_not(stays(t, to)))
            def _():
                grad_copy(t, to).wait_send()

    final.wait()


def hand_over(down_in, up_in, grad_in, down_out, up_out, grad_out, acts, grad, in_sems, out_sems):
    rows = TOK // HANDS
    moves = []
    for i, (src, dst) in enumerate(((down_in, down_out), (up_in, up_out))):
        for n in range(HANDS):
            part = (0, 0, pl.ds(n * rows, rows))
            moves.append((src.at[part], acts.at[i, pl.ds(n * rows, rows)], dst.at[part]))
    moves.append((grad_in.at[0], grad, grad_out.at[0]))
    loads, stores = [], []
    for i, (src, here, dst) in enumerate(moves):
        loads.append(pltpu.make_async_copy(src, here, in_sems.at[i]))
        stores.append(pltpu.make_async_copy(here, dst, out_sems.at[i]))
        loads[i].start()
    for load, store in zip(loads, stores):
        load.wait()
        store.start()
    for store in stores:
        store.wait()


def per_device(dims, *arrays):
    sections, spans, copies = dims
    share = WIDTH // (spans * copies)
    hbm = pl.BlockSpec(memory_space=pl.ANY)
    dma = pltpu.SemaphoreType.DMA
    down_acts, up_acts, grad = pl.pallas_call(
        functools.partial(kernel, dims),
        out_shape=(
            jax.ShapeDtypeStruct((1, 1, TOK, WIDTH), BF),
            jax.ShapeDtypeStruct((1, 1, TOK, WIDTH), BF),
            jax.ShapeDtypeStruct((1, share, WIDTH), F32),
        ),
        in_specs=[hbm] * 12,
        out_specs=(hbm, hbm, hbm),
        scratch_shapes=[
            pltpu.VMEM((2, WIDTH, 3 * WIDTH), BF),
            pltpu.VMEM((2, WIDTH, WIDTH), BF),
            pltpu.VMEM((2, 2 * HEADS, WIDTH), BF),
            pltpu.VMEM((2, 1, HEADS), F32),
            pltpu.VMEM((2, 2 * HEADS, TOK), F32),
            pltpu.VMEM((TOK, TOK), BF),
            pltpu.VMEM((2, CH, TOK, COLS), BF),
            pltpu.VMEM((2, CH, TOK, COLS), BF),
            pltpu.VMEM((TOK, 3 * WIDTH), F32),
            pltpu.VMEM((TOK, WIDTH), BF),
            pltpu.VMEM((2, TOK, DIM), F32),
            pltpu.VMEM((len(MASKS), DIM, DIM), BF),
            pltpu.VMEM((WIDTH, DIM), BF),
            pltpu.VMEM((TOK, DIM), F32),
            pltpu.VMEM((HEADS, TOK, DIM), BF),
            pltpu.VMEM((HEADS, TOK, DIM), F32),
            pltpu.VMEM((HEADS, DIM, DIM), BF),
            pltpu.VMEM((HEADS, DIM, DIM), F32),
            pltpu.VMEM((2, HEADS, DIM, DIM), BF),
            pltpu.VMEM((2, HEADS, DIM, DIM), BF),
            pltpu.VMEM((2, HEADS, DIM, DIM), BF),
            pltpu.VMEM((2, copies, TOK, WIDTH), BF),
            pltpu.VMEM((2, copies, spans * share, TOK), BF),
            pltpu.VMEM((2, copies, spans * share, TOK), BF),
            pltpu.VMEM((2, spans, share, WIDTH), BF),
            pltpu.VMEM((2 * spans, share, WIDTH), BF),
            pltpu.VMEM((share, WIDTH), F32),
            dma((2, 2)),
            dma((2, CH)),
            dma((2,)),
            dma((2, CH)),
            dma((2, CH)),
            dma((2, CH)),
            dma((2, HEADS)),
            dma((2, HEADS)),
            dma((2, 4)),
            dma((2, 4)),
            dma((2,)),
            dma((2, copies, len(PIECES))),
            dma((2, copies, len(PIECES))),
            dma((2 * spans,)),
            dma((2, spans)),
            dma,
        ],
        compiler_params=pltpu.CompilerParams(
            collective_id=0, has_side_effects=True, vmem_limit_bytes=60 * 1024 * 1024
        ),
    )(*arrays[:4], *(jnp.swapaxes(gates, 1, 2) for gates in arrays[4:6]), *arrays[6:])
    return pl.pallas_call(
        hand_over,
        out_shape=tuple(jax.ShapeDtypeStruct(a.shape, a.dtype) for a in (down_acts, up_acts, grad)),
        in_specs=[hbm] * 3,
        out_specs=(hbm, hbm, hbm),
        scratch_shapes=[
            pltpu.VMEM((2, TOK, WIDTH), BF),
            pltpu.VMEM((share, WIDTH), F32),
            dma((2 * HANDS + 1,)),
            dma((2 * HANDS + 1,)),
        ],
    )(down_acts, up_acts, grad)


def solution(mesh):
    dims = (mesh.shape["pipe"], mesh.shape["ctx"], mesh.shape["dp"])
    return jax.shard_map(
        functools.partial(per_device, dims),
        mesh=mesh,
        in_specs=(
            P("dp", "ctx", None),
            P("dp", "ctx", None),
            P("pipe", None, None),
            P("pipe", None, None),
            P("pipe", None, None),
            P("pipe", None, None),
            P("pipe", None),
            P("pipe", None),
            P("pipe", None, None),
            P("pipe", None, None),
            P("pipe", "dp", "ctx", None),
            P("pipe", "dp", "ctx", None),
        ),
        out_specs=(
            P("pipe", "dp", "ctx", None),
            P("pipe", "dp", "ctx", None),
            P("pipe", ("ctx", "dp"), None),
        ),
        check_vma=False,
    )
```

```python
import functools

import jax
import jax.numpy as jnp
from jax import lax
from jax.experimental import pallas as pl
from jax.experimental.pallas import tpu as pltpu
from jax.sharding import PartitionSpec as P

MESH = pl.DeviceIdType.MESH
EPSILON = 1e-06
EXACT = lax.Precision.HIGHEST
BF = jnp.bfloat16
F32 = jnp.float32
HEADS = 8
DIM = 128
TOK = 256
WIDTH = 1024
CH = 4
COLS = WIDTH // CH
UNIT = 32
PIECES = ((0, 2), (2, 4), (4, 6), (6, 8))


def mm(a, b):
    return jnp.dot(a, b, preferred_element_type=F32)


def mm_nt(a, b):
    return lax.dot_general(a, b, (((1,), (1,)), ((), ())), preferred_element_type=F32)


def band_mask(inner, outer):
    row = lax.broadcasted_iota(jnp.int32, (DIM, DIM), 0)
    col = lax.broadcasted_iota(jnp.int32, (DIM, DIM), 1)
    if outer == 1:
        return (row == col).astype(F32)
    if inner == 0:
        return (row >= col).astype(F32)
    same = (row // outer) == (col // outer)
    return (same & ((row // inner) > (col // inner))).astype(F32)


MASKS = ((1, 1), (1, 8), (8, 64), (64, 128), (0, 128))


def eightfold(starts, powers):
    squares = [mm(n, n).astype(BF) for n in powers]
    halves = [t + mm(n, t).astype(BF) for t, n in zip(starts, squares)]
    fourths = [mm(n, n).astype(BF) for n in squares]
    return [t + mm(n, t).astype(BF) for t, n in zip(halves, fourths)]


def block_inverses(parts, masks):
    inner = [a * masks[1] for a in parts]
    results = eightfold([masks[0] - a for a in inner], inner)
    steps = [mm(t, a * masks[2]).astype(BF) for t, a in zip(results, parts)]
    results = [t - mm(n, t).astype(BF) for t, n in zip(results, steps)]
    results = eightfold(results, steps)
    steps = [mm(a * masks[3], t).astype(BF) for t, a in zip(results, parts)]
    results = [t - mm(t, y).astype(BF) for t, y in zip(results, steps)]
    return results


def decay_of(gap):
    return jnp.exp(jnp.minimum(gap, 0.0)).astype(BF)


def lane_of(compact, lane):
    return jnp.broadcast_to(compact[:, lane : lane + 1], (TOK, DIM))


def gate_rows(logits, rates, triangle):
    row = lax.broadcasted_iota(jnp.int32, (2 * HEADS, TOK), 0)
    decay = -rates * (jnp.maximum(logits, 0.0) + jnp.log1p(jnp.exp(-jnp.abs(logits))))
    high = decay.astype(BF)
    rest = decay - high.astype(F32)
    middle = rest.astype(BF)
    low = (rest - middle.astype(F32)).astype(BF)
    sums = mm(jnp.concatenate([high, middle, low], axis=0), triangle)
    total = sums[0:16] + sums[16:32] + sums[32:48]
    return jnp.where(row < HEADS, jax.nn.sigmoid(logits), total)


def head_maps(proj, power, gates, select, masks, low, eye, put):
    first, second = slice(0, DIM), slice(DIM, TOK)
    rstd = lax.rsqrt(power)
    columns = jnp.concatenate([gates, jnp.zeros((DIM - 2 * HEADS, TOK), F32)], axis=0).T
    beta, cum = gates[0:HEADS], gates[HEADS : 2 * HEADS]
    last = jnp.broadcast_to(cum[:, TOK - 1 : TOK], (HEADS, TOK))
    weights = (beta * jnp.exp(last - cum)).astype(BF)
    fades = jnp.exp(last[:, 0:DIM])
    strengths = beta.astype(BF)

    def square_sums(start):
        raw = proj[:, start : start + WIDTH]
        return mm((raw * raw).astype(BF), select)

    nk = rstd * lax.rsqrt(square_sums(WIDTH) * (rstd * rstd) + EPSILON)

    def prepare(h):
        lane = HEADS + h
        q = proj[:, h * DIM : (h + 1) * DIM]
        k = proj[:, WIDTH + h * DIM : WIDTH + (h + 1) * DIM] * lane_of(nk, lane)
        v = proj[:, 2 * WIDTH + h * DIM : 2 * WIDTH + (h + 1) * DIM]
        c = lane_of(columns, lane)
        growth = jnp.exp(c)
        qb, kb = q.astype(BF), k.astype(BF)
        rhs = jnp.concatenate([(k * growth).astype(BF), (v * rstd).astype(BF)], axis=1)
        flipped = kb.T * weights[h : h + 1, :]
        qg = q * growth
        crow, brow = cum[h : h + 1, :], strengths[h : h + 1, :]
        d11 = decay_of(c[first] - crow[:, first]) * brow[:, first]
        d21 = decay_of(c[second] - crow[:, first]) * brow[:, first]
        d22 = decay_of(c[second] - crow[:, second]) * brow[:, second]
        g1 = mm_nt(jnp.concatenate([kb, qb], axis=0), kb[first]).astype(BF)
        g2 = mm_nt(jnp.concatenate([kb[second], qb[second]], axis=0), kb[second]).astype(BF)
        a11 = g1[0:128] * d11
        a21 = g1[128:256] * d21
        s11 = g1[256:384] * (d11 * low)
        s21 = g1[384:512] * d21
        a22 = g2[0:128] * d22
        s22 = g2[128:256] * (d22 * low)
        return h, a11, a22, a21, s11, s21, s22, rhs, flipped, qg

    def complete(state, inverses):
        n = len(state)
        x1 = [mm(inverses[i], state[i][7][first]).astype(BF) for i in range(n)]
        r2 = [state[i][7][second] - mm(state[i][3], x1[i]).astype(BF) for i in range(n)]
        x2 = [mm(inverses[n + i], r2[i]).astype(BF) for i in range(n)]
        for i in range(n):
            h, _, _, _, s11, s21, s22, _, flipped, qg = state[i]
            x = jnp.concatenate([x1[i], x2[i]], axis=0)
            z1 = mm(s11, x1[i])
            z2 = mm(jnp.concatenate([s21, s22], axis=1), x)
            kx = mm(flipped, x)
            put(h, qg, z1, z2, kx, eye * fades[h : h + 1, :])

    state = [prepare(h) for h in range(HEADS)]
    inverses = block_inverses([s[1] for s in state] + [s[2] for s in state], masks)
    complete(state, inverses)
    return (EPSILON * DIM) * (square_sums(0) + EPSILON * power)


def kernel(
    dims,
    down_in, up_in, down_qkv, up_qkv, down_gates, up_gates, down_rates, up_rates,
    down_wo, up_wo, down_ct, up_ct,
    ybuf, gsum,
    wqkv, wo, wg, rate_in, rates, triangle, xbuf, proj, hid, obuf, maskb, select, floor, pmap, rmap, mmap, bmap, bsend, sin, sout,
    cot, ht, hg, part, gbuf,
    gate_sem, w_sem, wo_sem, x_recv, x_send, s_recv, s_send, ct_recv, ct_send,
    ct_own, h_recv, h_send, g_recv, g_send,
):
    sections, spans, copies = dims
    p, c, d = lax.axis_index("pipe"), lax.axis_index("ctx"), lax.axis_index("dp")
    low_half = p < sections // 2
    share = WIDTH // (spans * copies)
    column = WIDTH // spans

    def is_down(t):
        return low_half == (t == 0)

    def at(pipe, ctx, dp):
        return (pipe, ctx, dp)

    def remote(src, dst, send, recv, where):
        return pltpu.make_async_remote_copy(
            src_ref=src, dst_ref=dst, send_sem=send, recv_sem=recv,
            device_id=where, device_id_type=MESH,
        )

    def weight_copy(t, n, qkv):
        rows = pl.ds(n * COLS, COLS)
        return pltpu.make_async_copy(qkv.at[0, rows], wqkv.at[t, rows], w_sem.at[t, n])

    def out_copy(t, out):
        return pltpu.make_async_copy(out.at[0], wo.at[t], wo_sem.at[t])

    def start_weights(t, qkv, out):
        for n in range(CH):
            weight_copy(t, n, qkv).start()
        out_copy(t, out).start()

    def input_copy(src, n):
        return pltpu.make_async_copy(
            src.at[0, :, pl.ds(n * COLS, COLS)], xbuf.at[0, n], x_recv.at[0, n]
        )

    @pl.when(p == 0)
    def _():
        for n in range(CH):
            input_copy(down_in, n).start()

    @pl.when(p == sections - 1)
    def _():
        for n in range(CH):
            input_copy(up_in, n).start()

    def load(t):
        @pl.when(is_down(t))
        def _():
            start_weights(t, down_qkv, down_wo)

        @pl.when(jnp.logical_not(is_down(t)))
        def _():
            start_weights(t, up_qkv, up_wo)

    def gate_copies(t, gates, rate):
        return (
            pltpu.make_async_copy(gates.at[0], wg.at[t], gate_sem.at[t, 0]),
            pltpu.make_async_copy(rate, rate_in.at[t], gate_sem.at[t, 1]),
        )

    for t in range(2):
        @pl.when(is_down(t))
        def _():
            for copy in gate_copies(t, down_gates, down_rates):
                copy.start()

        @pl.when(jnp.logical_not(is_down(t)))
        def _():
            for copy in gate_copies(t, up_gates, up_rates):
                copy.start()

    load(0)

    barrier = pltpu.get_barrier_semaphore()
    mirror = sections - 1 - p
    pair = p + 1 - 2 * lax.rem(p, 2)
    peers = [at(pair, c, d), at(mirror, c, d)]
    for k in range(1, spans):
        other = lax.rem(c + k, spans)
        peers += [at(p, other, d), at(mirror, other, d)]
    for k in range(1, copies):
        peers.append(at(p, c, lax.rem(d + k, copies)))
    for peer in peers:
        pl.semaphore_signal(barrier, inc=1, device_id=peer, device_id_type=MESH)

    for level, (inner, outer_size) in enumerate(MASKS):
        maskb[level] = band_mask(inner, outer_size).astype(BF)
    for h in range(HEADS):
        lanes = lax.broadcasted_iota(jnp.int32, (DIM, DIM), 1)
        select[h * DIM : (h + 1) * DIM] = (lanes == HEADS + h).astype(F32).astype(BF)
    token = lax.broadcasted_iota(jnp.int32, (TOK, TOK), 0)
    until = lax.broadcasted_iota(jnp.int32, (TOK, TOK), 1)
    triangle[...] = (token <= until).astype(F32).astype(BF)
    for t in range(2):
        for copy in gate_copies(t, down_gates, down_rates):
            copy.wait()
        rate = jnp.concatenate(
            [jnp.zeros((1, HEADS), F32), rate_in[t], jnp.zeros((1, DIM - 2 * HEADS), F32)], axis=1
        )
        rates[t] = jnp.broadcast_to(rate, (TOK, DIM)).T[0 : 2 * HEADS]

    half = TOK // 2
    before, after = lax.rem(d + copies - 1, copies), lax.rem(d + 1, copies)
    ways = ((0, after),) if copies == 2 else ((0, after), (1, before))

    def cot_own(t, source):
        return pltpu.make_async_copy(source.at[0, 0], cot.at[t, d], ct_own.at[t])

    def cot_copy(t, source, way, to):
        return remote(
            source.at[0, 0], cot.at[t, d], ct_send.at[t, way], ct_recv.at[t, way], at(p, c, to)
        )

    def cot_relay(t, way, to):
        owner = before if way == 0 else after
        part_rows = pl.ds(way * half, half)
        return remote(
            cot.at[t, owner, part_rows], cot.at[t, owner, part_rows], ct_send.at[t, 2 + way],
            ct_recv.at[t, 2 + way], at(p, c, to),
        )

    def start_cot(t, source):
        cot_own(t, source).start()
        for way, to in ways:
            cot_copy(t, source, way, to).start()

    def relay_cots(t):
        for way, to in ways:
            cot_copy(t, down_ct, way, to).wait_recv()
        if copies == 4:
            for way, to in ways:
                cot_relay(t, way, to).start()

    def wait_cots(t):
        cot_own(t, down_ct).wait()
        if copies == 4:
            for way, to in ways:
                cot_relay(t, way, to).wait_recv()

    def start_cots(t):
        @pl.when(is_down(t))
        def _():
            start_cot(t, down_ct)

        @pl.when(jnp.logical_not(is_down(t)))
        def _():
            start_cot(t, up_ct)

    def meet():
        pl.semaphore_wait(barrier, len(peers))
        start_cots(0)

        @pl.when(jnp.logical_not(outer))
        def _():
            start_cots(1)

    outer = (p == 0) | (p == sections - 1)

    @pl.when(jnp.logical_not(outer))
    def _():
        meet()

    def state_copy(t, h):
        return remote(
            sout.at[t, h], sin.at[t, h], s_send.at[t, h], s_recv.at[t, h],
            at(p, lax.rem(c + 1, spans), d),
        )

    def first_copy(t, h):
        return remote(
            bsend.at[t, h], sin.at[t, h], s_send.at[t, h], s_recv.at[t, h],
            at(p, lax.rem(c + 1, spans), d),
        )

    def stage_of(t):
        early = jnp.where(low_half, p, sections - 1 - p)
        return jnp.where(t == 0, early, sections - 1 - early)

    def stream_copy(t, n):
        slot = jnp.where(stage_of(t) == 0, 0, 1)
        to = jnp.clip(jnp.where(is_down(t), p + 1, p - 1), 0, sections - 1)
        return remote(
            ybuf.at[half_of(t), n], xbuf.at[slot, n], x_send.at[t, n], x_recv.at[slot, n], at(to, c, d)
        )

    def half_of(t):
        return jnp.where(is_down(t), 0, 1)

    def piece_rows(piece):
        first, end = (spans * share // HEADS * head for head in PIECES[piece])
        return pl.ds(first, end - first)

    def hidden_own(t, piece):
        rows = piece_rows(piece)
        return pltpu.make_async_copy(
            ht.at[t, d, rows], hg.at[t, d, rows], h_recv.at[t, d, piece]
        )

    def hidden_copy(t, k, piece):
        to = lax.rem(d + k, copies)
        rows = piece_rows(piece)
        return remote(
            ht.at[t, to, rows], hg.at[t, d, rows], h_send.at[t, k - 1, piece],
            h_recv.at[t, d, piece], at(p, c, to),
        )

    def grad_own(t, to):
        return pltpu.make_async_copy(part.at[t, to], gbuf.at[to], g_recv.at[to])

    def grad_copy(t, to):
        slot = c + jnp.where(is_down(t), 0, spans)
        pipe = jnp.where(is_down(t), p, mirror)
        return remote(
            part.at[t, to], gbuf.at[slot], g_send.at[t, to], g_recv.at[slot], at(pipe, to, d)
        )

    def stays(t, to):
        return (c == to) & is_down(t)

    def section(t):
        ones = jnp.ones((COLS, DIM), BF)
        square = jnp.zeros((TOK, DIM), F32)
        square_row = jnp.zeros((2 * HEADS, TOK), F32)
        logits = jnp.zeros((2 * HEADS, TOK), F32)
        for n in range(CH):
            pltpu.make_async_copy(xbuf.at[t, n], xbuf.at[t, n], x_recv.at[t, n]).wait()
            weight_copy(t, n, down_qkv).wait()
            x = xbuf[t, n]
            xf = x.astype(F32)
            x2 = (xf * xf).astype(BF)
            square += mm(x2, ones)
            square_row += mm_nt(ones[0 : 2 * HEADS, 0:DIM], x2[:, 0:DIM])
            square_row += mm_nt(ones[0 : 2 * HEADS, 0:DIM], x2[:, DIM:COLS])
            logits += mm_nt(wg[t, :, n * COLS : (n + 1) * COLS], x)
            for j in range(6):
                block = slice(512 * j, 512 * (j + 1))
                product = mm(x, wqkv[t, n * COLS : (n + 1) * COLS, block])
                if n == 0:
                    proj[:, block] = product
                else:
                    proj[:, block] += product

        power = square * (1.0 / WIDTH) + EPSILON
        scale = lax.rsqrt(square_row * (1.0 / WIDTH) + EPSILON)
        gates = gate_rows(logits * scale, rates[t], triangle[...])


        masks = [maskb[level] for level in range(4)]
        low = maskb[4]
        eye = maskb[0].astype(F32)

        def put(h, qg, z1, z2, kx, fade):
            pmap[h, 0:DIM] = (qg[0:DIM] - z1[:, 0:DIM]).astype(BF)
            pmap[h, DIM:TOK] = (qg[DIM:TOK] - z2[:, 0:DIM]).astype(BF)
            rmap[h, 0:DIM] = z1[:, DIM:TOK]
            rmap[h, DIM:TOK] = z2[:, DIM:TOK]
            mmap[h] = (fade - kx[:, 0:DIM]).astype(BF)
            bmap[h] = kx[:, DIM:TOK]
            bsend[t, h] = kx[:, DIM:TOK].astype(BF)

        floor[...] = head_maps(
            proj, power, gates, select[...], masks, low, eye, put
        )

        @pl.when(t == 0)
        def _():
            load(1)

        @pl.when((t == 0) & outer)
        def _():
            meet()

        @pl.when(c == 0)
        def _():
            for h in range(HEADS):
                first_copy(t, h).start()
                sin[t, h] = jnp.zeros((DIM, DIM), BF)

        def finish_head(h):
            o = obuf[h % 2]
            level = jnp.mean(o * o, axis=-1, keepdims=True)
            o = o * lax.rsqrt(level + floor[:, HEADS + h : HEADS + h + 1])
            o = o.astype(BF)
            hid[:, h * DIM : (h + 1) * DIM] = o
            flipped = o.T
            for u in range(DIM // UNIT):
                row0 = h * DIM + u * UNIT
                span, rest = row0 // column, row0 % column
                to, i = rest // share, rest % share
                ht[t, to, span * share + i : span * share + i + UNIT] = flipped[
                    u * UNIT : (u + 1) * UNIT
                ]

        def send_pieces(h):
            for piece, (_, end) in enumerate(PIECES):
                if h == (end - 1 if spans == HEADS else HEADS - 1):
                    hidden_own(t, piece).start()
                    for k in range(1, copies):
                        hidden_copy(t, k, piece).start()

        for h in range(HEADS):
            @pl.when(c > 0)
            def _():
                state_copy(t, h).wait_recv()

            s = sin[t, h]
            sout[t, h] = (mm(mmap[h], s) + bmap[h]).astype(BF)
            if h < HEADS - 1:
                obuf[h % 2] = mm(pmap[h], s) + rmap[h]
                if h > 0:
                    finish_head(h - 1)

            @pl.when((c > 0) & (c < spans - 1))
            def _():
                state_copy(t, h).start()

            if h == HEADS - 1:
                obuf[h % 2] = mm(pmap[h], s) + rmap[h]
                finish_head(h - 1)

            if h > 0:
                send_pieces(h - 1)
        finish_head(HEADS - 1)
        send_pieces(HEADS - 1)

        out_copy(t, down_wo).wait()
        for n in range(CH):
            block = slice(n * COLS, (n + 1) * COLS)
            y = xbuf[t, n].astype(F32) + mm(hid[...], wo[t, :, block])
            ybuf[half_of(t), n] = y.astype(BF)

            @pl.when(stage_of(t) < sections - 1)
            def _():
                stream_copy(t, n).start()

        @pl.when(t == 0)
        def _():
            relay_cots(0)

            @pl.when(outer)
            def _():
                start_cots(1)

            @pl.when(jnp.logical_not(outer))
            def _():
                relay_cots(1)

    def gradient(t):
        wait_cots(t)
        for piece in range(len(PIECES)):
            rows = piece_rows(piece)
            start, size = rows.start, rows.size
            for j in range(copies):
                pltpu.make_async_copy(
                    hg.at[t, j, rows], hg.at[t, j, rows], h_recv.at[t, j, piece]
                ).wait()
            total = mm(hg[t, 0, start : start + size], cot[t, 0])
            for j in range(1, copies):
                total += mm(hg[t, j, start : start + size], cot[t, j])
            total = total.astype(BF)
            for row0 in range(0, size, UNIT):
                to, at_row = divmod(start + row0, share)
                part[t, to, at_row : at_row + UNIT] = total[row0 : row0 + UNIT]
                if at_row + UNIT == share:
                    @pl.when(stays(t, to))
                    def _():
                        grad_own(t, to).start()

                    @pl.when(jnp.logical_not(stays(t, to)))
                    def _():
                        grad_copy(t, to).start()

    def turn(i, carry):
        middle = jnp.where(outer, 2, 1)
        is_section = (i == 0) | (i == middle)

        @pl.when(is_section)
        def _():
            section(jnp.where(i == 0, 0, 1))

        @pl.when(jnp.logical_not(is_section))
        def _():
            gradient(jnp.where(i == 3, 1, 0))

            @pl.when(outer & (i == 1))
            def _():
                relay_cots(1)

        return carry

    lax.fori_loop(0, 4, turn, 0)

    for j in range(2 * spans):
        pltpu.make_async_copy(gbuf.at[j], gbuf.at[j], g_recv.at[j]).wait()
    total = gbuf[0].astype(F32)
    for j in range(1, 2 * spans):
        total += gbuf[j].astype(F32)
    gsum[0] = total

    for t in range(2):
        for n in range(CH):
            @pl.when(stage_of(t) < sections - 1)
            def _():
                stream_copy(t, n).wait_send()

        @pl.when(c < spans - 1)
        def _():
            for h in range(HEADS):
                state_copy(t, h).wait_send()

        for way, to in ways:
            cot_copy(t, down_ct, way, to).wait_send()
            if copies == 4:
                cot_relay(t, way, to).wait_send()
        for k in range(1, copies):
            for piece in range(len(PIECES)):
                hidden_copy(t, k, piece).wait_send()
        for to in range(spans):
            @pl.when(jnp.logical_not(stays(t, to)))
            def _():
                grad_copy(t, to).wait_send()


def hand_over(acts, grad, down_out, up_out, grad_out, sems):
    moves = [pltpu.make_async_copy(grad, grad_out, sems.at[2 * CH])]
    for i, out in enumerate((down_out, up_out)):
        for n in range(CH):
            to = out.at[0, 0, :, pl.ds(n * COLS, COLS)]
            moves.append(pltpu.make_async_copy(acts.at[i, n], to, sems.at[i * CH + n]))
    for move in moves:
        move.start()
    for move in moves:
        move.wait()


def per_device(dims, *arrays):
    sections, spans, copies = dims
    share = WIDTH // (spans * copies)
    hbm = pl.BlockSpec(memory_space=pl.ANY)
    vmem = pl.BlockSpec(memory_space=pltpu.VMEM)
    dma = pltpu.SemaphoreType.DMA
    acts, grad = pl.pallas_call(
        functools.partial(kernel, dims),
        out_shape=(
            pltpu.VMEM((2, CH, TOK, COLS), BF),
            pltpu.VMEM((1, share, WIDTH), F32),
        ),
        in_specs=[hbm] * 12,
        out_specs=(vmem, vmem),
        scratch_shapes=[
            pltpu.VMEM((2, WIDTH, 3 * WIDTH), BF),
            pltpu.VMEM((2, WIDTH, WIDTH), BF),
            pltpu.VMEM((2, 2 * HEADS, WIDTH), BF),
            pltpu.VMEM((2, 1, HEADS), F32),
            pltpu.VMEM((2, 2 * HEADS, TOK), F32),
            pltpu.VMEM((TOK, TOK), BF),
            pltpu.VMEM((2, CH, TOK, COLS), BF),
            pltpu.VMEM((TOK, 3 * WIDTH), F32),
            pltpu.VMEM((TOK, WIDTH), BF),
            pltpu.VMEM((2, TOK, DIM), F32),
            pltpu.VMEM((len(MASKS), DIM, DIM), BF),
            pltpu.VMEM((WIDTH, DIM), BF),
            pltpu.VMEM((TOK, DIM), F32),
            pltpu.VMEM((HEADS, TOK, DIM), BF),
            pltpu.VMEM((HEADS, TOK, DIM), F32),
            pltpu.VMEM((HEADS, DIM, DIM), BF),
            pltpu.VMEM((HEADS, DIM, DIM), F32),
            pltpu.VMEM((2, HEADS, DIM, DIM), BF),
            pltpu.VMEM((2, HEADS, DIM, DIM), BF),
            pltpu.VMEM((2, HEADS, DIM, DIM), BF),
            pltpu.VMEM((2, copies, TOK, WIDTH), BF),
            pltpu.VMEM((2, copies, spans * share, TOK), BF),
            pltpu.VMEM((2, copies, spans * share, TOK), BF),
            pltpu.VMEM((2, spans, share, WIDTH), BF),
            pltpu.VMEM((2 * spans, share, WIDTH), BF),
            dma((2, 2)),
            dma((2, CH)),
            dma((2,)),
            dma((2, CH)),
            dma((2, CH)),
            dma((2, HEADS)),
            dma((2, HEADS)),
            dma((2, 4)),
            dma((2, 4)),
            dma((2,)),
            dma((2, copies, len(PIECES))),
            dma((2, copies, len(PIECES))),
            dma((2 * spans,)),
            dma((2, spans)),
        ],
        compiler_params=pltpu.CompilerParams(
            collective_id=0, has_side_effects=True, vmem_limit_bytes=60 * 1024 * 1024
        ),
    )(*arrays[:4], *(jnp.swapaxes(gates, 1, 2) for gates in arrays[4:6]), *arrays[6:])
    return pl.pallas_call(
        hand_over,
        out_shape=(
            jax.ShapeDtypeStruct((1, 1, TOK, WIDTH), BF),
            jax.ShapeDtypeStruct((1, 1, TOK, WIDTH), BF),
            jax.ShapeDtypeStruct((1, share, WIDTH), F32),
        ),
        in_specs=[vmem] * 2,
        out_specs=(hbm, hbm, hbm),
        scratch_shapes=[dma((2 * CH + 1,))],
    )(acts, grad)


def solution(mesh):
    dims = (mesh.shape["pipe"], mesh.shape["ctx"], mesh.shape["dp"])
    return jax.shard_map(
        functools.partial(per_device, dims),
        mesh=mesh,
        in_specs=(
            P("dp", "ctx", None),
            P("dp", "ctx", None),
            P("pipe", None, None),
            P("pipe", None, None),
            P("pipe", None, None),
            P("pipe", None, None),
            P("pipe", None),
            P("pipe", None),
            P("pipe", None, None),
            P("pipe", None, None),
            P("pipe", "dp", "ctx", None),
            P("pipe", "dp", "ctx", None),
        ),
        out_specs=(
            P("pipe", "dp", "ctx", None),
            P("pipe", "dp", "ctx", None),
            P("pipe", ("ctx", "dp"), None),
        ),
        check_vma=False,
    )
```

```python
import functools

import jax
import jax.numpy as jnp
from jax import lax
from jax.experimental import pallas as pl
from jax.experimental.pallas import tpu as pltpu
from jax.sharding import PartitionSpec as P

MESH = pl.DeviceIdType.MESH
EPSILON = 1e-06
EXACT = lax.Precision.HIGHEST
BF = jnp.bfloat16
F32 = jnp.float32
HEADS = 8
DIM = 128
TOK = 256
WIDTH = 1024
CH = 4
COLS = WIDTH // CH
UNIT = 32
PIECES = 4
HANDS = 2


def mm(a, b):
    return jnp.dot(a, b, preferred_element_type=F32)


def mm_nt(a, b):
    return lax.dot_general(a, b, (((1,), (1,)), ((), ())), preferred_element_type=F32)


def band_mask(inner, outer):
    row = lax.broadcasted_iota(jnp.int32, (DIM, DIM), 0)
    col = lax.broadcasted_iota(jnp.int32, (DIM, DIM), 1)
    if outer == 1:
        return (row == col).astype(F32)
    if inner == 0:
        return (row >= col).astype(F32)
    same = (row // outer) == (col // outer)
    return (same & ((row // inner) > (col // inner))).astype(F32)


MASKS = ((1, 1), (1, 8), (8, 64), (64, 128), (0, 128))


def eightfold(starts, powers):
    squares = [mm(n, n).astype(BF) for n in powers]
    halves = [t + mm(n, t).astype(BF) for t, n in zip(starts, squares)]
    fourths = [mm(n, n).astype(BF) for n in squares]
    return [t + mm(n, t).astype(BF) for t, n in zip(halves, fourths)]


def block_inverses(parts, masks):
    inner = [a * masks[1] for a in parts]
    results = eightfold([masks[0] - a for a in inner], inner)
    steps = [mm(t, a * masks[2]).astype(BF) for t, a in zip(results, parts)]
    results = [t - mm(n, t).astype(BF) for t, n in zip(results, steps)]
    results = eightfold(results, steps)
    steps = [mm(a * masks[3], t).astype(BF) for t, a in zip(results, parts)]
    results = [t - mm(t, y).astype(BF) for t, y in zip(results, steps)]
    return results


def decay_of(gap):
    return jnp.exp(jnp.minimum(gap, 0.0)).astype(BF)


def lane_of(compact, lane):
    return jnp.broadcast_to(compact[:, lane : lane + 1], (TOK, DIM))


def gate_rows(logits, rates, triangle):
    row = lax.broadcasted_iota(jnp.int32, (2 * HEADS, TOK), 0)
    decay = -rates * (jnp.maximum(logits, 0.0) + jnp.log1p(jnp.exp(-jnp.abs(logits))))
    high = decay.astype(BF)
    rest = decay - high.astype(F32)
    middle = rest.astype(BF)
    low = (rest - middle.astype(F32)).astype(BF)
    sums = mm(jnp.concatenate([high, middle, low], axis=0), triangle)
    total = sums[0:16] + sums[16:32] + sums[32:48]
    return jnp.where(row < HEADS, jax.nn.sigmoid(logits), total)


def head_maps(proj, power, gates, select, masks, low, eye, put):
    first, second = slice(0, DIM), slice(DIM, TOK)
    rstd = lax.rsqrt(power)
    columns = jnp.concatenate([gates, jnp.zeros((DIM - 2 * HEADS, TOK), F32)], axis=0).T
    beta, cum = gates[0:HEADS], gates[HEADS : 2 * HEADS]
    last = jnp.broadcast_to(cum[:, TOK - 1 : TOK], (HEADS, TOK))
    weights = (beta * jnp.exp(last - cum)).astype(BF)
    fades = jnp.exp(last[:, 0:DIM])
    strengths = beta.astype(BF)

    def square_sums(start):
        raw = proj[:, start : start + WIDTH]
        return mm((raw * raw).astype(BF), select)

    nk = rstd * lax.rsqrt(square_sums(WIDTH) * (rstd * rstd) + EPSILON)

    def prepare(h):
        lane = HEADS + h
        q = proj[:, h * DIM : (h + 1) * DIM]
        k = proj[:, WIDTH + h * DIM : WIDTH + (h + 1) * DIM] * lane_of(nk, lane)
        v = proj[:, 2 * WIDTH + h * DIM : 2 * WIDTH + (h + 1) * DIM]
        c = lane_of(columns, lane)
        growth = jnp.exp(c)
        qb, kb = q.astype(BF), k.astype(BF)
        rhs = jnp.concatenate([(k * growth).astype(BF), (v * rstd).astype(BF)], axis=1)
        flipped = kb.T * weights[h : h + 1, :]
        qg = q * growth
        crow, brow = cum[h : h + 1, :], strengths[h : h + 1, :]
        d11 = decay_of(c[first] - crow[:, first]) * brow[:, first]
        d21 = decay_of(c[second] - crow[:, first]) * brow[:, first]
        d22 = decay_of(c[second] - crow[:, second]) * brow[:, second]
        g1 = mm_nt(jnp.concatenate([kb, qb], axis=0), kb[first]).astype(BF)
        g2 = mm_nt(jnp.concatenate([kb[second], qb[second]], axis=0), kb[second]).astype(BF)
        a11 = g1[0:128] * d11
        a21 = g1[128:256] * d21
        s11 = g1[256:384] * (d11 * low)
        s21 = g1[384:512] * d21
        a22 = g2[0:128] * d22
        s22 = g2[128:256] * (d22 * low)
        return h, a11, a22, a21, s11, s21, s22, rhs, flipped, qg

    def complete(state, inverses):
        n = len(state)
        x1 = [mm(inverses[i], state[i][7][first]).astype(BF) for i in range(n)]
        r2 = [state[i][7][second] - mm(state[i][3], x1[i]).astype(BF) for i in range(n)]
        x2 = [mm(inverses[n + i], r2[i]).astype(BF) for i in range(n)]
        for i in range(n):
            h, _, _, _, s11, s21, s22, _, flipped, qg = state[i]
            x = jnp.concatenate([x1[i], x2[i]], axis=0)
            z1 = mm(s11, x1[i])
            z2 = mm(jnp.concatenate([s21, s22], axis=1), x)
            kx = mm(flipped, x)
            put(h, qg, z1, z2, kx, eye * fades[h : h + 1, :])

    state = [prepare(h) for h in range(HEADS)]
    inverses = block_inverses([s[1] for s in state] + [s[2] for s in state], masks)
    complete(state, inverses)
    return (EPSILON * DIM) * (square_sums(0) + EPSILON * power)


def kernel(
    dims,
    down_in, up_in, down_qkv, up_qkv, down_gates, up_gates, down_rates, up_rates,
    down_wo, up_wo, down_ct, up_ct,
    down_out, up_out, grad_out,
    wqkv, wo, wg, rates, triangle, xbuf, ybuf, proj, hid, obuf, maskb, select, floor, pmap, rmap, mmap, bmap, bsend, sin, sout,
    cot, ht, hg, part, gbuf, gsum,
    w_sem, wo_sem, x_recv, x_send, y_sem, s_recv, s_send, ct_recv, ct_send,
    ct_own, h_recv, h_send, g_recv, g_send, go_sem,
):
    sections, spans, copies = dims
    p, c, d = lax.axis_index("pipe"), lax.axis_index("ctx"), lax.axis_index("dp")
    low_half = p < sections // 2
    share = WIDTH // (spans * copies)
    column = WIDTH // spans

    def is_down(t):
        return low_half == (t == 0)

    def at(pipe, ctx, dp):
        return (pipe, ctx, dp)

    def remote(src, dst, send, recv, where):
        return pltpu.make_async_remote_copy(
            src_ref=src, dst_ref=dst, send_sem=send, recv_sem=recv,
            device_id=where, device_id_type=MESH,
        )

    def weight_copy(t, n, qkv):
        rows = pl.ds(n * COLS, COLS)
        return pltpu.make_async_copy(qkv.at[0, rows], wqkv.at[t, rows], w_sem.at[t, n])

    def out_copy(t, out):
        return pltpu.make_async_copy(out.at[0], wo.at[t], wo_sem.at[t])

    def start_weights(t, qkv, out):
        for n in range(CH):
            weight_copy(t, n, qkv).start()
        if t == 1:
            out_copy(t, out).start()

    def input_copy(src, n):
        return pltpu.make_async_copy(
            src.at[0, :, pl.ds(n * COLS, COLS)], xbuf.at[0, n], x_recv.at[0, n]
        )

    @pl.when(p == 0)
    def _():
        for n in range(CH):
            input_copy(down_in, n).start()

    @pl.when(p == sections - 1)
    def _():
        for n in range(CH):
            input_copy(up_in, n).start()

    def load(t):
        @pl.when(is_down(t))
        def _():
            start_weights(t, down_qkv, down_wo)

        @pl.when(jnp.logical_not(is_down(t)))
        def _():
            start_weights(t, up_qkv, up_wo)

    load(0)

    barrier = pltpu.get_barrier_semaphore()
    mirror = sections - 1 - p
    pair = p + 1 - 2 * lax.rem(p, 2)
    peers = [at(pair, c, d), at(mirror, c, d)]
    for k in range(1, spans):
        other = lax.rem(c + k, spans)
        peers += [at(p, other, d), at(mirror, other, d)]
    for k in range(1, copies):
        peers.append(at(p, c, lax.rem(d + k, copies)))
    for peer in peers:
        pl.semaphore_signal(barrier, inc=1, device_id=peer, device_id_type=MESH)

    for level, (inner, outer_size) in enumerate(MASKS):
        maskb[level] = band_mask(inner, outer_size).astype(BF)
    for h in range(HEADS):
        lanes = lax.broadcasted_iota(jnp.int32, (DIM, DIM), 1)
        select[h * DIM : (h + 1) * DIM] = (lanes == HEADS + h).astype(F32).astype(BF)
    for t in range(2):
        wg[t] = jnp.where(is_down(t), down_gates[0], up_gates[0])
        rate = jnp.where(is_down(t), down_rates[...], up_rates[...])
        rate = jnp.concatenate(
            [jnp.zeros((1, HEADS), F32), rate, jnp.zeros((1, DIM - 2 * HEADS), F32)], axis=1
        )
        rate = jnp.broadcast_to(rate, (TOK, DIM)).T
        rates[t] = rate[0 : 2 * HEADS]
    token = lax.broadcasted_iota(jnp.int32, (TOK, TOK), 0)
    until = lax.broadcasted_iota(jnp.int32, (TOK, TOK), 1)
    triangle[...] = (token <= until).astype(F32).astype(BF)

    half = TOK // 2
    before, after = lax.rem(d + copies - 1, copies), lax.rem(d + 1, copies)
    ways = ((0, after),) if copies == 2 else ((0, after), (1, before))

    def cot_own(t, source):
        return pltpu.make_async_copy(source.at[0, 0], cot.at[t, d], ct_own.at[t])

    def cot_copy(t, source, way, to):
        return remote(
            source.at[0, 0], cot.at[t, d], ct_send.at[t, way], ct_recv.at[t, way], at(p, c, to)
        )

    def cot_relay(t, way, to):
        owner = before if way == 0 else after
        part_rows = pl.ds(way * half, half)
        return remote(
            cot.at[t, owner, part_rows], cot.at[t, owner, part_rows], ct_send.at[t, 2 + way],
            ct_recv.at[t, 2 + way], at(p, c, to),
        )

    def start_cot(t, source):
        cot_own(t, source).start()
        for way, to in ways:
            cot_copy(t, source, way, to).start()

    def relay_cots(t):
        for way, to in ways:
            cot_copy(t, down_ct, way, to).wait_recv()
        if copies == 4:
            for way, to in ways:
                cot_relay(t, way, to).start()

    def wait_cots(t):
        cot_own(t, down_ct).wait()
        if copies == 4:
            for way, to in ways:
                cot_relay(t, way, to).wait_recv()

    def start_cots(t):
        @pl.when(is_down(t))
        def _():
            start_cot(t, down_ct)

        @pl.when(jnp.logical_not(is_down(t)))
        def _():
            start_cot(t, up_ct)

    def meet():
        pl.semaphore_wait(barrier, len(peers))
        start_cots(0)

        @pl.when(jnp.logical_not(outer))
        def _():
            start_cots(1)

    outer = (p == 0) | (p == sections - 1)

    @pl.when(jnp.logical_not(outer))
    def _():
        meet()

    def state_copy(t, h):
        return remote(
            sout.at[t, h], sin.at[t, h], s_send.at[t, h], s_recv.at[t, h],
            at(p, lax.rem(c + 1, spans), d),
        )

    def first_copy(t, h):
        return remote(
            bsend.at[t, h], sin.at[t, h], s_send.at[t, h], s_recv.at[t, h],
            at(p, lax.rem(c + 1, spans), d),
        )

    def stage_of(t):
        early = jnp.where(low_half, p, sections - 1 - p)
        return jnp.where(t == 0, early, sections - 1 - early)

    def stream_copy(t, n):
        slot = jnp.where(stage_of(t) == 0, 0, 1)
        to = jnp.clip(jnp.where(is_down(t), p + 1, p - 1), 0, sections - 1)
        return remote(
            ybuf.at[t, n], xbuf.at[slot, n], x_send.at[t, n], x_recv.at[slot, n], at(to, c, d)
        )

    def result_copy(t, n, out):
        return pltpu.make_async_copy(
            ybuf.at[t, n], out.at[0, 0, :, pl.ds(n * COLS, COLS)], y_sem.at[t, n]
        )

    def hidden_own(t, piece):
        rows = pl.ds(piece * (spans * share // PIECES), spans * share // PIECES)
        return pltpu.make_async_copy(
            ht.at[t, d, rows], hg.at[t, d, rows], h_recv.at[t, d, piece]
        )

    def hidden_copy(t, k, piece):
        to = lax.rem(d + k, copies)
        rows = pl.ds(piece * (spans * share // PIECES), spans * share // PIECES)
        return remote(
            ht.at[t, to, rows], hg.at[t, d, rows], h_send.at[t, k - 1, piece],
            h_recv.at[t, d, piece], at(p, c, to),
        )

    def grad_own(t, to):
        return pltpu.make_async_copy(part.at[t, to], gbuf.at[to], g_recv.at[to])

    def grad_copy(t, to):
        slot = c + jnp.where(is_down(t), 0, spans)
        pipe = jnp.where(is_down(t), p, mirror)
        return remote(
            part.at[t, to], gbuf.at[slot], g_send.at[t, to], g_recv.at[slot], at(pipe, to, d)
        )

    def stays(t, to):
        return (c == to) & is_down(t)

    def section(t):
        ones = jnp.ones((COLS, DIM), BF)
        square = jnp.zeros((TOK, DIM), F32)
        square_row = jnp.zeros((2 * HEADS, TOK), F32)
        logits = jnp.zeros((2 * HEADS, TOK), F32)
        for n in range(CH):
            pltpu.make_async_copy(xbuf.at[t, n], xbuf.at[t, n], x_recv.at[t, n]).wait()
            weight_copy(t, n, down_qkv).wait()
            x = xbuf[t, n]
            xf = x.astype(F32)
            x2 = (xf * xf).astype(BF)
            square += mm(x2, ones)
            square_row += mm_nt(ones[0 : 2 * HEADS, 0:DIM], x2[:, 0:DIM])
            square_row += mm_nt(ones[0 : 2 * HEADS, 0:DIM], x2[:, DIM:COLS])
            logits += mm_nt(wg[t, :, n * COLS : (n + 1) * COLS], x)
            for j in range(6):
                block = slice(512 * j, 512 * (j + 1))
                product = mm(x, wqkv[t, n * COLS : (n + 1) * COLS, block])
                if n == 0:
                    proj[:, block] = product
                else:
                    proj[:, block] += product

        power = square * (1.0 / WIDTH) + EPSILON
        scale = lax.rsqrt(square_row * (1.0 / WIDTH) + EPSILON)
        gates = gate_rows(logits * scale, rates[t], triangle[...])


        masks = [maskb[level] for level in range(4)]
        low = maskb[4]
        eye = maskb[0].astype(F32)

        def put(h, qg, z1, z2, kx, fade):
            pmap[h, 0:DIM] = (qg[0:DIM] - z1[:, 0:DIM]).astype(BF)
            pmap[h, DIM:TOK] = (qg[DIM:TOK] - z2[:, 0:DIM]).astype(BF)
            rmap[h, 0:DIM] = z1[:, DIM:TOK]
            rmap[h, DIM:TOK] = z2[:, DIM:TOK]
            mmap[h] = (fade - kx[:, 0:DIM]).astype(BF)
            bmap[h] = kx[:, DIM:TOK]
            bsend[t, h] = kx[:, DIM:TOK].astype(BF)

        floor[...] = head_maps(
            proj, power, gates, select[...], masks, low, eye, put
        )

        @pl.when(t == 0)
        def _():
            @pl.when(low_half)
            def _():
                out_copy(0, down_wo).start()

            @pl.when(jnp.logical_not(low_half))
            def _():
                out_copy(0, up_wo).start()

            load(1)

        @pl.when((t == 0) & outer)
        def _():
            meet()

        @pl.when(c == 0)
        def _():
            for h in range(HEADS):
                first_copy(t, h).start()
                sin[t, h] = jnp.zeros((DIM, DIM), BF)

        def finish_head(h):
            o = obuf[h % 2]
            level = jnp.mean(o * o, axis=-1, keepdims=True)
            o = o * lax.rsqrt(level + floor[:, HEADS + h : HEADS + h + 1])
            o = o.astype(BF)
            hid[:, h * DIM : (h + 1) * DIM] = o
            flipped = o.T
            for u in range(DIM // UNIT):
                row0 = h * DIM + u * UNIT
                span, rest = row0 // column, row0 % column
                to, i = rest // share, rest % share
                ht[t, to, span * share + i : span * share + i + UNIT] = flipped[
                    u * UNIT : (u + 1) * UNIT
                ]

        def send_pieces(h):
            for piece in range(PIECES):
                last = HEADS // PIECES * (piece + 1) - 1 if spans == HEADS else HEADS - 1
                if last == h:
                    hidden_own(t, piece).start()
                    for k in sorted(range(1, copies), key=lambda k: abs(2 * k - copies)):
                        hidden_copy(t, k, piece).start()

        for h in range(HEADS):
            @pl.when(c > 0)
            def _():
                state_copy(t, h).wait_recv()

            s = sin[t, h]
            sout[t, h] = (mm(mmap[h], s) + bmap[h]).astype(BF)
            if h < HEADS - 1:
                obuf[h % 2] = mm(pmap[h], s) + rmap[h]
                if h > 0:
                    finish_head(h - 1)

            @pl.when((c > 0) & (c < spans - 1))
            def _():
                state_copy(t, h).start()

            if h == HEADS - 1:
                obuf[h % 2] = mm(pmap[h], s) + rmap[h]
                finish_head(h - 1)

            if h > 0:
                send_pieces(h - 1)
        finish_head(HEADS - 1)
        send_pieces(HEADS - 1)

        out_copy(t, down_wo).wait()
        for n in range(CH):
            block = slice(n * COLS, (n + 1) * COLS)
            y = xbuf[t, n].astype(F32) + mm(hid[...], wo[t, :, block])
            ybuf[t, n] = y.astype(BF)

            @pl.when(stage_of(t) < sections - 1)
            def _():
                stream_copy(t, n).start()

        @pl.when(is_down(t))
        def _():
            for n in range(CH):
                result_copy(t, n, down_out).start()

        @pl.when(jnp.logical_not(is_down(t)))
        def _():
            for n in range(CH):
                result_copy(t, n, up_out).start()

        @pl.when(t == 0)
        def _():
            relay_cots(0)

            @pl.when(outer)
            def _():
                start_cots(1)

            @pl.when(jnp.logical_not(outer))
            def _():
                relay_cots(1)

    def gradient(t):
        wait_cots(t)
        size = spans * share // PIECES
        for piece in range(PIECES):
            rows = pl.ds(piece * size, size)
            for j in range(copies):
                pltpu.make_async_copy(
                    hg.at[t, j, rows], hg.at[t, j, rows], h_recv.at[t, j, piece]
                ).wait()
            total = mm(hg[t, 0, piece * size : (piece + 1) * size], cot[t, 0])
            for j in range(1, copies):
                total += mm(hg[t, j, piece * size : (piece + 1) * size], cot[t, j])
            total = total.astype(BF)
            for row0 in range(0, size, UNIT):
                to, at_row = divmod(piece * size + row0, share)
                part[t, to, at_row : at_row + UNIT] = total[row0 : row0 + UNIT]
                if at_row + UNIT == share:
                    @pl.when(stays(t, to))
                    def _():
                        grad_own(t, to).start()

                    @pl.when(jnp.logical_not(stays(t, to)))
                    def _():
                        grad_copy(t, to).start()

    def turn(i, carry):
        middle = jnp.where(outer, 2, 1)
        is_section = (i == 0) | (i == middle)

        @pl.when(is_section)
        def _():
            section(jnp.where(i == 0, 0, 1))

        @pl.when(jnp.logical_not(is_section))
        def _():
            gradient(jnp.where(i == 3, 1, 0))

            @pl.when(outer & (i == 1))
            def _():
                relay_cots(1)

        return carry

    lax.fori_loop(0, 4, turn, 0)

    for j in range(2 * spans):
        pltpu.make_async_copy(gbuf.at[j], gbuf.at[j], g_recv.at[j]).wait()
    total = gbuf[0].astype(F32)
    for j in range(1, 2 * spans):
        total += gbuf[j].astype(F32)
    gsum[...] = total
    final = pltpu.make_async_copy(gsum, grad_out.at[0], go_sem)
    final.start()

    for t in range(2):
        for n in range(CH):
            result_copy(t, n, down_out).wait()

            @pl.when(stage_of(t) < sections - 1)
            def _():
                stream_copy(t, n).wait_send()

        @pl.when(c < spans - 1)
        def _():
            for h in range(HEADS):
                state_copy(t, h).wait_send()

        for way, to in ways:
            cot_copy(t, down_ct, way, to).wait_send()
            if copies == 4:
                cot_relay(t, way, to).wait_send()
        for k in range(1, copies):
            for piece in range(PIECES):
                hidden_copy(t, k, piece).wait_send()
        for to in range(spans):
            @pl.when(jnp.logical_not(stays(t, to)))
            def _():
                grad_copy(t, to).wait_send()

    final.wait()


def hand_over(down_in, up_in, grad_in, down_out, up_out, grad_out, acts, grad, in_sems, out_sems):
    rows = TOK // HANDS
    moves = []
    for i, (src, dst) in enumerate(((down_in, down_out), (up_in, up_out))):
        for n in range(HANDS):
            part = (0, 0, pl.ds(n * rows, rows))
            moves.append((src.at[part], acts.at[i, pl.ds(n * rows, rows)], dst.at[part]))
    moves.append((grad_in.at[0], grad, grad_out.at[0]))
    loads, stores = [], []
    for i, (src, here, dst) in enumerate(moves):
        loads.append(pltpu.make_async_copy(src, here, in_sems.at[i]))
        stores.append(pltpu.make_async_copy(here, dst, out_sems.at[i]))
        loads[i].start()
    for load, store in zip(loads, stores):
        load.wait()
        store.start()
    for store in stores:
        store.wait()


def per_device(dims, *arrays):
    sections, spans, copies = dims
    share = WIDTH // (spans * copies)
    hbm = pl.BlockSpec(memory_space=pl.ANY)
    vmem = pl.BlockSpec(memory_space=pltpu.VMEM)
    dma = pltpu.SemaphoreType.DMA
    down_acts, up_acts, grad = pl.pallas_call(
        functools.partial(kernel, dims),
        out_shape=(
            jax.ShapeDtypeStruct((1, 1, TOK, WIDTH), BF),
            jax.ShapeDtypeStruct((1, 1, TOK, WIDTH), BF),
            jax.ShapeDtypeStruct((1, share, WIDTH), F32),
        ),
        in_specs=[hbm] * 4 + [vmem] * 4 + [hbm] * 4,
        out_specs=(hbm, hbm, hbm),
        scratch_shapes=[
            pltpu.VMEM((2, WIDTH, 3 * WIDTH), BF),
            pltpu.VMEM((2, WIDTH, WIDTH), BF),
            pltpu.VMEM((2, 2 * HEADS, WIDTH), BF),
            pltpu.VMEM((2, 2 * HEADS, TOK), F32),
            pltpu.VMEM((TOK, TOK), BF),
            pltpu.VMEM((2, CH, TOK, COLS), BF),
            pltpu.VMEM((2, CH, TOK, COLS), BF),
            pltpu.VMEM((TOK, 3 * WIDTH), F32),
            pltpu.VMEM((TOK, WIDTH), BF),
            pltpu.VMEM((2, TOK, DIM), F32),
            pltpu.VMEM((len(MASKS), DIM, DIM), BF),
            pltpu.VMEM((WIDTH, DIM), BF),
            pltpu.VMEM((TOK, DIM), F32),
            pltpu.VMEM((HEADS, TOK, DIM), BF),
            pltpu.VMEM((HEADS, TOK, DIM), F32),
            pltpu.VMEM((HEADS, DIM, DIM), BF),
            pltpu.VMEM((HEADS, DIM, DIM), F32),
            pltpu.VMEM((2, HEADS, DIM, DIM), BF),
            pltpu.VMEM((2, HEADS, DIM, DIM), BF),
            pltpu.VMEM((2, HEADS, DIM, DIM), BF),
            pltpu.VMEM((2, copies, TOK, WIDTH), BF),
            pltpu.VMEM((2, copies, spans * share, TOK), BF),
            pltpu.VMEM((2, copies, spans * share, TOK), BF),
            pltpu.VMEM((2, spans, share, WIDTH), BF),
            pltpu.VMEM((2 * spans, share, WIDTH), BF),
            pltpu.VMEM((share, WIDTH), F32),
            dma((2, CH)),
            dma((2,)),
            dma((2, CH)),
            dma((2, CH)),
            dma((2, CH)),
            dma((2, HEADS)),
            dma((2, HEADS)),
            dma((2, 4)),
            dma((2, 4)),
            dma((2,)),
            dma((2, copies, PIECES)),
            dma((2, copies, PIECES)),
            dma((2 * spans,)),
            dma((2, spans)),
            dma,
        ],
        compiler_params=pltpu.CompilerParams(
            collective_id=0, has_side_effects=True, vmem_limit_bytes=60 * 1024 * 1024
        ),
    )(*arrays[:4], *(jnp.swapaxes(gates, 1, 2) for gates in arrays[4:6]), *arrays[6:])
    return pl.pallas_call(
        hand_over,
        out_shape=tuple(jax.ShapeDtypeStruct(a.shape, a.dtype) for a in (down_acts, up_acts, grad)),
        in_specs=[hbm] * 3,
        out_specs=(hbm, hbm, hbm),
        scratch_shapes=[
            pltpu.VMEM((2, TOK, WIDTH), BF),
            pltpu.VMEM((share, WIDTH), F32),
            dma((2 * HANDS + 1,)),
            dma((2 * HANDS + 1,)),
        ],
    )(down_acts, up_acts, grad)


def solution(mesh):
    dims = (mesh.shape["pipe"], mesh.shape["ctx"], mesh.shape["dp"])
    return jax.shard_map(
        functools.partial(per_device, dims),
        mesh=mesh,
        in_specs=(
            P("dp", "ctx", None),
            P("dp", "ctx", None),
            P("pipe", None, None),
            P("pipe", None, None),
            P("pipe", None, None),
            P("pipe", None, None),
            P("pipe", None),
            P("pipe", None),
            P("pipe", None, None),
            P("pipe", None, None),
            P("pipe", "dp", "ctx", None),
            P("pipe", "dp", "ctx", None),
        ),
        out_specs=(
            P("pipe", "dp", "ctx", None),
            P("pipe", "dp", "ctx", None),
            P("pipe", ("ctx", "dp"), None),
        ),
        check_vma=False,
    )
```

```python
import functools

import jax
import jax.numpy as jnp
from jax import lax
from jax.experimental import pallas as pl
from jax.experimental.pallas import tpu as pltpu
from jax.sharding import PartitionSpec as P

MESH = pl.DeviceIdType.MESH
EPSILON = 1e-06
EXACT = lax.Precision.HIGHEST
BF = jnp.bfloat16
F32 = jnp.float32
HEADS = 8
DIM = 128
TOK = 256
WIDTH = 1024
CH = 4
COLS = WIDTH // CH
UNIT = 32
PIECES = 4
HANDS = 2


def mm(a, b):
    return jnp.dot(a, b, preferred_element_type=F32)


def mm_nt(a, b):
    return lax.dot_general(a, b, (((1,), (1,)), ((), ())), preferred_element_type=F32)


def band_mask(inner, outer):
    row = lax.broadcasted_iota(jnp.int32, (DIM, DIM), 0)
    col = lax.broadcasted_iota(jnp.int32, (DIM, DIM), 1)
    if outer == 1:
        return (row == col).astype(F32)
    if inner == 0:
        return (row >= col).astype(F32)
    same = (row // outer) == (col // outer)
    return (same & ((row // inner) > (col // inner))).astype(F32)


MASKS = ((1, 1), (1, 8), (8, 64), (64, 128), (0, 128))


def eightfold(starts, powers):
    squares = [mm(n, n).astype(BF) for n in powers]
    halves = [t + mm(n, t).astype(BF) for t, n in zip(starts, squares)]
    fourths = [mm(n, n).astype(BF) for n in squares]
    return [t + mm(n, t).astype(BF) for t, n in zip(halves, fourths)]


def block_inverses(parts, masks):
    inner = [a * masks[1] for a in parts]
    results = eightfold([masks[0] - a for a in inner], inner)
    steps = [mm(t, a * masks[2]).astype(BF) for t, a in zip(results, parts)]
    results = [t - mm(n, t).astype(BF) for t, n in zip(results, steps)]
    results = eightfold(results, steps)
    steps = [mm(a * masks[3], t).astype(BF) for t, a in zip(results, parts)]
    results = [t - mm(t, y).astype(BF) for t, y in zip(results, steps)]
    return results


def decay_of(gap):
    return jnp.exp(jnp.minimum(gap, 0.0)).astype(BF)


def lane_of(compact, lane):
    return jnp.broadcast_to(compact[:, lane : lane + 1], (TOK, DIM))


def gate_rows(logits, rates, triangle):
    row = lax.broadcasted_iota(jnp.int32, (2 * HEADS, TOK), 0)
    decay = -rates * (jnp.maximum(logits, 0.0) + jnp.log1p(jnp.exp(-jnp.abs(logits))))
    high = decay.astype(BF)
    rest = decay - high.astype(F32)
    middle = rest.astype(BF)
    low = (rest - middle.astype(F32)).astype(BF)
    sums = mm(jnp.concatenate([high, middle, low], axis=0), triangle)
    total = sums[0:16] + sums[16:32] + sums[32:48]
    return jnp.where(row < HEADS, jax.nn.sigmoid(logits), total)


def head_maps(proj, power, gates, select, masks, low, eye, put):
    first, second = slice(0, DIM), slice(DIM, TOK)
    rstd = lax.rsqrt(power)
    columns = jnp.concatenate([gates, jnp.zeros((DIM - 2 * HEADS, TOK), F32)], axis=0).T
    beta, cum = gates[0:HEADS], gates[HEADS : 2 * HEADS]
    last = jnp.broadcast_to(cum[:, TOK - 1 : TOK], (HEADS, TOK))
    weights = (beta * jnp.exp(last - cum)).astype(BF)
    fades = jnp.exp(last[:, 0:DIM])
    strengths = beta.astype(BF)

    def square_sums(start):
        raw = proj[:, start : start + WIDTH]
        return mm((raw * raw).astype(BF), select)

    nk = rstd * lax.rsqrt(square_sums(WIDTH) * (rstd * rstd) + EPSILON)

    def prepare(h):
        lane = HEADS + h
        q = proj[:, h * DIM : (h + 1) * DIM]
        k = proj[:, WIDTH + h * DIM : WIDTH + (h + 1) * DIM] * lane_of(nk, lane)
        v = proj[:, 2 * WIDTH + h * DIM : 2 * WIDTH + (h + 1) * DIM]
        c = lane_of(columns, lane)
        growth = jnp.exp(c)
        qb, kb = q.astype(BF), k.astype(BF)
        rhs = jnp.concatenate([(k * growth).astype(BF), (v * rstd).astype(BF)], axis=1)
        flipped = kb.T * weights[h : h + 1, :]
        qg = q * growth
        crow, brow = cum[h : h + 1, :], strengths[h : h + 1, :]
        d11 = decay_of(c[first] - crow[:, first]) * brow[:, first]
        d21 = decay_of(c[second] - crow[:, first]) * brow[:, first]
        d22 = decay_of(c[second] - crow[:, second]) * brow[:, second]
        g1 = mm_nt(jnp.concatenate([kb, qb], axis=0), kb[first]).astype(BF)
        g2 = mm_nt(jnp.concatenate([kb[second], qb[second]], axis=0), kb[second]).astype(BF)
        a11 = g1[0:128] * d11
        a21 = g1[128:256] * d21
        s11 = g1[256:384] * (d11 * low)
        s21 = g1[384:512] * d21
        a22 = g2[0:128] * d22
        s22 = g2[128:256] * (d22 * low)
        return h, a11, a22, a21, s11, s21, s22, rhs, flipped, qg

    def complete(state, inverses):
        n = len(state)
        x1 = [mm(inverses[i], state[i][7][first]).astype(BF) for i in range(n)]
        r2 = [state[i][7][second] - mm(state[i][3], x1[i]).astype(BF) for i in range(n)]
        x2 = [mm(inverses[n + i], r2[i]).astype(BF) for i in range(n)]
        for i in range(n):
            h, _, _, _, s11, s21, s22, _, flipped, qg = state[i]
            x = jnp.concatenate([x1[i], x2[i]], axis=0)
            z1 = mm(s11, x1[i])
            z2 = mm(jnp.concatenate([s21, s22], axis=1), x)
            kx = mm(flipped, x)
            put(h, qg, z1, z2, kx, eye * fades[h : h + 1, :])

    state = [prepare(h) for h in range(HEADS)]
    inverses = block_inverses([s[1] for s in state] + [s[2] for s in state], masks)
    complete(state, inverses)
    return (EPSILON * DIM) * (square_sums(0) + EPSILON * power)


def kernel(
    dims,
    down_in, up_in, down_qkv, up_qkv, down_gates, up_gates, down_rates, up_rates,
    down_wo, up_wo, down_ct, up_ct,
    down_out, up_out, grad_out,
    wqkv, wo, wg, rates, triangle, xbuf, ybuf, proj, hid, obuf, maskb, select, floor, pmap, rmap, mmap, bmap, bsend, sin, sout,
    cot, ht, hg, part, gbuf, gsum,
    w_sem, wo_sem, x_recv, x_send, y_sem, s_recv, s_send, ct_recv, ct_send,
    ct_own, h_recv, h_send, g_recv, g_send, go_sem,
):
    sections, spans, copies = dims
    p, c, d = lax.axis_index("pipe"), lax.axis_index("ctx"), lax.axis_index("dp")
    low_half = p < sections // 2
    share = WIDTH // (spans * copies)
    column = WIDTH // spans

    def is_down(t):
        return low_half == (t == 0)

    def at(pipe, ctx, dp):
        return (pipe, ctx, dp)

    def remote(src, dst, send, recv, where):
        return pltpu.make_async_remote_copy(
            src_ref=src, dst_ref=dst, send_sem=send, recv_sem=recv,
            device_id=where, device_id_type=MESH,
        )

    def weight_copy(t, n, qkv):
        rows = pl.ds(n * COLS, COLS)
        return pltpu.make_async_copy(qkv.at[0, rows], wqkv.at[t, rows], w_sem.at[t, n])

    def out_copy(t, out):
        return pltpu.make_async_copy(out.at[0], wo.at[t], wo_sem.at[t])

    def start_weights(t, qkv, out):
        for n in range(CH):
            weight_copy(t, n, qkv).start()
        if t == 1:
            out_copy(t, out).start()

    def input_copy(src, n):
        return pltpu.make_async_copy(
            src.at[0, :, pl.ds(n * COLS, COLS)], xbuf.at[0, n], x_recv.at[0, n]
        )

    @pl.when(p == 0)
    def _():
        for n in range(CH):
            input_copy(down_in, n).start()

    @pl.when(p == sections - 1)
    def _():
        for n in range(CH):
            input_copy(up_in, n).start()

    def load(t):
        @pl.when(is_down(t))
        def _():
            start_weights(t, down_qkv, down_wo)

        @pl.when(jnp.logical_not(is_down(t)))
        def _():
            start_weights(t, up_qkv, up_wo)

    load(0)

    barrier = pltpu.get_barrier_semaphore()
    mirror = sections - 1 - p
    pair = p + 1 - 2 * lax.rem(p, 2)
    peers = [at(pair, c, d), at(mirror, c, d)]
    for k in range(1, spans):
        other = lax.rem(c + k, spans)
        peers += [at(p, other, d), at(mirror, other, d)]
    for k in range(1, copies):
        peers.append(at(p, c, lax.rem(d + k, copies)))
    for peer in peers:
        pl.semaphore_signal(barrier, inc=1, device_id=peer, device_id_type=MESH)

    for level, (inner, outer_size) in enumerate(MASKS):
        maskb[level] = band_mask(inner, outer_size).astype(BF)
    for h in range(HEADS):
        lanes = lax.broadcasted_iota(jnp.int32, (DIM, DIM), 1)
        select[h * DIM : (h + 1) * DIM] = (lanes == HEADS + h).astype(F32).astype(BF)
    for t in range(2):
        wg[t] = jnp.where(is_down(t), down_gates[0], up_gates[0])
        rate = jnp.where(is_down(t), down_rates[...], up_rates[...])
        rate = jnp.concatenate(
            [jnp.zeros((1, HEADS), F32), rate, jnp.zeros((1, DIM - 2 * HEADS), F32)], axis=1
        )
        rate = jnp.broadcast_to(rate, (TOK, DIM)).T
        rates[t] = rate[0 : 2 * HEADS]
    token = lax.broadcasted_iota(jnp.int32, (TOK, TOK), 0)
    until = lax.broadcasted_iota(jnp.int32, (TOK, TOK), 1)
    triangle[...] = (token <= until).astype(F32).astype(BF)

    half = TOK // 2
    before, after = lax.rem(d + copies - 1, copies), lax.rem(d + 1, copies)
    ways = ((0, after),) if copies == 2 else ((0, after), (1, before))

    def cot_own(t, source):
        return pltpu.make_async_copy(source.at[0, 0], cot.at[t, d], ct_own.at[t])

    def cot_copy(t, source, way, to):
        return remote(
            source.at[0, 0], cot.at[t, d], ct_send.at[t, way], ct_recv.at[t, way], at(p, c, to)
        )

    def cot_relay(t, way, to):
        owner = before if way == 0 else after
        part_rows = pl.ds(way * half, half)
        return remote(
            cot.at[t, owner, part_rows], cot.at[t, owner, part_rows], ct_send.at[t, 2 + way],
            ct_recv.at[t, 2 + way], at(p, c, to),
        )

    def start_cot(t, source):
        cot_own(t, source).start()
        for way, to in ways:
            cot_copy(t, source, way, to).start()

    def relay_cots(t):
        for way, to in ways:
            cot_copy(t, down_ct, way, to).wait_recv()
        if copies == 4:
            for way, to in ways:
                cot_relay(t, way, to).start()

    def wait_cots(t):
        cot_own(t, down_ct).wait()
        if copies == 4:
            for way, to in ways:
                cot_relay(t, way, to).wait_recv()

    def start_cots(t):
        @pl.when(is_down(t))
        def _():
            start_cot(t, down_ct)

        @pl.when(jnp.logical_not(is_down(t)))
        def _():
            start_cot(t, up_ct)

    def meet():
        pl.semaphore_wait(barrier, len(peers))
        start_cots(0)

        @pl.when(jnp.logical_not(outer))
        def _():
            start_cots(1)

    outer = (p == 0) | (p == sections - 1)

    @pl.when(jnp.logical_not(outer))
    def _():
        meet()

    def state_copy(t, h):
        return remote(
            sout.at[t, h], sin.at[t, h], s_send.at[t, h], s_recv.at[t, h],
            at(p, lax.rem(c + 1, spans), d),
        )

    def first_copy(t, h):
        return remote(
            bsend.at[t, h], sin.at[t, h], s_send.at[t, h], s_recv.at[t, h],
            at(p, lax.rem(c + 1, spans), d),
        )

    def stage_of(t):
        early = jnp.where(low_half, p, sections - 1 - p)
        return jnp.where(t == 0, early, sections - 1 - early)

    def stream_copy(t, n):
        slot = jnp.where(stage_of(t) == 0, 0, 1)
        to = jnp.clip(jnp.where(is_down(t), p + 1, p - 1), 0, sections - 1)
        return remote(
            ybuf.at[t, n], xbuf.at[slot, n], x_send.at[t, n], x_recv.at[slot, n], at(to, c, d)
        )

    def result_copy(t, n, out):
        return pltpu.make_async_copy(
            ybuf.at[t, n], out.at[0, 0, :, pl.ds(n * COLS, COLS)], y_sem.at[t, n]
        )

    def hidden_own(t, piece):
        rows = pl.ds(piece * (spans * share // PIECES), spans * share // PIECES)
        return pltpu.make_async_copy(
            ht.at[t, d, rows], hg.at[t, d, rows], h_recv.at[t, d, piece]
        )

    def hidden_copy(t, k, piece):
        to = lax.rem(d + k, copies)
        rows = pl.ds(piece * (spans * share // PIECES), spans * share // PIECES)
        return remote(
            ht.at[t, to, rows], hg.at[t, d, rows], h_send.at[t, k - 1, piece],
            h_recv.at[t, d, piece], at(p, c, to),
        )

    def grad_own(t, to):
        return pltpu.make_async_copy(part.at[t, to], gbuf.at[to], g_recv.at[to])

    def grad_copy(t, to):
        slot = c + jnp.where(is_down(t), 0, spans)
        pipe = jnp.where(is_down(t), p, mirror)
        return remote(
            part.at[t, to], gbuf.at[slot], g_send.at[t, to], g_recv.at[slot], at(pipe, to, d)
        )

    def stays(t, to):
        return (c == to) & is_down(t)

    def section(t):
        ones = jnp.ones((COLS, DIM), BF)
        square = jnp.zeros((TOK, DIM), F32)
        square_row = jnp.zeros((2 * HEADS, TOK), F32)
        logits = jnp.zeros((2 * HEADS, TOK), F32)
        for n in range(CH):
            pltpu.make_async_copy(xbuf.at[t, n], xbuf.at[t, n], x_recv.at[t, n]).wait()
            weight_copy(t, n, down_qkv).wait()
            if n == CH - 1:
                @pl.when((t == 0) & low_half)
                def _():
                    out_copy(0, down_wo).start()

                @pl.when((t == 0) & jnp.logical_not(low_half))
                def _():
                    out_copy(0, up_wo).start()

            x = xbuf[t, n]
            xf = x.astype(F32)
            x2 = (xf * xf).astype(BF)
            square += mm(x2, ones)
            square_row += mm_nt(ones[0 : 2 * HEADS, 0:DIM], x2[:, 0:DIM])
            square_row += mm_nt(ones[0 : 2 * HEADS, 0:DIM], x2[:, DIM:COLS])
            logits += mm_nt(wg[t, :, n * COLS : (n + 1) * COLS], x)
            for j in range(6):
                block = slice(512 * j, 512 * (j + 1))
                product = mm(x, wqkv[t, n * COLS : (n + 1) * COLS, block])
                if n == 0:
                    proj[:, block] = product
                else:
                    proj[:, block] += product

        power = square * (1.0 / WIDTH) + EPSILON
        scale = lax.rsqrt(square_row * (1.0 / WIDTH) + EPSILON)
        gates = gate_rows(logits * scale, rates[t], triangle[...])


        masks = [maskb[level] for level in range(4)]
        low = maskb[4]
        eye = maskb[0].astype(F32)

        def put(h, qg, z1, z2, kx, fade):
            pmap[h, 0:DIM] = (qg[0:DIM] - z1[:, 0:DIM]).astype(BF)
            pmap[h, DIM:TOK] = (qg[DIM:TOK] - z2[:, 0:DIM]).astype(BF)
            rmap[h, 0:DIM] = z1[:, DIM:TOK]
            rmap[h, DIM:TOK] = z2[:, DIM:TOK]
            mmap[h] = (fade - kx[:, 0:DIM]).astype(BF)
            bmap[h] = kx[:, DIM:TOK]
            bsend[t, h] = kx[:, DIM:TOK].astype(BF)

        floor[...] = head_maps(
            proj, power, gates, select[...], masks, low, eye, put
        )

        @pl.when(t == 0)
        def _():
            load(1)

        @pl.when((t == 0) & outer)
        def _():
            meet()

        @pl.when(c == 0)
        def _():
            for h in range(HEADS):
                first_copy(t, h).start()
                sin[t, h] = jnp.zeros((DIM, DIM), BF)

        def finish_head(h):
            o = obuf[h % 2]
            level = jnp.mean(o * o, axis=-1, keepdims=True)
            o = o * lax.rsqrt(level + floor[:, HEADS + h : HEADS + h + 1])
            o = o.astype(BF)
            hid[:, h * DIM : (h + 1) * DIM] = o
            flipped = o.T
            for u in range(DIM // UNIT):
                row0 = h * DIM + u * UNIT
                span, rest = row0 // column, row0 % column
                to, i = rest // share, rest % share
                ht[t, to, span * share + i : span * share + i + UNIT] = flipped[
                    u * UNIT : (u + 1) * UNIT
                ]

        def send_pieces(h):
            for piece in range(PIECES):
                last = HEADS // PIECES * (piece + 1) - 1 if spans == HEADS else HEADS - 1
                if last == h:
                    hidden_own(t, piece).start()
                    for k in sorted(range(1, copies), key=lambda k: abs(2 * k - copies)):
                        hidden_copy(t, k, piece).start()

        for h in range(HEADS):
            @pl.when(c > 0)
            def _():
                state_copy(t, h).wait_recv()

            s = sin[t, h]
            sout[t, h] = (mm(mmap[h], s) + bmap[h]).astype(BF)
            if h < HEADS - 1:
                obuf[h % 2] = mm(pmap[h], s) + rmap[h]
                if h > 0:
                    finish_head(h - 1)

            @pl.when((c > 0) & (c < spans - 1))
            def _():
                state_copy(t, h).start()

            if h == HEADS - 1:
                obuf[h % 2] = mm(pmap[h], s) + rmap[h]
                finish_head(h - 1)

            if h > 0:
                send_pieces(h - 1)
        finish_head(HEADS - 1)
        send_pieces(HEADS - 1)

        out_copy(t, down_wo).wait()
        for n in range(CH):
            block = slice(n * COLS, (n + 1) * COLS)
            y = xbuf[t, n].astype(F32) + mm(hid[...], wo[t, :, block])
            ybuf[t, n] = y.astype(BF)

            @pl.when(stage_of(t) < sections - 1)
            def _():
                stream_copy(t, n).start()

        @pl.when(is_down(t))
        def _():
            for n in range(CH):
                result_copy(t, n, down_out).start()

        @pl.when(jnp.logical_not(is_down(t)))
        def _():
            for n in range(CH):
                result_copy(t, n, up_out).start()

        @pl.when(t == 0)
        def _():
            relay_cots(0)

            @pl.when(outer)
            def _():
                start_cots(1)

            @pl.when(jnp.logical_not(outer))
            def _():
                relay_cots(1)

    def gradient(t):
        wait_cots(t)
        size = spans * share // PIECES
        for piece in range(PIECES):
            rows = pl.ds(piece * size, size)
            for j in range(copies):
                pltpu.make_async_copy(
                    hg.at[t, j, rows], hg.at[t, j, rows], h_recv.at[t, j, piece]
                ).wait()
            total = mm(hg[t, 0, piece * size : (piece + 1) * size], cot[t, 0])
            for j in range(1, copies):
                total += mm(hg[t, j, piece * size : (piece + 1) * size], cot[t, j])
            total = total.astype(BF)
            for row0 in range(0, size, UNIT):
                to, at_row = divmod(piece * size + row0, share)
                part[t, to, at_row : at_row + UNIT] = total[row0 : row0 + UNIT]
                if at_row + UNIT == share:
                    @pl.when(stays(t, to))
                    def _():
                        grad_own(t, to).start()

                    @pl.when(jnp.logical_not(stays(t, to)))
                    def _():
                        grad_copy(t, to).start()

    def turn(i, carry):
        middle = jnp.where(outer, 2, 1)
        is_section = (i == 0) | (i == middle)

        @pl.when(is_section)
        def _():
            section(jnp.where(i == 0, 0, 1))

        @pl.when(jnp.logical_not(is_section))
        def _():
            gradient(jnp.where(i == 3, 1, 0))

            @pl.when(outer & (i == 1))
            def _():
                relay_cots(1)

        return carry

    lax.fori_loop(0, 4, turn, 0)

    for j in range(2 * spans):
        pltpu.make_async_copy(gbuf.at[j], gbuf.at[j], g_recv.at[j]).wait()
    total = gbuf[0].astype(F32)
    for j in range(1, 2 * spans):
        total += gbuf[j].astype(F32)
    gsum[...] = total
    final = pltpu.make_async_copy(gsum, grad_out.at[0], go_sem)
    final.start()

    for t in range(2):
        for n in range(CH):
            result_copy(t, n, down_out).wait()

            @pl.when(stage_of(t) < sections - 1)
            def _():
                stream_copy(t, n).wait_send()

        @pl.when(c < spans - 1)
        def _():
            for h in range(HEADS):
                state_copy(t, h).wait_send()

        for way, to in ways:
            cot_copy(t, down_ct, way, to).wait_send()
            if copies == 4:
                cot_relay(t, way, to).wait_send()
        for k in range(1, copies):
            for piece in range(PIECES):
                hidden_copy(t, k, piece).wait_send()
        for to in range(spans):
            @pl.when(jnp.logical_not(stays(t, to)))
            def _():
                grad_copy(t, to).wait_send()

    final.wait()


def hand_over(down_in, up_in, grad_in, down_out, up_out, grad_out, acts, grad, in_sems, out_sems):
    rows = TOK // HANDS
    moves = []
    for i, (src, dst) in enumerate(((down_in, down_out), (up_in, up_out))):
        for n in range(HANDS):
            part = (0, 0, pl.ds(n * rows, rows))
            moves.append((src.at[part], acts.at[i, pl.ds(n * rows, rows)], dst.at[part]))
    moves.append((grad_in.at[0], grad, grad_out.at[0]))
    loads, stores = [], []
    for i, (src, here, dst) in enumerate(moves):
        loads.append(pltpu.make_async_copy(src, here, in_sems.at[i]))
        stores.append(pltpu.make_async_copy(here, dst, out_sems.at[i]))
        loads[i].start()
    for load, store in zip(loads, stores):
        load.wait()
        store.start()
    for store in stores:
        store.wait()


def per_device(dims, *arrays):
    sections, spans, copies = dims
    share = WIDTH // (spans * copies)
    hbm = pl.BlockSpec(memory_space=pl.ANY)
    vmem = pl.BlockSpec(memory_space=pltpu.VMEM)
    dma = pltpu.SemaphoreType.DMA
    down_acts, up_acts, grad = pl.pallas_call(
        functools.partial(kernel, dims),
        out_shape=(
            jax.ShapeDtypeStruct((1, 1, TOK, WIDTH), BF),
            jax.ShapeDtypeStruct((1, 1, TOK, WIDTH), BF),
            jax.ShapeDtypeStruct((1, share, WIDTH), F32),
        ),
        in_specs=[hbm] * 4 + [vmem] * 4 + [hbm] * 4,
        out_specs=(hbm, hbm, hbm),
        scratch_shapes=[
            pltpu.VMEM((2, WIDTH, 3 * WIDTH), BF),
            pltpu.VMEM((2, WIDTH, WIDTH), BF),
            pltpu.VMEM((2, 2 * HEADS, WIDTH), BF),
            pltpu.VMEM((2, 2 * HEADS, TOK), F32),
            pltpu.VMEM((TOK, TOK), BF),
            pltpu.VMEM((2, CH, TOK, COLS), BF),
            pltpu.VMEM((2, CH, TOK, COLS), BF),
            pltpu.VMEM((TOK, 3 * WIDTH), F32),
            pltpu.VMEM((TOK, WIDTH), BF),
            pltpu.VMEM((2, TOK, DIM), F32),
            pltpu.VMEM((len(MASKS), DIM, DIM), BF),
            pltpu.VMEM((WIDTH, DIM), BF),
            pltpu.VMEM((TOK, DIM), F32),
            pltpu.VMEM((HEADS, TOK, DIM), BF),
            pltpu.VMEM((HEADS, TOK, DIM), F32),
            pltpu.VMEM((HEADS, DIM, DIM), BF),
            pltpu.VMEM((HEADS, DIM, DIM), F32),
            pltpu.VMEM((2, HEADS, DIM, DIM), BF),
            pltpu.VMEM((2, HEADS, DIM, DIM), BF),
            pltpu.VMEM((2, HEADS, DIM, DIM), BF),
            pltpu.VMEM((2, copies, TOK, WIDTH), BF),
            pltpu.VMEM((2, copies, spans * share, TOK), BF),
            pltpu.VMEM((2, copies, spans * share, TOK), BF),
            pltpu.VMEM((2, spans, share, WIDTH), BF),
            pltpu.VMEM((2 * spans, share, WIDTH), BF),
            pltpu.VMEM((share, WIDTH), F32),
            dma((2, CH)),
            dma((2,)),
            dma((2, CH)),
            dma((2, CH)),
            dma((2, CH)),
            dma((2, HEADS)),
            dma((2, HEADS)),
            dma((2, 4)),
            dma((2, 4)),
            dma((2,)),
            dma((2, copies, PIECES)),
            dma((2, copies, PIECES)),
            dma((2 * spans,)),
            dma((2, spans)),
            dma,
        ],
        compiler_params=pltpu.CompilerParams(
            collective_id=0, has_side_effects=True, vmem_limit_bytes=60 * 1024 * 1024
        ),
    )(*arrays[:4], *(jnp.swapaxes(gates, 1, 2) for gates in arrays[4:6]), *arrays[6:])
    return pl.pallas_call(
        hand_over,
        out_shape=tuple(jax.ShapeDtypeStruct(a.shape, a.dtype) for a in (down_acts, up_acts, grad)),
        in_specs=[hbm] * 3,
        out_specs=(hbm, hbm, hbm),
        scratch_shapes=[
            pltpu.VMEM((2, TOK, WIDTH), BF),
            pltpu.VMEM((share, WIDTH), F32),
            dma((2 * HANDS + 1,)),
            dma((2 * HANDS + 1,)),
        ],
    )(down_acts, up_acts, grad)


def solution(mesh):
    dims = (mesh.shape["pipe"], mesh.shape["ctx"], mesh.shape["dp"])
    return jax.shard_map(
        functools.partial(per_device, dims),
        mesh=mesh,
        in_specs=(
            P("dp", "ctx", None),
            P("dp", "ctx", None),
            P("pipe", None, None),
            P("pipe", None, None),
            P("pipe", None, None),
            P("pipe", None, None),
            P("pipe", None),
            P("pipe", None),
            P("pipe", None, None),
            P("pipe", None, None),
            P("pipe", "dp", "ctx", None),
            P("pipe", "dp", "ctx", None),
        ),
        out_specs=(
            P("pipe", "dp", "ctx", None),
            P("pipe", "dp", "ctx", None),
            P("pipe", ("ctx", "dp"), None),
        ),
        check_vma=False,
    )
```

```python
import functools

import jax
import jax.numpy as jnp
from jax import lax
from jax.experimental import pallas as pl
from jax.experimental.pallas import tpu as pltpu
from jax.sharding import PartitionSpec as P

MESH = pl.DeviceIdType.MESH
EPSILON = 1e-06
EXACT = lax.Precision.HIGHEST
BF = jnp.bfloat16
F32 = jnp.float32
HEADS = 8
DIM = 128
TOK = 256
WIDTH = 1024
CH = 4
COLS = WIDTH // CH
UNIT = 32
PIECES = 4
HANDS = 4


def mm(a, b):
    return jnp.dot(a, b, preferred_element_type=F32)


def mm_nt(a, b):
    return lax.dot_general(a, b, (((1,), (1,)), ((), ())), preferred_element_type=F32)


def band_mask(inner, outer):
    row = lax.broadcasted_iota(jnp.int32, (DIM, DIM), 0)
    col = lax.broadcasted_iota(jnp.int32, (DIM, DIM), 1)
    if outer == 1:
        return (row == col).astype(F32)
    if inner == 0:
        return (row >= col).astype(F32)
    same = (row // outer) == (col // outer)
    return (same & ((row // inner) > (col // inner))).astype(F32)


MASKS = ((1, 1), (1, 8), (8, 64), (64, 128), (0, 128))


def eightfold(starts, powers):
    squares = [mm(n, n).astype(BF) for n in powers]
    halves = [t + mm(n, t).astype(BF) for t, n in zip(starts, squares)]
    fourths = [mm(n, n).astype(BF) for n in squares]
    return [t + mm(n, t).astype(BF) for t, n in zip(halves, fourths)]


def block_inverses(parts, masks):
    inner = [a * masks[1] for a in parts]
    results = eightfold([masks[0] - a for a in inner], inner)
    steps = [mm(t, a * masks[2]).astype(BF) for t, a in zip(results, parts)]
    results = [t - mm(n, t).astype(BF) for t, n in zip(results, steps)]
    results = eightfold(results, steps)
    steps = [mm(a * masks[3], t).astype(BF) for t, a in zip(results, parts)]
    results = [t - mm(t, y).astype(BF) for t, y in zip(results, steps)]
    return results


def decay_of(gap):
    return jnp.exp(jnp.minimum(gap, 0.0)).astype(BF)


def lane_of(compact, lane):
    return jnp.broadcast_to(compact[:, lane : lane + 1], (TOK, DIM))


def gate_rows(logits, rates, triangle):
    row = lax.broadcasted_iota(jnp.int32, (2 * HEADS, TOK), 0)
    decay = -rates * (jnp.maximum(logits, 0.0) + jnp.log1p(jnp.exp(-jnp.abs(logits))))
    high = decay.astype(BF)
    rest = decay - high.astype(F32)
    middle = rest.astype(BF)
    low = (rest - middle.astype(F32)).astype(BF)
    sums = mm(jnp.concatenate([high, middle, low], axis=0), triangle)
    total = sums[0:16] + sums[16:32] + sums[32:48]
    return jnp.where(row < HEADS, jax.nn.sigmoid(logits), total)


def head_maps(proj, power, gates, select, masks, low, eye, put):
    first, second = slice(0, DIM), slice(DIM, TOK)
    rstd = lax.rsqrt(power)
    columns = jnp.concatenate([gates, jnp.zeros((DIM - 2 * HEADS, TOK), F32)], axis=0).T
    beta, cum = gates[0:HEADS], gates[HEADS : 2 * HEADS]
    last = jnp.broadcast_to(cum[:, TOK - 1 : TOK], (HEADS, TOK))
    weights = (beta * jnp.exp(last - cum)).astype(BF)
    fades = jnp.exp(last[:, 0:DIM])
    strengths = beta.astype(BF)

    def square_sums(start):
        raw = proj[:, start : start + WIDTH]
        return mm((raw * raw).astype(BF), select)

    nk = rstd * lax.rsqrt(square_sums(WIDTH) * (rstd * rstd) + EPSILON)

    def prepare(h):
        lane = HEADS + h
        q = proj[:, h * DIM : (h + 1) * DIM]
        k = proj[:, WIDTH + h * DIM : WIDTH + (h + 1) * DIM] * lane_of(nk, lane)
        v = proj[:, 2 * WIDTH + h * DIM : 2 * WIDTH + (h + 1) * DIM]
        c = lane_of(columns, lane)
        growth = jnp.exp(c)
        qb, kb = q.astype(BF), k.astype(BF)
        rhs = jnp.concatenate([(k * growth).astype(BF), (v * rstd).astype(BF)], axis=1)
        flipped = kb.T * weights[h : h + 1, :]
        qg = q * growth
        crow, brow = cum[h : h + 1, :], strengths[h : h + 1, :]
        d11 = decay_of(c[first] - crow[:, first]) * brow[:, first]
        d21 = decay_of(c[second] - crow[:, first]) * brow[:, first]
        d22 = decay_of(c[second] - crow[:, second]) * brow[:, second]
        g1 = mm_nt(jnp.concatenate([kb, qb], axis=0), kb[first]).astype(BF)
        g2 = mm_nt(jnp.concatenate([kb[second], qb[second]], axis=0), kb[second]).astype(BF)
        a11 = g1[0:128] * d11
        a21 = g1[128:256] * d21
        s11 = g1[256:384] * (d11 * low)
        s21 = g1[384:512] * d21
        a22 = g2[0:128] * d22
        s22 = g2[128:256] * (d22 * low)
        return h, a11, a22, a21, s11, s21, s22, rhs, flipped, qg

    def complete(state, inverses):
        n = len(state)
        x1 = [mm(inverses[i], state[i][7][first]).astype(BF) for i in range(n)]
        r2 = [state[i][7][second] - mm(state[i][3], x1[i]).astype(BF) for i in range(n)]
        x2 = [mm(inverses[n + i], r2[i]).astype(BF) for i in range(n)]
        for i in range(n):
            h, _, _, _, s11, s21, s22, _, flipped, qg = state[i]
            x = jnp.concatenate([x1[i], x2[i]], axis=0)
            z1 = mm(s11, x1[i])
            z2 = mm(jnp.concatenate([s21, s22], axis=1), x)
            kx = mm(flipped, x)
            put(h, qg, z1, z2, kx, eye * fades[h : h + 1, :])

    state = [prepare(h) for h in range(HEADS)]
    inverses = block_inverses([s[1] for s in state] + [s[2] for s in state], masks)
    complete(state, inverses)
    return (EPSILON * DIM) * (square_sums(0) + EPSILON * power)


def kernel(
    dims,
    down_in, up_in, down_qkv, up_qkv, down_gates, up_gates, down_rates, up_rates,
    down_wo, up_wo, down_ct, up_ct,
    down_out, up_out, grad_out,
    wqkv, wo, wg, rates, triangle, xbuf, ybuf, proj, hid, obuf, maskb, select, floor, pmap, rmap, mmap, bmap, bsend, sin, sout,
    cot, ht, hg, part, gbuf, gsum,
    w_sem, wo_sem, x_recv, x_send, y_sem, s_recv, s_send, ct_recv, ct_send,
    ct_own, h_recv, h_send, g_recv, g_send, go_sem,
):
    sections, spans, copies = dims
    p, c, d = lax.axis_index("pipe"), lax.axis_index("ctx"), lax.axis_index("dp")
    low_half = p < sections // 2
    share = WIDTH // (spans * copies)
    column = WIDTH // spans

    def is_down(t):
        return low_half == (t == 0)

    def at(pipe, ctx, dp):
        return (pipe, ctx, dp)

    def remote(src, dst, send, recv, where):
        return pltpu.make_async_remote_copy(
            src_ref=src, dst_ref=dst, send_sem=send, recv_sem=recv,
            device_id=where, device_id_type=MESH,
        )

    def weight_copy(t, n, qkv):
        rows = pl.ds(n * COLS, COLS)
        return pltpu.make_async_copy(qkv.at[0, rows], wqkv.at[t, rows], w_sem.at[t, n])

    def out_copy(t, out):
        return pltpu.make_async_copy(out.at[0], wo.at[t], wo_sem.at[t])

    def start_weights(t, qkv, out):
        for n in range(CH):
            weight_copy(t, n, qkv).start()
        if t == 1:
            out_copy(t, out).start()

    def input_copy(src, n):
        return pltpu.make_async_copy(
            src.at[0, :, pl.ds(n * COLS, COLS)], xbuf.at[0, n], x_recv.at[0, n]
        )

    @pl.when(p == 0)
    def _():
        for n in range(CH):
            input_copy(down_in, n).start()

    @pl.when(p == sections - 1)
    def _():
        for n in range(CH):
            input_copy(up_in, n).start()

    def load(t):
        @pl.when(is_down(t))
        def _():
            start_weights(t, down_qkv, down_wo)

        @pl.when(jnp.logical_not(is_down(t)))
        def _():
            start_weights(t, up_qkv, up_wo)

    load(0)

    barrier = pltpu.get_barrier_semaphore()
    mirror = sections - 1 - p
    pair = p + 1 - 2 * lax.rem(p, 2)
    peers = [at(pair, c, d), at(mirror, c, d)]
    for k in range(1, spans):
        other = lax.rem(c + k, spans)
        peers += [at(p, other, d), at(mirror, other, d)]
    for k in range(1, copies):
        peers.append(at(p, c, lax.rem(d + k, copies)))
    for peer in peers:
        pl.semaphore_signal(barrier, inc=1, device_id=peer, device_id_type=MESH)

    for level, (inner, outer_size) in enumerate(MASKS):
        maskb[level] = band_mask(inner, outer_size).astype(BF)
    for h in range(HEADS):
        lanes = lax.broadcasted_iota(jnp.int32, (DIM, DIM), 1)
        select[h * DIM : (h + 1) * DIM] = (lanes == HEADS + h).astype(F32).astype(BF)
    for t in range(2):
        wg[t] = jnp.where(is_down(t), down_gates[0], up_gates[0])
        rate = jnp.where(is_down(t), down_rates[...], up_rates[...])
        rate = jnp.concatenate(
            [jnp.zeros((1, HEADS), F32), rate, jnp.zeros((1, DIM - 2 * HEADS), F32)], axis=1
        )
        rate = jnp.broadcast_to(rate, (TOK, DIM)).T
        rates[t] = rate[0 : 2 * HEADS]
    token = lax.broadcasted_iota(jnp.int32, (TOK, TOK), 0)
    until = lax.broadcasted_iota(jnp.int32, (TOK, TOK), 1)
    triangle[...] = (token <= until).astype(F32).astype(BF)

    half = TOK // 2
    before, after = lax.rem(d + copies - 1, copies), lax.rem(d + 1, copies)
    ways = ((0, after),) if copies == 2 else ((0, after), (1, before))

    def cot_own(t, source):
        return pltpu.make_async_copy(source.at[0, 0], cot.at[t, d], ct_own.at[t])

    def cot_copy(t, source, way, to):
        return remote(
            source.at[0, 0], cot.at[t, d], ct_send.at[t, way], ct_recv.at[t, way], at(p, c, to)
        )

    def cot_relay(t, way, to):
        owner = before if way == 0 else after
        part_rows = pl.ds(way * half, half)
        return remote(
            cot.at[t, owner, part_rows], cot.at[t, owner, part_rows], ct_send.at[t, 2 + way],
            ct_recv.at[t, 2 + way], at(p, c, to),
        )

    def start_cot(t, source):
        cot_own(t, source).start()
        for way, to in ways:
            cot_copy(t, source, way, to).start()

    def relay_cots(t):
        for way, to in ways:
            cot_copy(t, down_ct, way, to).wait_recv()
        if copies == 4:
            for way, to in ways:
                cot_relay(t, way, to).start()

    def wait_cots(t):
        cot_own(t, down_ct).wait()
        if copies == 4:
            for way, to in ways:
                cot_relay(t, way, to).wait_recv()

    def start_cots(t):
        @pl.when(is_down(t))
        def _():
            start_cot(t, down_ct)

        @pl.when(jnp.logical_not(is_down(t)))
        def _():
            start_cot(t, up_ct)

    def meet():
        pl.semaphore_wait(barrier, len(peers))
        start_cots(0)

        @pl.when(jnp.logical_not(outer))
        def _():
            start_cots(1)

    outer = (p == 0) | (p == sections - 1)

    @pl.when(jnp.logical_not(outer))
    def _():
        meet()

    def state_copy(t, h):
        return remote(
            sout.at[t, h], sin.at[t, h], s_send.at[t, h], s_recv.at[t, h],
            at(p, lax.rem(c + 1, spans), d),
        )

    def first_copy(t, h):
        return remote(
            bsend.at[t, h], sin.at[t, h], s_send.at[t, h], s_recv.at[t, h],
            at(p, lax.rem(c + 1, spans), d),
        )

    def stage_of(t):
        early = jnp.where(low_half, p, sections - 1 - p)
        return jnp.where(t == 0, early, sections - 1 - early)

    def stream_copy(t, n):
        slot = jnp.where(stage_of(t) == 0, 0, 1)
        to = jnp.clip(jnp.where(is_down(t), p + 1, p - 1), 0, sections - 1)
        return remote(
            ybuf.at[t, n], xbuf.at[slot, n], x_send.at[t, n], x_recv.at[slot, n], at(to, c, d)
        )

    def result_copy(t, n, out):
        return pltpu.make_async_copy(
            ybuf.at[t, n], out.at[0, 0, :, pl.ds(n * COLS, COLS)], y_sem.at[t, n]
        )

    def hidden_own(t, piece):
        rows = pl.ds(piece * (spans * share // PIECES), spans * share // PIECES)
        return pltpu.make_async_copy(
            ht.at[t, d, rows], hg.at[t, d, rows], h_recv.at[t, d, piece]
        )

    def hidden_copy(t, k, piece):
        to = lax.rem(d + k, copies)
        rows = pl.ds(piece * (spans * share // PIECES), spans * share // PIECES)
        return remote(
            ht.at[t, to, rows], hg.at[t, d, rows], h_send.at[t, k - 1, piece],
            h_recv.at[t, d, piece], at(p, c, to),
        )

    def grad_own(t, to):
        return pltpu.make_async_copy(part.at[t, to], gbuf.at[to], g_recv.at[to])

    def grad_copy(t, to):
        slot = c + jnp.where(is_down(t), 0, spans)
        pipe = jnp.where(is_down(t), p, mirror)
        return remote(
            part.at[t, to], gbuf.at[slot], g_send.at[t, to], g_recv.at[slot], at(pipe, to, d)
        )

    def stays(t, to):
        return (c == to) & is_down(t)

    def section(t):
        ones = jnp.ones((COLS, DIM), BF)
        square = jnp.zeros((TOK, DIM), F32)
        square_row = jnp.zeros((2 * HEADS, TOK), F32)
        logits = jnp.zeros((2 * HEADS, TOK), F32)
        for n in range(CH):
            pltpu.make_async_copy(xbuf.at[t, n], xbuf.at[t, n], x_recv.at[t, n]).wait()
            weight_copy(t, n, down_qkv).wait()
            if n == CH - 1:
                @pl.when((t == 0) & low_half)
                def _():
                    out_copy(0, down_wo).start()

                @pl.when((t == 0) & jnp.logical_not(low_half))
                def _():
                    out_copy(0, up_wo).start()

            x = xbuf[t, n]
            xf = x.astype(F32)
            x2 = (xf * xf).astype(BF)
            square += mm(x2, ones)
            square_row += mm_nt(ones[0 : 2 * HEADS, 0:DIM], x2[:, 0:DIM])
            square_row += mm_nt(ones[0 : 2 * HEADS, 0:DIM], x2[:, DIM:COLS])
            logits += mm_nt(wg[t, :, n * COLS : (n + 1) * COLS], x)
            for j in range(6):
                block = slice(512 * j, 512 * (j + 1))
                product = mm(x, wqkv[t, n * COLS : (n + 1) * COLS, block])
                if n == 0:
                    proj[:, block] = product
                else:
                    proj[:, block] += product

        power = square * (1.0 / WIDTH) + EPSILON
        scale = lax.rsqrt(square_row * (1.0 / WIDTH) + EPSILON)
        gates = gate_rows(logits * scale, rates[t], triangle[...])


        masks = [maskb[level] for level in range(4)]
        low = maskb[4]
        eye = maskb[0].astype(F32)

        def put(h, qg, z1, z2, kx, fade):
            pmap[h, 0:DIM] = (qg[0:DIM] - z1[:, 0:DIM]).astype(BF)
            pmap[h, DIM:TOK] = (qg[DIM:TOK] - z2[:, 0:DIM]).astype(BF)
            rmap[h, 0:DIM] = z1[:, DIM:TOK]
            rmap[h, DIM:TOK] = z2[:, DIM:TOK]
            mmap[h] = (fade - kx[:, 0:DIM]).astype(BF)
            bmap[h] = kx[:, DIM:TOK]
            bsend[t, h] = kx[:, DIM:TOK].astype(BF)

        floor[...] = head_maps(
            proj, power, gates, select[...], masks, low, eye, put
        )

        @pl.when(t == 0)
        def _():
            load(1)

        @pl.when((t == 0) & outer)
        def _():
            meet()

        @pl.when(c == 0)
        def _():
            for h in range(HEADS):
                first_copy(t, h).start()
                sin[t, h] = jnp.zeros((DIM, DIM), BF)

        def finish_head(h):
            o = obuf[h % 2]
            level = jnp.mean(o * o, axis=-1, keepdims=True)
            o = o * lax.rsqrt(level + floor[:, HEADS + h : HEADS + h + 1])
            o = o.astype(BF)
            hid[:, h * DIM : (h + 1) * DIM] = o
            flipped = o.T
            for u in range(DIM // UNIT):
                row0 = h * DIM + u * UNIT
                span, rest = row0 // column, row0 % column
                to, i = rest // share, rest % share
                ht[t, to, span * share + i : span * share + i + UNIT] = flipped[
                    u * UNIT : (u + 1) * UNIT
                ]

        def send_pieces(h):
            for piece in range(PIECES):
                last = HEADS // PIECES * (piece + 1) - 1 if spans == HEADS else HEADS - 1
                if last == h:
                    hidden_own(t, piece).start()
                    for k in sorted(range(1, copies), key=lambda k: abs(2 * k - copies)):
                        hidden_copy(t, k, piece).start()

        for h in range(HEADS):
            @pl.when(c > 0)
            def _():
                state_copy(t, h).wait_recv()

            s = sin[t, h]
            sout[t, h] = (mm(mmap[h], s) + bmap[h]).astype(BF)
            if h < HEADS - 1:
                obuf[h % 2] = mm(pmap[h], s) + rmap[h]
                if h > 0:
                    finish_head(h - 1)

            @pl.when((c > 0) & (c < spans - 1))
            def _():
                state_copy(t, h).start()

            if h == HEADS - 1:
                obuf[h % 2] = mm(pmap[h], s) + rmap[h]
                finish_head(h - 1)

            if h > 0:
                send_pieces(h - 1)
        finish_head(HEADS - 1)
        send_pieces(HEADS - 1)

        out_copy(t, down_wo).wait()
        for n in range(CH):
            block = slice(n * COLS, (n + 1) * COLS)
            y = xbuf[t, n].astype(F32) + mm(hid[...], wo[t, :, block])
            ybuf[t, n] = y.astype(BF)

            @pl.when(stage_of(t) < sections - 1)
            def _():
                stream_copy(t, n).start()

        @pl.when(is_down(t))
        def _():
            for n in range(CH):
                result_copy(t, n, down_out).start()

        @pl.when(jnp.logical_not(is_down(t)))
        def _():
            for n in range(CH):
                result_copy(t, n, up_out).start()

        @pl.when(t == 0)
        def _():
            relay_cots(0)

            @pl.when(outer)
            def _():
                start_cots(1)

            @pl.when(jnp.logical_not(outer))
            def _():
                relay_cots(1)

    def gradient(t):
        wait_cots(t)
        size = spans * share // PIECES
        for piece in range(PIECES):
            rows = pl.ds(piece * size, size)
            for j in range(copies):
                pltpu.make_async_copy(
                    hg.at[t, j, rows], hg.at[t, j, rows], h_recv.at[t, j, piece]
                ).wait()
            total = mm(hg[t, 0, piece * size : (piece + 1) * size], cot[t, 0])
            for j in range(1, copies):
                total += mm(hg[t, j, piece * size : (piece + 1) * size], cot[t, j])
            total = total.astype(BF)
            for row0 in range(0, size, UNIT):
                to, at_row = divmod(piece * size + row0, share)
                part[t, to, at_row : at_row + UNIT] = total[row0 : row0 + UNIT]
                if at_row + UNIT == share:
                    @pl.when(stays(t, to))
                    def _():
                        grad_own(t, to).start()

                    @pl.when(jnp.logical_not(stays(t, to)))
                    def _():
                        grad_copy(t, to).start()

    def turn(i, carry):
        middle = jnp.where(outer, 2, 1)
        is_section = (i == 0) | (i == middle)

        @pl.when(is_section)
        def _():
            section(jnp.where(i == 0, 0, 1))

        @pl.when(jnp.logical_not(is_section))
        def _():
            gradient(jnp.where(i == 3, 1, 0))

            @pl.when(outer & (i == 1))
            def _():
                relay_cots(1)

        return carry

    lax.fori_loop(0, 4, turn, 0)

    for j in range(2 * spans):
        pltpu.make_async_copy(gbuf.at[j], gbuf.at[j], g_recv.at[j]).wait()
    total = gbuf[0].astype(F32)
    for j in range(1, 2 * spans):
        total += gbuf[j].astype(F32)
    gsum[...] = total
    final = pltpu.make_async_copy(gsum, grad_out.at[0], go_sem)
    final.start()

    for t in range(2):
        for n in range(CH):
            result_copy(t, n, down_out).wait()

            @pl.when(stage_of(t) < sections - 1)
            def _():
                stream_copy(t, n).wait_send()

        @pl.when(c < spans - 1)
        def _():
            for h in range(HEADS):
                state_copy(t, h).wait_send()

        for way, to in ways:
            cot_copy(t, down_ct, way, to).wait_send()
            if copies == 4:
                cot_relay(t, way, to).wait_send()
        for k in range(1, copies):
            for piece in range(PIECES):
                hidden_copy(t, k, piece).wait_send()
        for to in range(spans):
            @pl.when(jnp.logical_not(stays(t, to)))
            def _():
                grad_copy(t, to).wait_send()

    final.wait()


def hand_over(down_in, up_in, grad_in, down_out, up_out, grad_out, acts, grad, in_sems, out_sems):
    rows = TOK // HANDS
    moves = []
    for i, (src, dst) in enumerate(((down_in, down_out), (up_in, up_out))):
        for n in range(HANDS):
            part = (0, 0, pl.ds(n * rows, rows))
            moves.append((src.at[part], acts.at[i, pl.ds(n * rows, rows)], dst.at[part]))
    moves.append((grad_in.at[0], grad, grad_out.at[0]))
    loads, stores = [], []
    for i, (src, here, dst) in enumerate(moves):
        loads.append(pltpu.make_async_copy(src, here, in_sems.at[i]))
        stores.append(pltpu.make_async_copy(here, dst, out_sems.at[i]))
        loads[i].start()
    for load, store in zip(loads, stores):
        load.wait()
        store.start()
    for store in stores:
        store.wait()


def per_device(dims, *arrays):
    sections, spans, copies = dims
    share = WIDTH // (spans * copies)
    hbm = pl.BlockSpec(memory_space=pl.ANY)
    vmem = pl.BlockSpec(memory_space=pltpu.VMEM)
    dma = pltpu.SemaphoreType.DMA
    down_acts, up_acts, grad = pl.pallas_call(
        functools.partial(kernel, dims),
        out_shape=(
            jax.ShapeDtypeStruct((1, 1, TOK, WIDTH), BF),
            jax.ShapeDtypeStruct((1, 1, TOK, WIDTH), BF),
            jax.ShapeDtypeStruct((1, share, WIDTH), F32),
        ),
        in_specs=[hbm] * 4 + [vmem] * 4 + [hbm] * 4,
        out_specs=(hbm, hbm, hbm),
        scratch_shapes=[
            pltpu.VMEM((2, WIDTH, 3 * WIDTH), BF),
            pltpu.VMEM((2, WIDTH, WIDTH), BF),
            pltpu.VMEM((2, 2 * HEADS, WIDTH), BF),
            pltpu.VMEM((2, 2 * HEADS, TOK), F32),
            pltpu.VMEM((TOK, TOK), BF),
            pltpu.VMEM((2, CH, TOK, COLS), BF),
            pltpu.VMEM((2, CH, TOK, COLS), BF),
            pltpu.VMEM((TOK, 3 * WIDTH), F32),
            pltpu.VMEM((TOK, WIDTH), BF),
            pltpu.VMEM((2, TOK, DIM), F32),
            pltpu.VMEM((len(MASKS), DIM, DIM), BF),
            pltpu.VMEM((WIDTH, DIM), BF),
            pltpu.VMEM((TOK, DIM), F32),
            pltpu.VMEM((HEADS, TOK, DIM), BF),
            pltpu.VMEM((HEADS, TOK, DIM), F32),
            pltpu.VMEM((HEADS, DIM, DIM), BF),
            pltpu.VMEM((HEADS, DIM, DIM), F32),
            pltpu.VMEM((2, HEADS, DIM, DIM), BF),
            pltpu.VMEM((2, HEADS, DIM, DIM), BF),
            pltpu.VMEM((2, HEADS, DIM, DIM), BF),
            pltpu.VMEM((2, copies, TOK, WIDTH), BF),
            pltpu.VMEM((2, copies, spans * share, TOK), BF),
            pltpu.VMEM((2, copies, spans * share, TOK), BF),
            pltpu.VMEM((2, spans, share, WIDTH), BF),
            pltpu.VMEM((2 * spans, share, WIDTH), BF),
            pltpu.VMEM((share, WIDTH), F32),
            dma((2, CH)),
            dma((2,)),
            dma((2, CH)),
            dma((2, CH)),
            dma((2, CH)),
            dma((2, HEADS)),
            dma((2, HEADS)),
            dma((2, 4)),
            dma((2, 4)),
            dma((2,)),
            dma((2, copies, PIECES)),
            dma((2, copies, PIECES)),
            dma((2 * spans,)),
            dma((2, spans)),
            dma,
        ],
        compiler_params=pltpu.CompilerParams(
            collective_id=0, has_side_effects=True, vmem_limit_bytes=60 * 1024 * 1024
        ),
    )(*arrays[:4], *(jnp.swapaxes(gates, 1, 2) for gates in arrays[4:6]), *arrays[6:])
    return pl.pallas_call(
        hand_over,
        out_shape=tuple(jax.ShapeDtypeStruct(a.shape, a.dtype) for a in (down_acts, up_acts, grad)),
        in_specs=[hbm] * 3,
        out_specs=(hbm, hbm, hbm),
        scratch_shapes=[
            pltpu.VMEM((2, TOK, WIDTH), BF),
            pltpu.VMEM((share, WIDTH), F32),
            dma((2 * HANDS + 1,)),
            dma((2 * HANDS + 1,)),
        ],
    )(down_acts, up_acts, grad)


def solution(mesh):
    dims = (mesh.shape["pipe"], mesh.shape["ctx"], mesh.shape["dp"])
    return jax.shard_map(
        functools.partial(per_device, dims),
        mesh=mesh,
        in_specs=(
            P("dp", "ctx", None),
            P("dp", "ctx", None),
            P("pipe", None, None),
            P("pipe", None, None),
            P("pipe", None, None),
            P("pipe", None, None),
            P("pipe", None),
            P("pipe", None),
            P("pipe", None, None),
            P("pipe", None, None),
            P("pipe", "dp", "ctx", None),
            P("pipe", "dp", "ctx", None),
        ),
        out_specs=(
            P("pipe", "dp", "ctx", None),
            P("pipe", "dp", "ctx", None),
            P("pipe", ("ctx", "dp"), None),
        ),
        check_vma=False,
    )
```
